128 devices in a mesh: ctx: 64 (over x, y, z), hd: 2 (over core).
Axes of the slice: x: 4, y: 4, z: 4, core: 2. Of those that a mesh axis runs over, the one named last changes fastest.
Arguments:
- tokens: bfloat16 [65536, 640], P(('ctx', 'hd')), may hold values from -6 to 6
- gain_attn: bfloat16 [640], P(('ctx', 'hd')), may hold values from 0.5 to 1.5
- gain_ffn: bfloat16 [640], P(('ctx', 'hd')), may hold values from 0.5 to 1.5
- w_query: bfloat16 [1024, 640], P(('ctx', 'hd')), may hold values from -0.25 to 0.25
- w_keyval: bfloat16 [512, 640], P(('ctx', 'hd')), may hold values from -0.25 to 0.25
- w_out: bfloat16 [1024, 640], P(('ctx', 'hd')), may hold values from -3 to 3
- w_gate: bfloat16 [2048, 640], P(('ctx', 'hd')), may hold values from -0.25 to 0.25
- w_up: bfloat16 [2048, 640], P(('ctx', 'hd')), may hold values from -0.25 to 0.25
- w_down: bfloat16 [2048, 640], P(('ctx', 'hd')), may hold values from -0.125 to 0.125
- cotangent: bfloat16 [65536, 640], P(('ctx', 'hd')), may hold values from -6 to 6
Outputs:
- output: bfloat16 [65536, 640], P(('ctx', 'hd'))
- grad_tokens: float32 [65536, 640], P(('ctx', 'hd'))
- grad_query: float32 [1024, 640], P(('ctx', 'hd'))
- grad_keyval: float32 [512, 640], P(('ctx', 'hd'))
- grad_out: float32 [1024, 640], P(('ctx', 'hd'))
- grad_gate: float32 [2048, 640], P(('ctx', 'hd'))
- grad_up: float32 [2048, 640], P(('ctx', 'hd'))
- grad_down: float32 [2048, 640], P(('ctx', 'hd'))
- grad_gain_attn: float32 [640], P(('ctx', 'hd'))
- grad_gain_ffn: float32 [640], P(('ctx', 'hd'))
The draws below stay inside these ranges and needn't reach their ends.
All inputs are finite; a program needn't handle non-finite values.
Results may differ from the reference program's by a relative error of at most 0.015.
Values may be sent and summed in bfloat16 or wider, within the bound.
No kernel may reach another device: no remote copies, remote signals or barrier semaphores. Data moves between devices by JAX's collectives and lax.ppermute only.
A program may use at most 192 MiB of HBM per device.

```python
import math
import jax
import jax.numpy as jnp
from jax import lax

D = 640
HEADS = 4
HEAD = 256
FF = 2048
WIN = 512
TOK_DEV = 512
QD = 1024
KVD = 512
TOKENS = 65536


def block_scale(stream_key, shape, shards, low, high):
    def one(dim, shards_of):
        draws = jax.random.uniform(jax.random.fold_in(jax.random.fold_in(stream_key, 6), dim), (shards_of,), jnp.float32, low / len(shards), high / len(shards))
        return jnp.repeat(jnp.exp(draws), shape[dim] // shards_of).reshape((-1,) + (1,) * (len(shape) - dim - 1))

    loudness = one(*shards[0])
    for cut in shards[1:]:
        loudness = loudness * one(*cut)
    return loudness


def noise(stream_key, shape, deviation, most, cuts=(), held_as=jnp.bfloat16):
    drawn = jax.random.normal(stream_key, shape, jnp.float32) * deviation
    if len(cuts) > 0:
        drawn = block_scale(stream_key, shape, cuts, -0.22, 0.18) * drawn
    return jnp.clip(drawn, min=-most, max=most).astype(held_as)


def setup_inputs(seed: int = 0) -> dict:
    keys = jax.random.split(jax.random.key(seed), 11)
    tokens = noise(keys[0], (TOKENS, D), 1.0, 6.0, ((0, 128),))
    gain_attn = jnp.clip(1.0 + 0.1 * jax.random.normal(keys[1], (D,), jnp.float32), 0.5, 1.5).astype(jnp.bfloat16)
    gain_ffn = jnp.clip(1.0 + 0.1 * jax.random.normal(keys[2], (D,), jnp.float32), 0.5, 1.5).astype(jnp.bfloat16)
    w_query = noise(keys[3], (QD, D), D ** -0.5, 0.25, ((0, 128),))
    w_keyval = noise(keys[4], (KVD, D), D ** -0.5, 0.25, ((0, 128),))
    w_out = noise(keys[5], (QD, D), (2 * (QD // WIN)) ** -0.5, 3.0, ((0, 128),))
    w_gate = noise(keys[6], (FF, D), D ** -0.5, 0.25, ((0, 128),))
    w_up = noise(keys[7], (FF, D), D ** -0.5, 0.25, ((0, 128),))
    w_down = noise(keys[8], (FF, D), FF ** -0.5, 0.125, ((0, 128),))
    cotangent = noise(keys[9], (TOKENS, D), 1.0, 6.0, ((0, 128),))
    return dict(tokens=tokens, gain_attn=gain_attn, gain_ffn=gain_ffn, w_query=w_query, w_keyval=w_keyval, w_out=w_out, w_gate=w_gate, w_up=w_up, w_down=w_down, cotangent=cotangent)


@jax.custom_vjp
def low(v):
    return lax.optimization_barrier(v.astype(jnp.bfloat16)).astype(jnp.float32)

@jax.custom_vjp
def low_back(v):
    return v

def low_keep(v):
    return (low(v), None)

def low_pass(kept, grad):
    return (grad,)

def back_keep(v):
    return (v, None)

def back_low(kept, grad):
    return (low(grad),)
low.defvjp(low_keep, low_pass)
low_back.defvjp(back_keep, back_low)
EPSILON = 1e-06
MASKED = -1e+30
HIGHEST = lax.Precision.HIGHEST

def rms_scale(values, gain):
    return values * lax.rsqrt(lax.optimization_barrier(jnp.mean(values * values, axis=-1, keepdims=True)) + EPSILON) * gain

def times_rows(left, right):
    return lax.dot_general(left, right, (((1,), (1,)), ((), ())), precision=HIGHEST)

def times_plain(left, right):
    return jnp.dot(left, right, precision=HIGHEST)

def attend(queries, keyvals):
    total_rows = queries.shape[0]
    block_rows = TOK_DEV * 8
    block_count = total_rows // block_rows
    padded = jnp.concatenate([jnp.zeros((WIN, 2 * HEAD), keyvals.dtype), keyvals], axis=0)
    query_blocks = queries.reshape(block_count, block_rows, HEADS, HEAD)
    offsets = (jnp.arange(block_count, dtype=jnp.int32) * block_rows).astype(jnp.int32)
    scale = 1.0 / math.sqrt(HEAD)

    def one_block(operands):
        query_block, offset = operands
        window = lax.dynamic_slice_in_dim(padded, offset, block_rows + WIN, 0)
        scores = jnp.einsum('qhd,kd->hqk', query_block, window[:, :HEAD], precision=HIGHEST) * scale
        scores = low_back(scores)
        query_pos = offset + jnp.arange(block_rows, dtype=jnp.int32)
        key_pos = offset - WIN + jnp.arange(block_rows + WIN, dtype=jnp.int32)
        allowed = (key_pos[None, :] <= query_pos[:, None]) & (key_pos[None, :] > query_pos[:, None] - WIN) & (key_pos[None, :] >= 0)
        scores = jnp.where(allowed[None], scores, MASKED)
        weights = low(jax.nn.softmax(scores, axis=-1))
        return jnp.einsum('hqk,kd->qhd', weights, window[:, HEAD:], precision=HIGHEST)
    blocks = lax.map(jax.checkpoint(one_block), (query_blocks, offsets))
    return blocks.reshape(total_rows, HEADS * HEAD)

def layer(inputs, gain_one, gain_two, w_query, w_keyval, w_out, w_gate, w_up, w_down):
    normed = low(rms_scale(inputs, gain_one))
    queries = low_back(low(times_rows(normed, w_query)))
    keyvals = low_back(low(times_rows(normed, w_keyval)))
    attended = low_back(low(attend(queries, keyvals)))
    residual = inputs + low_back(times_plain(attended, w_out))
    normed_two = low(rms_scale(residual, gain_two))
    gate_value = low_back(times_rows(normed_two, w_gate))
    up_value = low_back(times_rows(normed_two, w_up))
    hidden = low(jax.nn.gelu(gate_value, approximate=True) * up_value)
    return residual + low_back(times_plain(hidden, w_down))

def reference(tokens, gain_attn, gain_ffn, w_query, w_keyval, w_out, w_gate, w_up, w_down, cotangent):
    operands = [value.astype(jnp.float32) for value in (tokens, gain_attn, gain_ffn, w_query, w_keyval, w_out, w_gate, w_up, w_down)]
    result, pullback = jax.vjp(layer, *operands)
    grads = pullback(cotangent.astype(jnp.float32))
    return (result.astype(jnp.bfloat16), grads[0], grads[3], grads[4], grads[5], grads[6], grads[7], grads[8], grads[1], grads[2])
```

```python
import math

import jax
import jax.numpy as jnp
from jax import lax
from jax.sharding import PartitionSpec as P

HEADS = 4
HEAD = 256
WIN = 512
SIDE = 4

EPSILON = 1e-06
MASKED = -1e30
AXES = ("ctx", "hd")
BF = jnp.bfloat16
F32 = jnp.float32

ATTN_ORDER = ((0, 0), (1, 2), (2, 1))
FFN_ORDER = ((1, 2), (2, 0), (0, 1))


def chip_pairs(axis_of_core, steps):
    pairs = []
    for chip in range(SIDE**3):
        spot = [chip // SIDE**2, chip // SIDE % SIDE, chip % SIDE]
        for core in range(2):
            goal = list(spot)
            axis = axis_of_core[core]
            goal[axis] = (goal[axis] + steps) % SIDE
            target = (goal[0] * SIDE + goal[1]) * SIDE + goal[2]
            pairs.append((chip * 2 + core, target * 2 + core))
    return pairs


def to_sibling(value):
    return lax.ppermute(value, "hd", [(0, 1), (1, 0)])


def gather_stage(value, axis_of_core):
    return [value] + [
        lax.ppermute(value, AXES, chip_pairs(axis_of_core, -steps)) for steps in range(1, SIDE)
    ]


def scatter_stage(pieces, axis_of_core):
    total = pieces[0].astype(F32)
    for steps in range(1, SIDE):
        total = total + lax.ppermute(
            pieces[steps].astype(BF), AXES, chip_pairs(axis_of_core, steps)
        ).astype(F32)
    return total


def shifted(value, steps):
    count = lax.axis_size(AXES)
    initial, last = (max(0, -steps), min(count, count - steps))
    return lax.ppermute(value, AXES, [(source, source + steps) for source in range(initial, last)])


def rms_scale(values, gain):
    return values * lax.rsqrt(jnp.mean(values * values, axis=-1, keepdims=True) + EPSILON) * gain


def times_rows(left, right):
    return lax.dot_general(left, right, (((1,), (1,)), ((), ())), preferred_element_type=F32)


def times_cols(left, right):
    return lax.dot_general(left, right, (((0,), (0,)), ((), ())), preferred_element_type=F32)


def times_plain(left, right):
    return jnp.dot(left, right, preferred_element_type=F32)


def geglu(gate_value, up_value):
    return jax.nn.gelu(gate_value, approximate=True) * up_value


def keyval_order(place):
    core = place % 2
    chip = place // 2
    spot = [chip // SIDE**2, chip // SIDE % SIDE, chip % SIDE]

    def device_of(half, first, last, mid):
        owner = jnp.bitwise_xor(core, half)
        x = (spot[0] + first) % SIDE
        y = (spot[1] + jnp.where(owner == 0, mid, last)) % SIDE
        z = (spot[2] + jnp.where(owner == 0, last, mid)) % SIDE
        return x, ((x * SIDE + y) * SIDE + z) * 2 + owner

    row = jnp.arange(2 * HEAD, dtype=jnp.int32)
    kind, feature = row // HEAD, row % HEAD
    _, device = device_of(feature // 128, 0 * row, feature // 32 % 4, feature // 8 % 4)
    goal = kind * HEAD + device % 32 * 8 + feature % 8
    _, device = device_of(row // 256, row // 64 % 4, row // 16 % 4, row // 4 % 4)
    have = device * 4 + row % 4
    return (goal[:, None] == have[None, :]).astype(BF), (goal[:, None] == row[None, :]).astype(BF)


def local(tokens, gain_attn, gain_ffn, w_query, w_keyval, w_out, w_gate, w_up, w_down, cotangent):
    row_count, model_width = tokens.shape
    place = lax.axis_index(AXES)
    scale = 1.0 / math.sqrt(HEAD)

    width = gain_attn.shape[0]
    lane = jnp.arange(model_width, dtype=jnp.int32)
    mine = lane // width == place
    gain_rows = jnp.where(
        mine[None, :], jnp.stack([jnp.tile(gain_attn, 128), jnp.tile(gain_ffn, 128)]), 0
    ).astype(BF)
    payload = jnp.concatenate([w_query, w_out, w_keyval, jnp.pad(gain_rows, ((0, 2), (0, 0)))])
    got = gather_stage(payload, ATTN_ORDER[0])
    query_part = jnp.stack([one[0:8] for one in got])
    out_part = jnp.stack([one[8:16] for one in got])
    keyval_part = jnp.stack([one[16:20] for one in got])
    gains = got[0][20:22] + got[1][20:22] + got[2][20:22] + got[3][20:22]
    payload = jnp.concatenate(
        [
            query_part.reshape(-1, model_width),
            out_part.reshape(-1, model_width),
            keyval_part.reshape(-1, model_width),
            jnp.pad(gains, ((0, 14), (0, 0))),
        ]
    )
    got = gather_stage(payload, ATTN_ORDER[1])
    query_part = jnp.stack([one[0:32].reshape(4, 8, model_width) for one in got], axis=1)
    out_part = jnp.stack([one[32:64].reshape(4, 8, model_width) for one in got], axis=1)
    keyval_part = jnp.stack([one[64:80].reshape(4, 4, model_width) for one in got], axis=1)
    gains = got[0][80:82] + got[1][80:82] + got[2][80:82] + got[3][80:82]
    payload = jnp.concatenate(
        [
            query_part.reshape(-1, model_width),
            out_part.reshape(-1, model_width),
            keyval_part.reshape(-1, model_width),
            jnp.pad(gains, ((0, 14), (0, 0))),
        ]
    )
    got = gather_stage(payload, ATTN_ORDER[2])
    halves = [got, [to_sibling(one) for one in got]]

    def assembled(first, rows):
        return jnp.stack(
            [
                jnp.stack(
                    [one[first : first + rows].reshape(4, rows // 4, model_width) for one in half],
                    axis=1,
                )
                for half in halves
            ],
            axis=1,
        )

    full_query = assembled(0, 128).reshape(HEADS * HEAD, model_width)
    full_out = assembled(128, 128).reshape(HEADS * HEAD, model_width)
    order, natural = keyval_order(place)
    full_keyval = jnp.stack(
        [
            jnp.stack([one[256:320].reshape(4, 16, model_width) for one in half], axis=1)
            for half in halves
        ],
        axis=0,
    ).reshape(2 * HEAD, model_width)
    full_keyval = times_plain(order, full_keyval).astype(BF)
    gains = sum(one[320:322].astype(F32) for half in halves for one in half)
    gain_one, gain_two = gains[0], gains[1]

    ffn = jnp.stack([w_gate, w_up, w_down])
    ffn = jnp.concatenate(gather_stage(ffn, FFN_ORDER[0]), axis=1)
    ffn = jnp.concatenate(gather_stage(ffn, FFN_ORDER[1]), axis=1)
    ffn = gather_stage(ffn, FFN_ORDER[2])
    ffn = jnp.concatenate(ffn + [to_sibling(one) for one in ffn], axis=1)
    full_gate, full_up, full_down = ffn[0], ffn[1], ffn[2]

    inputs = tokens.astype(F32)
    before = shifted(tokens, 1)
    normed = rms_scale(inputs, gain_one).astype(BF)
    normed_before = rms_scale(before.astype(F32), gain_one).astype(BF)
    queries = times_rows(normed, full_query).astype(BF)
    keyvals = times_rows(jnp.concatenate([normed_before, normed]), full_keyval).astype(BF)
    query_rows = jnp.concatenate([queries[:, h * HEAD : (h + 1) * HEAD] for h in range(HEADS)])
    key_rows = keyvals[:, :HEAD]
    value_rows = keyvals[:, HEAD:]
    query_pos = jnp.arange(HEADS * row_count, dtype=jnp.int32) % row_count + WIN
    key_pos = jnp.arange(2 * row_count, dtype=jnp.int32)
    allowed = (
        (key_pos[None, :] <= query_pos[:, None])
        & (key_pos[None, :] > query_pos[:, None] - WIN)
        & (key_pos[None, :] >= jnp.where(place == 0, WIN, 0))
    )
    scores = jnp.where(allowed, times_rows(query_rows, key_rows) * scale, MASKED)
    top_score = jnp.max(scores, axis=1, keepdims=True)
    raised = jnp.exp(scores - top_score)
    row_total = jnp.sum(raised, axis=1, keepdims=True)
    probs = raised / row_total
    probs_low = probs.astype(BF)
    attended = times_plain(probs_low, value_rows).astype(BF)
    attended = jnp.concatenate(
        [attended[h * row_count : (h + 1) * row_count] for h in range(HEADS)], axis=1
    )
    residual = inputs + times_plain(attended, full_out)
    normed_two = rms_scale(residual, gain_two).astype(BF)

    gate_value = times_rows(normed_two, full_gate)
    up_value = times_rows(normed_two, full_up)
    hidden = geglu(gate_value, up_value).astype(BF)
    output = (residual + times_plain(hidden, full_down)).astype(BF)
    hidden_grad = times_rows(cotangent, full_down)
    _, pullback = jax.vjp(geglu, gate_value, up_value)
    gate_grad, up_grad = pullback(hidden_grad)
    gate_grad = gate_grad.astype(BF)
    up_grad = up_grad.astype(BF)
    normed_grad = times_plain(gate_grad, full_gate) + times_plain(up_grad, full_up)
    ffn_terms = jnp.stack(
        [
            times_cols(gate_grad, normed_two),
            times_cols(up_grad, normed_two),
            times_cols(hidden, cotangent),
        ]
    )

    part = ffn_terms[:, :1024] + to_sibling(ffn_terms[:, 1024:].astype(BF)).astype(F32)
    for stage in (2, 1, 0):
        rows = part.shape[1] // SIDE
        part = scatter_stage(
            [part[:, k * rows : (k + 1) * rows] for k in range(SIDE)], FFN_ORDER[stage]
        )
    grad_gate, grad_up, grad_down = part[0], part[1], part[2]

    _, second_pull = jax.vjp(rms_scale, residual, gain_two)
    residual_part, gain_two_grad = second_pull(normed_grad)
    residual_grad = cotangent.astype(F32) + residual_part
    residual_low = residual_grad.astype(BF)
    out_term = times_cols(attended, residual_low)
    attended_grad = times_rows(residual_low, full_out).astype(BF)
    grad_rows = jnp.concatenate([attended_grad[:, h * HEAD : (h + 1) * HEAD] for h in range(HEADS)])
    prob_grad = times_rows(grad_rows, value_rows)
    centre = jnp.sum(probs * prob_grad, axis=1, keepdims=True)
    score_grad = (probs * (prob_grad - centre)).astype(BF)
    query_grad = (times_plain(score_grad, key_rows) * scale).astype(BF)
    query_grad = jnp.concatenate(
        [query_grad[h * row_count : (h + 1) * row_count] for h in range(HEADS)], axis=1
    )
    key_grad = times_cols(score_grad, query_rows) * scale
    value_grad = times_cols(probs_low, grad_rows)
    window_grad = jnp.concatenate([key_grad, value_grad], axis=1)
    later = shifted(times_plain(window_grad[:row_count].astype(BF), natural).astype(BF), -1)
    keyval_grad = window_grad[row_count:] + times_rows(later, natural)
    keyval_low = keyval_grad.astype(BF)
    normed_one_grad = times_plain(query_grad, full_query) + times_plain(keyval_low, full_keyval)
    query_term = times_cols(query_grad, normed)
    keyval_term = times_cols(keyval_low, normed)
    keyval_term = times_cols(order, keyval_term.astype(BF))
    _, first_pull = jax.vjp(rms_scale, inputs, gain_one)
    input_part, gain_one_grad = first_pull(normed_one_grad)
    input_grad = residual_grad + input_part

    gain_terms = jnp.stack([gain_one_grad, gain_two_grad])

    def split(value):
        high = value.astype(BF)
        return jnp.pad(
            jnp.concatenate([high, (value - high.astype(F32)).astype(BF)]), ((0, 12), (0, 0))
        )

    def joined(rows):
        return rows[0:2].astype(F32) + rows[2:4].astype(F32)

    query_half = query_term.reshape(4, 2, 4, 4, 8, model_width)
    out_half = out_term.reshape(4, 2, 4, 4, 8, model_width)
    keyval_half = keyval_term.reshape(2, 4, 4, 4, 4, model_width)
    sent = jnp.concatenate(
        [
            query_half[:, 1].reshape(-1, model_width).astype(BF),
            out_half[:, 1].reshape(-1, model_width).astype(BF),
            keyval_half[1].reshape(-1, model_width).astype(BF),
            split(gain_terms),
        ]
    )
    came = to_sibling(sent)
    query_part = query_half[:, 0] + came[0:512].reshape(4, 4, 4, 8, model_width).astype(F32)
    out_part = out_half[:, 0] + came[512:1024].reshape(4, 4, 4, 8, model_width).astype(F32)
    keyval_part = keyval_half[0] + came[1024:1280].reshape(4, 4, 4, 4, model_width).astype(F32)
    gain_terms = gain_terms + joined(came[1280:])
    for stage in (2, 1, 0):
        axis = {2: 1, 1: 1, 0: 0}[stage]
        query_new, out_new, keyval_new, gain_new = None, None, None, gain_terms
        for k in range(SIDE):
            parts = [
                lax.index_in_dim(one, k, axis, keepdims=False)
                for one in (query_part, out_part, keyval_part)
            ]
            if k == 0:
                query_new, out_new, keyval_new = parts
                continue
            sent = jnp.concatenate(
                [one.reshape(-1, model_width).astype(BF) for one in parts] + [split(gain_terms)]
            )
            came = lax.ppermute(sent, AXES, chip_pairs(ATTN_ORDER[stage], k))
            rows = [one.size // model_width for one in parts]
            query_new = query_new + came[: rows[0]].reshape(parts[0].shape).astype(F32)
            out_new = out_new + came[rows[0] : rows[0] + rows[1]].reshape(parts[1].shape).astype(
                F32
            )
            keyval_new = keyval_new + came[rows[0] + rows[1] : sum(rows)].reshape(
                parts[2].shape
            ).astype(F32)
            gain_new = gain_new + joined(came[sum(rows) :])
        query_part, out_part, keyval_part, gain_terms = query_new, out_new, keyval_new, gain_new
    gain_shares = lax.dynamic_slice_in_dim(gain_terms, place * width, width, 1)
    return (
        output,
        input_grad,
        query_part,
        keyval_part,
        out_part,
        grad_gate,
        grad_up,
        grad_down,
        gain_shares[0],
        gain_shares[1],
    )


def solution(mesh):
    rows, flat = P(AXES, None), P(AXES)
    return jax.shard_map(
        local,
        mesh=mesh,
        in_specs=(rows, flat, flat, rows, rows, rows, rows, rows, rows, rows),
        out_specs=(rows, rows, rows, rows, rows, rows, rows, rows, flat, flat),
        check_vma=False,
    )
```

```python
import math

import jax
import jax.numpy as jnp
from jax import lax
from jax.experimental import pallas as pl
from jax.experimental.pallas import tpu as pltpu
from jax.sharding import PartitionSpec as P

HEADS = 4
HEAD = 256
WIN = 512
SIDE = 4

EPSILON = 1e-06
MASKED = -1e30
AXES = ("ctx", "hd")
BF = jnp.bfloat16
F32 = jnp.float32

SCALE = 1.0 / math.sqrt(HEAD)
TILE = 128
SPAN = WIN + TILE
MEGA = 1 << 20

ORDER = ((0, 0), (1, 2), (2, 1))


def chip_pairs(axis_of_core, steps):
    pairs = []
    for chip in range(SIDE**3):
        spot = [chip // SIDE**2, chip // SIDE % SIDE, chip % SIDE]
        for core in range(2):
            goal = list(spot)
            axis = axis_of_core[core]
            goal[axis] = (goal[axis] + steps) % SIDE
            target = (goal[0] * SIDE + goal[1]) * SIDE + goal[2]
            pairs.append((chip * 2 + core, target * 2 + core))
    return pairs


def to_sibling(value):
    return lax.ppermute(value, "hd", [(0, 1), (1, 0)])


def gather_stage(value, stage):
    return [value] + [
        lax.ppermute(value, AXES, chip_pairs(ORDER[stage], -steps)) for steps in range(1, SIDE)
    ]


def scatter_stage(pieces, stage):
    return [
        lax.ppermute(pieces[steps], AXES, chip_pairs(ORDER[stage], steps))
        for steps in range(1, SIDE)
    ]


def shifted(value, steps):
    count = lax.axis_size(AXES)
    initial, last = (max(0, -steps), min(count, count - steps))
    return lax.ppermute(value, AXES, [(source, source + steps) for source in range(initial, last)])


def times_rows(left, right):
    return lax.dot_general(left, right, (((1,), (1,)), ((), ())), preferred_element_type=F32)


def times_cols(left, right):
    return lax.dot_general(left, right, (((0,), (0,)), ((), ())), preferred_element_type=F32)


def times_plain(left, right):
    return jnp.dot(left, right, preferred_element_type=F32)


def shape(dims, kind):
    return jax.ShapeDtypeStruct(dims, kind)


def run(kernel, outs, *operands, scratch=(), flops=0, limit=48, in_specs=None, out_specs=None, **more):
    moved = sum(one.size * one.dtype.itemsize for one in operands)
    moved += sum(math.prod(one.shape) * one.dtype.itemsize for one in outs)
    specs = {}
    if in_specs is not None:
        specs["in_specs"] = in_specs
    if out_specs is not None:
        specs["out_specs"] = out_specs
    return pl.pallas_call(
        kernel,
        out_shape=outs,
        scratch_shapes=list(scratch),
        cost_estimate=pl.CostEstimate(flops=flops, bytes_accessed=moved, transcendentals=0),
        compiler_params=pltpu.CompilerParams(vmem_limit_bytes=limit * MEGA),
        **specs,
        **more,
    )(*operands)


def selectors(place):
    core = place % 2
    chip = place // 2
    spot = [chip // SIDE**2, chip // SIDE % SIDE, chip % SIDE]

    def device_of(half, first, last, mid):
        owner = jnp.bitwise_xor(core, half)
        x = (spot[0] + first) % SIDE
        y = (spot[1] + jnp.where(owner == 0, mid, last)) % SIDE
        z = (spot[2] + jnp.where(owner == 0, last, mid)) % SIDE
        return ((x * SIDE + y) * SIDE + z) * 2 + owner

    row = jnp.arange(528, dtype=jnp.int32)
    kind, feature = row // HEAD, row % HEAD
    device = device_of(feature // 128, 0 * row, feature // 32 % 4, feature // 8 % 4)
    goal = kind * HEAD + device % 32 * 8 + feature % 8
    column = jnp.arange(1024, dtype=jnp.int32)
    device = device_of(column // 512, column // 32 % 4, column // 128 % 4, column // 8 % 4)
    part = column % 8
    have = jnp.where(part < 4, device * 4 + part, -1)
    keyval = (goal[:, None] == have[None, :]) & (row[:, None] < 512)
    gains = (row[:, None] >= 512) & (part[None, :] == row[:, None] - 508) & (part[None, :] < 6)
    natural = (goal[:HEAD, None] == row[None, :HEAD]).astype(BF)
    return (keyval | gains).astype(BF), natural


def normalise(values, gain):
    inverse = lax.rsqrt(jnp.mean(values * values, axis=-1, keepdims=True) + EPSILON)
    return (values * inverse * gain).astype(BF)


def normalise_back(values, gain, grad):
    inverse = lax.rsqrt(jnp.mean(values * values, axis=-1, keepdims=True) + EPSILON)
    unit = values * inverse
    gain_grad = jnp.sum(grad * unit, axis=0, keepdims=True)
    scaled = grad * gain
    return inverse * (scaled - unit * jnp.mean(scaled * unit, axis=-1, keepdims=True)), gain_grad


def own_mask():
    row = lax.broadcasted_iota(jnp.int32, (HEADS * TILE, TILE), 0) % TILE
    column = lax.broadcasted_iota(jnp.int32, (HEADS * TILE, TILE), 1)
    return column <= row


def folded(wide, own):
    return jnp.concatenate(
        [jnp.where(own, wide[:, WIN:], wide[:, :TILE]), wide[:, TILE:WIN]], axis=1
    )


def unfolded(narrow, own):
    edge = narrow[:, :TILE]
    none = jnp.zeros_like(edge)
    return jnp.concatenate(
        [jnp.where(own, none, edge), narrow[:, TILE:], jnp.where(own, edge, none)], axis=1
    )


def forward_kernel(
    place_ref, tokens_ref, before_ref, select_ref, a0, a1, a2, a3, b0, b1, b2, b3,
    residual_ref, normed_two_ref, normed_ref, query_ref, keyval_ref, attended_ref, probs_ref,
    weight_query_ref, weight_out_ref, weight_keyval_ref, gains_ref,
):
    count = tokens_ref.shape[0]
    halves = ((a0, a1, a2, a3), (b0, b1, b2, b3))
    for head in range(HEADS):
        for half in range(2):
            for last in range(SIDE):
                here = pl.ds(head * HEAD + half * 128 + last * 32, 32)
                weight_query_ref[here, :] = halves[half][last][0, pl.ds(head * 32, 32), :]
                weight_out_ref[here, :] = halves[half][last][1, pl.ds(head * 32, 32), :]
    mixed = jnp.concatenate([one[2] for half in halves for one in half], axis=0)
    sorted_rows = times_plain(select_ref[...], mixed)
    weight_keyval_ref[...] = sorted_rows[:512].astype(BF)
    gains_ref[...] = sorted_rows[512:520]
    gain_one = sorted_rows[512:513]
    gain_two = sorted_rows[513:514]
    inputs = tokens_ref[...].astype(F32)
    normed = normalise(inputs, gain_one)
    normed_ref[...] = normed
    normed_before = normalise(before_ref[...].astype(F32), gain_one)
    weight_keyval = weight_keyval_ref[...]
    keyval_ref[:WIN, :] = times_rows(normed_before, weight_keyval).astype(BF)
    keyval_ref[WIN:, :] = times_rows(normed, weight_keyval).astype(BF)
    for head in range(HEADS):
        query_ref[head] = times_rows(
            normed, weight_query_ref[pl.ds(head * HEAD, HEAD), :]
        ).astype(BF)
    own = own_mask()
    first_key = jnp.where(place_ref[0] == 0, WIN, 0)

    @pl.loop(0, count // TILE)
    def _(tile):
        start = pl.multiple_of(tile * TILE, TILE)
        queries = query_ref[:, pl.ds(start, TILE), :].reshape(HEADS * TILE, HEAD)
        scores = times_rows(queries, keyval_ref[pl.ds(start, SPAN), :HEAD]) * SCALE
        spot = start + lax.broadcasted_iota(jnp.int32, (1, SPAN), 1)
        scores = folded(jnp.where(spot >= first_key, scores, MASKED), own)
        raised = jnp.exp(scores - jnp.max(scores, axis=1, keepdims=True))
        probs = (raised / jnp.sum(raised, axis=1, keepdims=True)).astype(BF)
        probs_ref[pl.ds(pl.multiple_of(tile * HEADS * TILE, TILE), HEADS * TILE), :] = probs
        mixed = times_plain(unfolded(probs, own), keyval_ref[pl.ds(start, SPAN), HEAD:]).astype(BF)
        for head in range(HEADS):
            attended_ref[pl.ds(start, TILE), pl.ds(head * HEAD, HEAD)] = mixed[
                head * TILE : (head + 1) * TILE
            ]

    residual = inputs + times_plain(attended_ref[...], weight_out_ref[...])
    residual_ref[...] = residual
    normed_two_ref[...] = normalise(residual, gain_two)


GELU_A = math.sqrt(2.0 / math.pi)
GELU_B = 0.044715


def ffn_kernel(
    normed_ref, grad_ref, branch_in_ref, normed_grad_in_ref, w0, w1, w2, w3,
    branch_ref, normed_grad_ref, terms_ref, weight_ref, sems,
):
    step = pl.program_id(0)
    pieces = (w0, w1, w2, w3)

    @pl.when(step == 0)
    def _():
        for k in range(SIDE):
            pltpu.make_async_copy(pieces[k], weight_ref.at[k], sems.at[k]).start()
        branch_ref[...] = branch_in_ref[...]
        normed_grad_ref[...] = normed_grad_in_ref[...]

    pltpu.make_async_copy(w0, weight_ref.at[step], sems.at[step]).wait()
    units = weight_ref[step, 0:4].reshape(512, -1)
    down = weight_ref[step, 4:6].reshape(256, -1)
    normed = normed_ref[...]
    grad = grad_ref[...]
    both = times_rows(normed, units)
    gate, up = both[:, :256], both[:, 256:]
    hidden_grad = times_rows(grad, down)
    square = gate * gate
    bend = jnp.tanh(GELU_A * gate * (1.0 + GELU_B * square))
    half = 0.5 * (1.0 + bend)
    active = gate * half
    slope = half + 0.5 * gate * (1.0 - bend * bend) * (GELU_A + (3.0 * GELU_A * GELU_B) * square)
    hidden = (active * up).astype(BF)
    both_grad = jnp.concatenate(
        [(hidden_grad * up * slope).astype(BF), (hidden_grad * active).astype(BF)], axis=1
    )
    branch_ref[...] += times_plain(hidden, down)
    normed_grad_ref[...] += times_plain(both_grad, units)
    terms_ref[0, 0:4] = times_cols(both_grad, normed).astype(BF).reshape(4, 128, -1)
    terms_ref[0, 4:6] = times_cols(hidden, grad).astype(BF).reshape(2, 128, -1)


def ffn(normed_two, cotangent, branch, normed_grad, pieces):
    rows, width = normed_two.shape
    whole = pl.BlockSpec((rows, width), lambda i: (0, 0))
    return run(
        ffn_kernel,
        (
            shape((rows, width), F32),
            shape((rows, width), F32),
            shape((SIDE, 6, 128, width), BF),
        ),
        normed_two, cotangent, branch, normed_grad, *pieces,
        grid=(SIDE,),
        in_specs=[whole] * 4 + [pl.BlockSpec(memory_space=pl.ANY)] * 4,
        out_specs=(whole, whole, pl.BlockSpec((1, 6, 128, width), lambda i: (i, 0, 0, 0))),
        scratch=[pltpu.VMEM((SIDE, 6, 128, width), BF), pltpu.SemaphoreType.DMA((SIDE,))],
        flops=SIDE * 9 * 2 * rows * width * 256,
    )


def middle_kernel(
    residual_ref, normed_grad_ref, cotangent_ref, branch_ref, gains_ref, weight_out_ref, query_ref, keyval_ref, probs_ref, natural_ref,
    output_ref, residual_grad_ref, low_ref, query_grad_ref, own_ref, sent_ref, gain_ref,
    rows_ref, window_ref,
):
    count = residual_ref.shape[0]
    residual = residual_ref[...]
    output_ref[...] = (residual + branch_ref[...]).astype(BF)
    part, gain_grad = normalise_back(residual, gains_ref[1:2, :], normed_grad_ref[...])
    gain_ref[...] = jnp.broadcast_to(gain_grad, gain_ref.shape)
    residual_grad = cotangent_ref[...].astype(F32) + part
    residual_grad_ref[...] = residual_grad
    low = residual_grad.astype(BF)
    low_ref[...] = low
    for head in range(HEADS):
        rows_ref[head] = times_rows(low, weight_out_ref[pl.ds(head * HEAD, HEAD), :]).astype(BF)
    window_ref[...] = jnp.zeros_like(window_ref)
    own = own_mask()

    @pl.loop(0, count // TILE)
    def _(tile):
        start = pl.multiple_of(tile * TILE, TILE)
        span = pl.ds(start, SPAN)
        queries = query_ref[:, pl.ds(start, TILE), :].reshape(HEADS * TILE, HEAD)
        rows = rows_ref[:, pl.ds(start, TILE), :].reshape(HEADS * TILE, HEAD)
        low_probs = probs_ref[pl.ds(pl.multiple_of(tile * HEADS * TILE, TILE), HEADS * TILE), :]
        probs = low_probs.astype(F32)
        prob_grad = folded(times_rows(rows, keyval_ref[span, HEAD:]), own)
        centre = jnp.sum(probs * prob_grad, axis=1, keepdims=True) / jnp.sum(
            probs, axis=1, keepdims=True
        )
        score_grad = unfolded((probs * (prob_grad - centre)).astype(BF), own)
        mixed = (times_plain(score_grad, keyval_ref[span, :HEAD]) * SCALE).astype(BF)
        for head in range(HEADS):
            query_grad_ref[pl.ds(start, TILE), pl.ds(head * HEAD, HEAD)] = mixed[
                head * TILE : (head + 1) * TILE
            ]
        window_ref[span, :HEAD] += times_cols(score_grad, queries) * SCALE
        window_ref[span, HEAD:] += times_cols(unfolded(low_probs, own), rows)

    own_ref[...] = window_ref[WIN:, :]
    natural = natural_ref[...]
    sent_ref[:, :HEAD] = times_plain(window_ref[:WIN, :HEAD].astype(BF), natural).astype(BF)
    sent_ref[:, HEAD:] = times_plain(window_ref[:WIN, HEAD:].astype(BF), natural).astype(BF)


def weights_kernel(
    normed_ref, low_ref, attended_ref, query_grad_ref, weight_query_ref, normed_grad_ref, query_ref, out_ref
):
    query_grad = query_grad_ref[...]
    normed_grad_ref[...] = times_plain(query_grad, weight_query_ref[...])
    query_ref[...] = times_cols(query_grad, normed_ref[...]).astype(BF)
    out_ref[...] = times_cols(attended_ref[...], low_ref[...]).astype(BF)


def last_kernel(
    tokens_ref, normed_ref, own_ref, came_ref, natural_ref, select_ref, weight_keyval_ref, gains_ref,
    partial_ref, residual_grad_ref, gain_two_ref, query_ref, out_ref,
    input_grad_ref, mine_ref, other_ref,
):
    natural = natural_ref[...]
    keyval = jnp.concatenate(
        [
            own_ref[:, :HEAD] + times_rows(came_ref[:, :HEAD], natural),
            own_ref[:, HEAD:] + times_rows(came_ref[:, HEAD:], natural),
        ],
        axis=1,
    ).astype(BF)
    grad = partial_ref[...] + times_plain(keyval, weight_keyval_ref[...])
    part, gain_grad = normalise_back(tokens_ref[...].astype(F32), gains_ref[0:1, :], grad)
    input_grad_ref[...] = residual_grad_ref[...] + part
    row = lax.broadcasted_iota(jnp.int32, (16, gain_grad.shape[1]), 0)
    gain_rows = jnp.where(
        row == 0, gain_grad, jnp.where(row == 1, gain_two_ref[0:1, :], 0.0)
    ).astype(BF)
    rows = jnp.concatenate([times_cols(keyval, normed_ref[...]).astype(BF), gain_rows], axis=0)
    mixed = times_cols(select_ref[...], rows).astype(BF)
    for half in range(2):
        goal = (mine_ref, other_ref)[half]
        for last in range(SIDE):
            first = (half * SIDE + last) * 128
            goal[last, 2] = mixed[first : first + 128]
            for head in range(HEADS):
                here = pl.ds(head * HEAD + half * 128 + last * 32, 32)
                goal[last, 0, pl.ds(head * 32, 32), :] = query_ref[here, :]
                goal[last, 1, pl.ds(head * 32, 32), :] = out_ref[here, :]


def meet_kernel(mine_ref, came_ref, p0, p1, p2, p3):
    p0[...] = mine_ref[0].astype(F32) + came_ref[0].astype(F32)
    for k, goal in ((1, p1), (2, p2), (3, p3)):
        goal[...] = (mine_ref[k].astype(F32) + came_ref[k].astype(F32)).astype(BF)


def sum_kernel(cut, held_ref, c1, c2, c3, *goals):
    total = held_ref[...]
    for one in (c1, c2, c3):
        total = total + one[...].astype(F32)
    if cut == 0:
        goals[0][...] = total
        return
    groups, rows, width = total.shape
    blocks = total.reshape(groups, rows // (SIDE * 8) if cut == 2 else 1, SIDE, 8, width)
    for k in range(SIDE):
        goals[k][...] = blocks[:, :, k].reshape(groups, rows // SIDE, width).astype(goals[k].dtype)


def scattered(mine, came):
    _, groups, rows, width = mine.shape
    pieces = run(
        meet_kernel, [shape((groups, rows, width), F32 if k == 0 else BF) for k in range(SIDE)], mine, came
    )
    for stage in (2, 1, 0):
        rows = pieces[0].shape[1] // SIDE
        outs = [shape((groups, rows, width), F32 if k == 0 else BF) for k in range(SIDE)]
        if stage == 0:
            outs = [shape(pieces[0].shape, F32)]
        pieces = run(
            lambda *refs, stage=stage: sum_kernel(stage, *refs),
            outs,
            pieces[0],
            *scatter_stage(pieces, stage),
        )
    return pieces[0]


def local(tokens, gain_attn, gain_ffn, w_query, w_keyval, w_out, w_gate, w_up, w_down, cotangent):
    row_count, model_width = tokens.shape
    place = lax.axis_index(AXES)

    width = gain_attn.shape[0]
    lane = jnp.arange(model_width, dtype=jnp.int32)
    mine = lane // width == place
    gain_rows = jnp.where(
        mine[None, :], jnp.stack([jnp.tile(gain_attn, 128), jnp.tile(gain_ffn, 128)]), 0
    ).astype(BF)
    payload = jnp.concatenate(
        [w_query, w_out, w_keyval, jnp.pad(gain_rows, ((0, 2), (0, 0))), w_gate, w_up, w_down]
    ).reshape(9, 8, model_width)
    before = shifted(tokens, 1)
    payload = jnp.stack(gather_stage(payload, 0), axis=1)
    payload = jnp.stack(gather_stage(payload, 1), axis=2)
    attn = gather_stage(payload[:3].reshape(3, 128, model_width), 2)
    attn += [to_sibling(one) for one in attn]
    units = gather_stage(payload[3:].reshape(6, 128, model_width), 2)
    others = [to_sibling(one) for one in units]
    select, natural = selectors(place)

    (
        residual, normed_two, normed, queries, keyvals, attended, probs, weight_query, weight_out, weight_keyval, gains
    ) = run(
        forward_kernel,
        (
            shape((row_count, model_width), F32),
            shape((row_count, model_width), BF),
            shape((row_count, model_width), BF),
            shape((HEADS, row_count, HEAD), BF),
            shape((2 * row_count, 2 * HEAD), BF),
            shape((row_count, HEADS * HEAD), BF),
            shape((HEADS * row_count, WIN), BF),
            shape((HEADS * HEAD, model_width), BF),
            shape((HEADS * HEAD, model_width), BF),
            shape((2 * HEAD, model_width), BF),
            shape((8, model_width), F32),
        ),
        place.reshape(1), tokens, before, select, *attn,
        in_specs=[pl.BlockSpec(memory_space=pltpu.SMEM)] + [pl.BlockSpec(memory_space=pltpu.VMEM)] * 11,
        flops=6 * 10**9,
    )

    nothing = jnp.zeros((row_count, model_width), F32)
    branch, normed_grad, mine = ffn(normed_two, cotangent, nothing, nothing, units)
    branch, normed_grad, other = ffn(normed_two, cotangent, branch, normed_grad, others)
    ffn_grads = scattered(mine, to_sibling(other))

    output, residual_grad, low, query_grad, keyval_own, keyval_sent, gain_two_grad = run(
        middle_kernel,
        (
            shape((row_count, model_width), BF),
            shape((row_count, model_width), F32),
            shape((row_count, model_width), BF),
            shape((row_count, HEADS * HEAD), BF),
            shape((row_count, 2 * HEAD), F32),
            shape((row_count, 2 * HEAD), BF),
            shape((8, model_width), F32),
        ),
        residual, normed_grad, cotangent, branch, gains, weight_out, queries, keyvals, probs, natural,
        scratch=[pltpu.VMEM((HEADS, row_count, HEAD), BF), pltpu.VMEM((2 * row_count, 2 * HEAD), F32)],
        flops=5 * 10**9,
    )
    came = shifted(keyval_sent, -1)
    partial, query_term, out_term = run(
        weights_kernel,
        (
            shape((row_count, model_width), F32),
            shape((HEADS * HEAD, model_width), BF),
            shape((HEADS * HEAD, model_width), BF),
        ),
        normed, low, attended, query_grad, weight_query,
        flops=2 * 10**9,
    )
    input_grad, mine, other = run(
        last_kernel,
        (
            shape((row_count, model_width), F32),
            shape((SIDE, 3, 128, model_width), BF),
            shape((SIDE, 3, 128, model_width), BF),
        ),
        tokens, normed, keyval_own, came, natural, select, weight_keyval, gains,
        partial, residual_grad, gain_two_grad, query_term, out_term,
        flops=2 * 10**9,
    )
    attn_grads = scattered(mine, to_sibling(other))
    gain_shares = lax.dynamic_slice_in_dim(attn_grads[2, 4:6], place * width, width, 1)
    ffn_grads = ffn_grads.reshape(3, 16, model_width)
    return (
        output,
        input_grad,
        attn_grads[0],
        attn_grads[2, :4],
        attn_grads[1],
        ffn_grads[0],
        ffn_grads[1],
        ffn_grads[2],
        gain_shares[0],
        gain_shares[1],
    )


def solution(mesh):
    rows, flat = P(AXES, None), P(AXES)
    return jax.shard_map(
        local,
        mesh=mesh,
        in_specs=(rows, flat, flat, rows, rows, rows, rows, rows, rows, rows),
        out_specs=(rows, rows, rows, rows, rows, rows, rows, rows, flat, flat),
        check_vma=False,
    )
```

```python
import math

import jax
import jax.numpy as jnp
from jax import lax
from jax.experimental import pallas as pl
from jax.experimental.pallas import tpu as pltpu
from jax.sharding import PartitionSpec as P

HEADS = 4
HEAD = 256
WIN = 512
SIDE = 4

EPSILON = 1e-06
MASKED = -1e30
AXES = ("ctx", "hd")
BF = jnp.bfloat16
F32 = jnp.float32

SCALE = 1.0 / math.sqrt(HEAD)
TILE = 128
SPAN = WIN + TILE
MEGA = 1 << 20

ORDER = ((0, 0), (1, 2), (2, 1))


def chip_pairs(axis_of_core, steps):
    pairs = []
    for chip in range(SIDE**3):
        spot = [chip // SIDE**2, chip // SIDE % SIDE, chip % SIDE]
        for core in range(2):
            goal = list(spot)
            axis = axis_of_core[core]
            goal[axis] = (goal[axis] + steps) % SIDE
            target = (goal[0] * SIDE + goal[1]) * SIDE + goal[2]
            pairs.append((chip * 2 + core, target * 2 + core))
    return pairs


def to_sibling(value):
    return lax.ppermute(value, "hd", [(0, 1), (1, 0)])


def gather_stage(value, stage):
    return [value] + [
        lax.ppermute(value, AXES, chip_pairs(ORDER[stage], -steps)) for steps in range(1, SIDE)
    ]


def scatter_stage(pieces, stage):
    return [
        lax.ppermute(pieces[steps], AXES, chip_pairs(ORDER[stage], steps))
        for steps in range(1, SIDE)
    ]


def shifted(value, steps):
    count = lax.axis_size(AXES)
    initial, last = (max(0, -steps), min(count, count - steps))
    return lax.ppermute(value, AXES, [(source, source + steps) for source in range(initial, last)])


def times_rows(left, right):
    return lax.dot_general(left, right, (((1,), (1,)), ((), ())), preferred_element_type=F32)


def times_cols(left, right):
    return lax.dot_general(left, right, (((0,), (0,)), ((), ())), preferred_element_type=F32)


def times_plain(left, right):
    return jnp.dot(left, right, preferred_element_type=F32)


def shape(dims, kind):
    return jax.ShapeDtypeStruct(dims, kind)


WHOLE = pl.BlockSpec(memory_space=pltpu.VMEM)
ANYWHERE = pl.BlockSpec(memory_space=pl.ANY)


def run(kernel, outs, *operands, after=(), flops=0, limit=32, in_specs=None, **more):
    moved = sum(one.size * one.dtype.itemsize for one in operands)
    moved += sum(math.prod(one.shape) * one.dtype.itemsize for one in outs)
    count = len(operands)

    def body(*refs):
        kernel(*refs[:count], *refs[count + len(after) :])

    return pl.pallas_call(
        body,
        out_shape=outs,
        in_specs=list(in_specs or [WHOLE] * count) + [ANYWHERE] * len(after),
        cost_estimate=pl.CostEstimate(flops=flops, bytes_accessed=moved, transcendentals=0),
        compiler_params=pltpu.CompilerParams(vmem_limit_bytes=limit * MEGA),
        **more,
    )(*operands, *after)


def selectors(place):
    core = place % 2
    chip = place // 2
    spot = [chip // SIDE**2, chip // SIDE % SIDE, chip % SIDE]

    def device_of(half, first, last, mid):
        owner = jnp.bitwise_xor(core, half)
        x = (spot[0] + first) % SIDE
        y = (spot[1] + jnp.where(owner == 0, mid, last)) % SIDE
        z = (spot[2] + jnp.where(owner == 0, last, mid)) % SIDE
        return ((x * SIDE + y) * SIDE + z) * 2 + owner

    row = jnp.arange(528, dtype=jnp.int32)
    kind, feature = row // HEAD, row % HEAD
    device = device_of(feature // 128, 0 * row, feature // 32 % 4, feature // 8 % 4)
    goal = kind * HEAD + device % 32 * 8 + feature % 8
    column = jnp.arange(1024, dtype=jnp.int32)
    device = device_of(column // 512, column // 32 % 4, column // 128 % 4, column // 8 % 4)
    part = column % 8
    have = jnp.where(part < 4, device * 4 + part, -1)
    keyval = (goal[:, None] == have[None, :]) & (row[:, None] < 512)
    gains = (row[:, None] >= 512) & (part[None, :] == row[:, None] - 508) & (part[None, :] < 6)
    natural = (goal[:HEAD, None] == row[None, :HEAD]).astype(BF)
    return (keyval | gains).astype(BF), natural


def normalise(values, gain):
    inverse = lax.rsqrt(jnp.mean(values * values, axis=-1, keepdims=True) + EPSILON)
    return (values * inverse * gain).astype(BF)


def normalise_back(values, gain, grad):
    inverse = lax.rsqrt(jnp.mean(values * values, axis=-1, keepdims=True) + EPSILON)
    unit = values * inverse
    gain_grad = jnp.sum(grad * unit, axis=0, keepdims=True)
    scaled = grad * gain
    return inverse * (scaled - unit * jnp.mean(scaled * unit, axis=-1, keepdims=True)), gain_grad


def own_mask():
    row = lax.broadcasted_iota(jnp.int32, (HEADS * TILE, TILE), 0) % TILE
    column = lax.broadcasted_iota(jnp.int32, (HEADS * TILE, TILE), 1)
    return column <= row


def folded(wide, own):
    return jnp.concatenate(
        [jnp.where(own, wide[:, WIN:], wide[:, :TILE]), wide[:, TILE:WIN]], axis=1
    )


def unfolded(narrow, own):
    edge = narrow[:, :TILE]
    none = jnp.zeros_like(edge)
    return jnp.concatenate(
        [jnp.where(own, none, edge), narrow[:, TILE:], jnp.where(own, edge, none)], axis=1
    )


def payload_kernel(
    place_ref, query_ref, out_ref, keyval_ref, gate_ref, up_ref, down_ref, gain_one_ref, gain_two_ref, payload_ref
):
    width = gain_one_ref.shape[1]
    row = lax.broadcasted_iota(jnp.int32, (8, query_ref.shape[1]), 0)
    lane = lax.broadcasted_iota(jnp.int32, (8, query_ref.shape[1]), 1) - place_ref[0] * width
    gains = jnp.zeros(row.shape, F32)
    for k, ref in ((4, gain_one_ref), (5, gain_two_ref)):
        values = ref[...].astype(F32)
        for i in range(width):
            gains = jnp.where((row == k) & (lane == i), values[:, i : i + 1], gains)
    keyval = jnp.concatenate([keyval_ref[...].astype(F32), gains[4:]], axis=0)
    payload_ref[0] = query_ref[...]
    payload_ref[1] = out_ref[...]
    payload_ref[2] = keyval.astype(BF)
    for k, ref in ((3, gate_ref), (5, up_ref), (7, down_ref)):
        payload_ref[k : k + 2] = ref[...].reshape(2, 8, -1)


def pack_kernel(r0, r1, r2, r3, goal_ref):
    groups, rows, width = r0.shape
    for k, ref in enumerate((r0, r1, r2, r3)):
        goal_ref[:, k] = ref[...]


def pack_two_kernel(r0, r1, r2, r3, attn_ref, units_ref):
    for k, ref in enumerate((r0, r1, r2, r3)):
        attn_ref[:, :, k] = ref[:3]
        units_ref[:, :, k] = ref[3:]


def nothing_kernel(*refs):
    pass


def forward_kernel(
    place_ref, tokens_ref, before_ref, select_ref, a0, a1, a2, a3, b0, b1, b2, b3,
    residual_ref, normed_two_ref, normed_ref, query_ref, keyval_ref, attended_ref, probs_ref,
    weight_query_ref, weight_out_ref, weight_keyval_ref, gains_ref,
):
    count = tokens_ref.shape[0]
    halves = ((a0, a1, a2, a3), (b0, b1, b2, b3))
    for head in range(HEADS):
        for half in range(2):
            for last in range(SIDE):
                here = pl.ds(head * HEAD + half * 128 + last * 32, 32)
                weight_query_ref[here, :] = halves[half][last][0, pl.ds(head * 32, 32), :]
                weight_out_ref[here, :] = halves[half][last][1, pl.ds(head * 32, 32), :]
    mixed = jnp.concatenate([one[2] for half in halves for one in half], axis=0)
    sorted_rows = times_plain(select_ref[...], mixed)
    weight_keyval_ref[...] = sorted_rows[:512].astype(BF)
    gains_ref[...] = sorted_rows[512:520]
    gain_one = sorted_rows[512:513]
    gain_two = sorted_rows[513:514]
    inputs = tokens_ref[...].astype(F32)
    normed = normalise(inputs, gain_one)
    normed_ref[...] = normed
    normed_before = normalise(before_ref[...].astype(F32), gain_one)
    weight_keyval = weight_keyval_ref[...]
    keyval_ref[:WIN, :] = times_rows(normed_before, weight_keyval).astype(BF)
    keyval_ref[WIN:, :] = times_rows(normed, weight_keyval).astype(BF)
    for head in range(HEADS):
        query_ref[head] = times_rows(
            normed, weight_query_ref[pl.ds(head * HEAD, HEAD), :]
        ).astype(BF)
    own = own_mask()
    first_key = jnp.where(place_ref[0] == 0, WIN, 0)

    @pl.loop(0, count // TILE)
    def _(tile):
        start = pl.multiple_of(tile * TILE, TILE)
        queries = query_ref[:, pl.ds(start, TILE), :].reshape(HEADS * TILE, HEAD)
        scores = times_rows(queries, keyval_ref[pl.ds(start, SPAN), :HEAD]) * SCALE
        spot = start + lax.broadcasted_iota(jnp.int32, (1, SPAN), 1)
        scores = folded(jnp.where(spot >= first_key, scores, MASKED), own)
        raised = jnp.exp(scores - jnp.max(scores, axis=1, keepdims=True))
        probs = (raised / jnp.sum(raised, axis=1, keepdims=True)).astype(BF)
        probs_ref[pl.ds(pl.multiple_of(tile * HEADS * TILE, TILE), HEADS * TILE), :] = probs
        mixed = times_plain(unfolded(probs, own), keyval_ref[pl.ds(start, SPAN), HEAD:]).astype(BF)
        for head in range(HEADS):
            attended_ref[pl.ds(start, TILE), pl.ds(head * HEAD, HEAD)] = mixed[
                head * TILE : (head + 1) * TILE
            ]

    residual = inputs + times_plain(attended_ref[...], weight_out_ref[...])
    residual_ref[...] = residual
    normed_two_ref[...] = normalise(residual, gain_two)


GELU_A = math.sqrt(2.0 / math.pi)
GELU_B = 0.044715


def ffn_kernel(
    first, normed_ref, grad_ref, branch_in_ref, normed_grad_in_ref, w0, w1, w2, w3,
    branch_ref, normed_grad_ref, terms_ref, *more,
):
    output_ref, (weight_ref, sems) = (None, more) if first else (more[0], more[1:])
    step = pl.program_id(0)
    pieces = (w0, w1, w2, w3)

    @pl.when(step == 0)
    def _():
        for k in range(SIDE):
            pltpu.make_async_copy(pieces[k], weight_ref.at[k], sems.at[k]).start()
        branch_ref[...] = branch_in_ref[...]
        normed_grad_ref[...] = jnp.zeros_like(normed_grad_ref) if first else normed_grad_in_ref[...]

    pltpu.make_async_copy(w0, weight_ref.at[step], sems.at[step]).wait()
    units = weight_ref[step, 0:4].reshape(512, -1)
    down = weight_ref[step, 4:6].reshape(256, -1)
    normed = normed_ref[...]
    grad = grad_ref[...]
    both = times_rows(normed, units)
    gate, up = both[:, :256], both[:, 256:]
    hidden_grad = times_rows(grad, down)
    square = gate * gate
    bend = jnp.tanh(GELU_A * gate * (1.0 + GELU_B * square))
    half = 0.5 * (1.0 + bend)
    active = gate * half
    slope = half + 0.5 * gate * (1.0 - bend * bend) * (GELU_A + (3.0 * GELU_A * GELU_B) * square)
    hidden = (active * up).astype(BF)
    both_grad = jnp.concatenate(
        [(hidden_grad * up * slope).astype(BF), (hidden_grad * active).astype(BF)], axis=1
    )
    branch_ref[...] += times_plain(hidden, down)
    normed_grad_ref[...] += times_plain(both_grad, units)
    terms_ref[0, 0:4] = times_cols(both_grad, normed).astype(BF).reshape(4, 128, -1)
    terms_ref[0, 4:6] = times_cols(hidden, grad).astype(BF).reshape(2, 128, -1)
    if not first:

        @pl.when(step == SIDE - 1)
        def _():
            output_ref[...] = branch_ref[...].astype(BF)


def ffn(first, normed_two, cotangent, branch, normed_grad, pieces):
    rows, width = normed_two.shape
    whole = pl.BlockSpec((rows, width), lambda i: (0, 0))
    more = () if first else (shape((rows, width), BF),)
    return run(
        lambda *refs: ffn_kernel(first, *refs),
        (shape((rows, width), F32), shape((rows, width), F32), shape((SIDE, 6, 128, width), BF)) + more,
        normed_two, cotangent, branch, normed_grad, *pieces,
        grid=(SIDE,),
        in_specs=[whole] * 3 + [ANYWHERE if first else whole] + [ANYWHERE] * 4,
        out_specs=(whole, whole, pl.BlockSpec((1, 6, 128, width), lambda i: (i, 0, 0, 0))) + (whole,) * len(more),
        scratch_shapes=[pltpu.VMEM((SIDE, 6, 128, width), BF), pltpu.SemaphoreType.DMA((SIDE,))],
        flops=SIDE * 9 * 2 * rows * width * 256,
    )


def middle_kernel(
    residual_ref, normed_grad_ref, cotangent_ref, gains_ref, weight_out_ref, query_ref, keyval_ref, probs_ref, natural_ref,
    residual_grad_ref, low_ref, query_grad_ref, own_ref, sent_ref, gain_ref,
    rows_ref, window_ref,
):
    count = residual_ref.shape[0]
    residual = residual_ref[...]
    part, gain_grad = normalise_back(residual, gains_ref[1:2, :], normed_grad_ref[...])
    gain_ref[...] = jnp.broadcast_to(gain_grad, gain_ref.shape)
    residual_grad = cotangent_ref[...].astype(F32) + part
    residual_grad_ref[...] = residual_grad
    low = residual_grad.astype(BF)
    low_ref[...] = low
    for head in range(HEADS):
        rows_ref[head] = times_rows(low, weight_out_ref[pl.ds(head * HEAD, HEAD), :]).astype(BF)
    window_ref[...] = jnp.zeros_like(window_ref)
    own = own_mask()

    @pl.loop(0, count // TILE)
    def _(tile):
        start = pl.multiple_of(tile * TILE, TILE)
        span = pl.ds(start, SPAN)
        queries = query_ref[:, pl.ds(start, TILE), :].reshape(HEADS * TILE, HEAD)
        rows = rows_ref[:, pl.ds(start, TILE), :].reshape(HEADS * TILE, HEAD)
        low_probs = probs_ref[pl.ds(pl.multiple_of(tile * HEADS * TILE, TILE), HEADS * TILE), :]
        probs = low_probs.astype(F32)
        prob_grad = folded(times_rows(rows, keyval_ref[span, HEAD:]), own)
        centre = jnp.sum(probs * prob_grad, axis=1, keepdims=True) / jnp.sum(
            probs, axis=1, keepdims=True
        )
        score_grad = unfolded((probs * (prob_grad - centre)).astype(BF), own)
        mixed = (times_plain(score_grad, keyval_ref[span, :HEAD]) * SCALE).astype(BF)
        for head in range(HEADS):
            query_grad_ref[pl.ds(start, TILE), pl.ds(head * HEAD, HEAD)] = mixed[
                head * TILE : (head + 1) * TILE
            ]
        window_ref[span, :HEAD] += times_cols(score_grad, queries) * SCALE
        window_ref[span, HEAD:] += times_cols(unfolded(low_probs, own), rows)

    own_ref[...] = window_ref[WIN:, :]
    natural = natural_ref[...]
    sent_ref[:, :HEAD] = times_plain(window_ref[:WIN, :HEAD].astype(BF), natural).astype(BF)
    sent_ref[:, HEAD:] = times_plain(window_ref[:WIN, HEAD:].astype(BF), natural).astype(BF)


def weights_kernel(
    normed_ref, low_ref, attended_ref, query_grad_ref, weight_query_ref, normed_grad_ref, query_ref, out_ref
):
    query_grad = query_grad_ref[...]
    normed_grad_ref[...] = times_plain(query_grad, weight_query_ref[...])
    query_ref[...] = times_cols(query_grad, normed_ref[...]).astype(BF)
    out_ref[...] = times_cols(attended_ref[...], low_ref[...]).astype(BF)


def last_kernel(
    tokens_ref, normed_ref, own_ref, came_ref, natural_ref, select_ref, weight_keyval_ref, gains_ref,
    partial_ref, residual_grad_ref, gain_two_ref, query_ref, out_ref,
    input_grad_ref, mine_ref, other_ref,
):
    natural = natural_ref[...]
    keyval = jnp.concatenate(
        [
            own_ref[:, :HEAD] + times_rows(came_ref[:, :HEAD], natural),
            own_ref[:, HEAD:] + times_rows(came_ref[:, HEAD:], natural),
        ],
        axis=1,
    ).astype(BF)
    grad = partial_ref[...] + times_plain(keyval, weight_keyval_ref[...])
    part, gain_grad = normalise_back(tokens_ref[...].astype(F32), gains_ref[0:1, :], grad)
    input_grad_ref[...] = residual_grad_ref[...] + part
    row = lax.broadcasted_iota(jnp.int32, (16, gain_grad.shape[1]), 0)
    gain_rows = jnp.where(
        row == 0, gain_grad, jnp.where(row == 1, gain_two_ref[0:1, :], 0.0)
    ).astype(BF)
    rows = jnp.concatenate([times_cols(keyval, normed_ref[...]).astype(BF), gain_rows], axis=0)
    mixed = times_cols(select_ref[...], rows).astype(BF)
    for half in range(2):
        goal = (mine_ref, other_ref)[half]
        for last in range(SIDE):
            first = (half * SIDE + last) * 128
            goal[last, 2] = mixed[first : first + 128]
            for head in range(HEADS):
                here = pl.ds(head * HEAD + half * 128 + last * 32, 32)
                goal[last, 0, pl.ds(head * 32, 32), :] = query_ref[here, :]
                goal[last, 1, pl.ds(head * 32, 32), :] = out_ref[here, :]


def meet_kernel(mine_ref, came_ref, p0, p1, p2, p3):
    p0[...] = mine_ref[0].astype(F32) + came_ref[0].astype(F32)
    for k, goal in ((1, p1), (2, p2), (3, p3)):
        goal[...] = (mine_ref[k].astype(F32) + came_ref[k].astype(F32)).astype(BF)


def meet(mine, came, after=()):
    _, groups, rows, width = mine.shape
    both = pl.BlockSpec((SIDE, 3, rows, width), lambda i: (0, i, 0, 0))
    return run(
        meet_kernel,
        [shape((groups, rows, width), F32 if k == 0 else BF) for k in range(SIDE)],
        mine, came,
        after=after,
        grid=(groups // 3,),
        in_specs=[both] * 2,
        out_specs=[pl.BlockSpec((3, rows, width), lambda i: (i, 0, 0))] * SIDE,
    )


def summed(refs):
    total = refs[0][...]
    for one in refs[1:]:
        total = total + one[...].astype(F32)
    return total


def middle_sum_kernel(*refs):
    total = summed(refs[:SIDE])
    groups, rows, width = total.shape
    blocks = total.reshape(groups, SIDE, SIDE, 8, width)
    for k, goal in enumerate(refs[SIDE:]):
        goal[...] = blocks[:, :, k].reshape(groups, 4 * 8, width).astype(goal.dtype)


def middle_sum(held, came, after=()):
    groups, rows, width = held.shape
    return run(
        middle_sum_kernel,
        [shape((groups, rows // SIDE, width), F32 if k == 0 else BF) for k in range(SIDE)],
        held, *came,
        after=after,
        grid=(groups // 3,),
        in_specs=[pl.BlockSpec((3, rows, width), lambda i: (i, 0, 0))] * SIDE,
        out_specs=[pl.BlockSpec((3, rows // SIDE, width), lambda i: (i, 0, 0))] * SIDE,
    )


def first_sum_kernel(*refs):
    for first, groups, parts in ((0, 3, refs[:SIDE]), (3, 6, refs[SIDE : 2 * SIDE])):
        total = summed(parts)
        for k, goal in enumerate(refs[2 * SIDE :]):
            goal[first : first + groups] = total[:, 8 * k : 8 * k + 8].astype(goal.dtype)


def end_kernel(place_ref, r0, r1, r2, r3, query_ref, keyval_ref, out_ref, gate_ref, up_ref, down_ref, one_ref, two_ref):
    total = summed((r0, r1, r2, r3))
    query_ref[...] = total[0]
    out_ref[...] = total[1]
    keyval_ref[...] = total[2, :4]
    for k, goal in ((3, gate_ref), (5, up_ref), (7, down_ref)):
        goal[...] = total[k : k + 2].reshape(goal.shape)
    width = one_ref.shape[0]
    full = total.shape[-1]
    rows = pltpu.roll(total[2], lax.rem(full - place_ref[0] * width, full), 1)
    one_ref[...] = rows[4, :width]
    two_ref[...] = rows[5, :width]


def local(tokens, gain_attn, gain_ffn, w_query, w_keyval, w_out, w_gate, w_up, w_down, cotangent):
    row_count, model_width = tokens.shape
    place = lax.axis_index(AXES)

    before = shifted(tokens, 1)
    spot = place.reshape(1)
    scalar = pl.BlockSpec(memory_space=pltpu.SMEM)
    payload, = run(
        payload_kernel,
        [shape((9, 8, model_width), BF)],
        spot, w_query, w_out, w_keyval, w_gate, w_up, w_down, gain_attn[None], gain_ffn[None],
        in_specs=[scalar] + [WHOLE] * 8,
    )
    payload, = run(
        pack_kernel, [shape((9, SIDE, 8, model_width), BF)], *gather_stage(payload, 0)
    )
    attn, units = run(
        pack_two_kernel,
        [shape((3, SIDE, SIDE, 8, model_width), BF), shape((6, SIDE, SIDE, 8, model_width), BF)],
        *gather_stage(payload, 1),
        after=(before,),
    )
    attn = gather_stage(attn.reshape(3, 128, model_width), 2)
    units = gather_stage(units.reshape(6, 128, model_width), 2)
    attn += [to_sibling(one) for one in attn]
    select, natural = selectors(place)

    (
        residual, normed_two, normed, queries, keyvals, attended, probs, weight_query, weight_out, weight_keyval, gains
    ) = run(
        forward_kernel,
        (
            shape((row_count, model_width), F32),
            shape((row_count, model_width), BF),
            shape((row_count, model_width), BF),
            shape((HEADS, row_count, HEAD), BF),
            shape((2 * row_count, 2 * HEAD), BF),
            shape((row_count, HEADS * HEAD), BF),
            shape((HEADS * row_count, WIN), BF),
            shape((HEADS * HEAD, model_width), BF),
            shape((HEADS * HEAD, model_width), BF),
            shape((2 * HEAD, model_width), BF),
            shape((8, model_width), F32),
        ),
        spot, tokens, before, select, *attn,
        in_specs=[scalar] + [WHOLE] * 11,
        flops=6 * 10**9,
    )

    units = run(
        nothing_kernel,
        [shape(one.shape, one.dtype) for one in units],
        *units,
        after=(normed_two,),
        in_specs=[ANYWHERE] * SIDE,
        out_specs=[ANYWHERE] * SIDE,
        input_output_aliases={k: k for k in range(SIDE)},
    )
    others = [to_sibling(one) for one in units]
    branch, normed_grad, mine = ffn(True, normed_two, cotangent, residual, residual, units)
    branch, normed_grad, other, output = ffn(False, normed_two, cotangent, branch, normed_grad, others)
    ffn_came = to_sibling(other)

    residual_grad, low, query_grad, keyval_own, keyval_sent, gain_two_grad = run(
        middle_kernel,
        (
            shape((row_count, model_width), F32),
            shape((row_count, model_width), BF),
            shape((row_count, HEADS * HEAD), BF),
            shape((row_count, 2 * HEAD), F32),
            shape((row_count, 2 * HEAD), BF),
            shape((8, model_width), F32),
        ),
        residual, normed_grad, cotangent, gains, weight_out, queries, keyvals, probs, natural,
        scratch_shapes=[pltpu.VMEM((HEADS, row_count, HEAD), BF), pltpu.VMEM((2 * row_count, 2 * HEAD), F32)],
        flops=5 * 10**9,
    )
    ffn_pieces = meet(mine, ffn_came, after=(low,))
    ffn_back = scatter_stage(ffn_pieces, 2)
    came = shifted(keyval_sent, -1)
    partial, query_term, out_term = run(
        weights_kernel,
        (
            shape((row_count, model_width), F32),
            shape((HEADS * HEAD, model_width), BF),
            shape((HEADS * HEAD, model_width), BF),
        ),
        normed, low, attended, query_grad, weight_query,
        after=(ffn_pieces[1],),
        flops=2 * 10**9,
    )
    input_grad, mine, other = run(
        last_kernel,
        (
            shape((row_count, model_width), F32),
            shape((SIDE, 3, 128, model_width), BF),
            shape((SIDE, 3, 128, model_width), BF),
        ),
        tokens, normed, keyval_own, came, natural, select, weight_keyval, gains,
        partial, residual_grad, gain_two_grad, query_term, out_term,
        flops=2 * 10**9,
    )
    attn_pieces = meet(mine, to_sibling(other))
    attn_back = scatter_stage(attn_pieces, 2)
    ffn_pieces = middle_sum(ffn_pieces[0], ffn_back, after=(attn_pieces[1],))
    ffn_back = scatter_stage(ffn_pieces, 1)
    attn_pieces = middle_sum(attn_pieces[0], attn_back, after=(ffn_pieces[1],))
    attn_back = scatter_stage(attn_pieces, 1)
    pieces = run(
        first_sum_kernel,
        [shape((9, 8, model_width), F32 if k == 0 else BF) for k in range(SIDE)],
        attn_pieces[0], *attn_back, ffn_pieces[0], *ffn_back,
    )
    query, keyval, out, gate, up, down, gain_one, gain_two = run(
        end_kernel,
        [shape(one.shape, F32) for one in (w_query, w_keyval, w_out, w_gate, w_up, w_down, gain_attn, gain_ffn)],
        spot, pieces[0], *scatter_stage(pieces, 0),
        in_specs=[scalar] + [WHOLE] * SIDE,
    )
    return output, input_grad, query, keyval, out, gate, up, down, gain_one, gain_two


def solution(mesh):
    rows, flat = P(AXES, None), P(AXES)
    return jax.shard_map(
        local,
        mesh=mesh,
        in_specs=(rows, flat, flat, rows, rows, rows, rows, rows, rows, rows),
        out_specs=(rows, rows, rows, rows, rows, rows, rows, rows, flat, flat),
        check_vma=False,
    )
```

```python
import math

import jax
import jax.numpy as jnp
from jax import lax
from jax.experimental import pallas as pl
from jax.experimental.pallas import tpu as pltpu
from jax.sharding import PartitionSpec as P

HEADS = 4
HEAD = 256
WIN = 512
SIDE = 4

EPSILON = 1e-06
MASKED = -1e30
AXES = ("ctx", "hd")
BF = jnp.bfloat16
F32 = jnp.float32

SCALE = 1.0 / math.sqrt(HEAD)
TILE = 128
SPAN = WIN + TILE
MEGA = 1 << 20

ORDER = ((2, 0), (1, 2), (0, 1))


def chip_pairs(axis_of_core, steps):
    pairs = []
    for chip in range(SIDE**3):
        spot = [chip // SIDE**2, chip // SIDE % SIDE, chip % SIDE]
        for core in range(2):
            goal = list(spot)
            axis = axis_of_core[core]
            goal[axis] = (goal[axis] + steps) % SIDE
            target = (goal[0] * SIDE + goal[1]) * SIDE + goal[2]
            pairs.append((chip * 2 + core, target * 2 + core))
    return pairs


def to_sibling(value):
    return lax.ppermute(value, "hd", [(0, 1), (1, 0)])


def gather_stage(value, stage):
    return [value] + [
        lax.ppermute(value, AXES, chip_pairs(ORDER[stage], -steps)) for steps in range(1, SIDE)
    ]


def scatter_stage(pieces, stage):
    return [
        lax.ppermute(pieces[steps], AXES, chip_pairs(ORDER[stage], steps))
        for steps in range(1, SIDE)
    ]


def shifted(value, steps):
    count = lax.axis_size(AXES)
    initial, last = (max(0, -steps), min(count, count - steps))
    return lax.ppermute(value, AXES, [(source, source + steps) for source in range(initial, last)])


def times_rows(left, right):
    return lax.dot_general(left, right, (((1,), (1,)), ((), ())), preferred_element_type=F32)


def times_cols(left, right):
    return lax.dot_general(left, right, (((0,), (0,)), ((), ())), preferred_element_type=F32)


def times_plain(left, right):
    return jnp.dot(left, right, preferred_element_type=F32)


def shape(dims, kind):
    return jax.ShapeDtypeStruct(dims, kind)


WHOLE = pl.BlockSpec(memory_space=pltpu.VMEM)
ANYWHERE = pl.BlockSpec(memory_space=pl.ANY)
OUTSIDE = pl.BlockSpec(memory_space=pltpu.HBM)


def run(kernel, outs, *operands, after=(), limit=16, flops=1, in_specs=None, **more):
    count = len(operands)

    def body(*refs):
        kernel(*refs[:count], *refs[count + len(after) :])

    return pl.pallas_call(
        body,
        out_shape=outs,
        in_specs=list(in_specs or [WHOLE] * count) + [ANYWHERE] * len(after),
        cost_estimate=pl.CostEstimate(flops=flops, bytes_accessed=1, transcendentals=0),
        compiler_params=pltpu.CompilerParams(vmem_limit_bytes=limit * MEGA),
        **more,
    )(*operands, *after)


def select_kernel(place_ref, select_ref, natural_ref):
    place = place_ref[0]
    core = place % 2
    chip = place // 2
    spot = [chip // SIDE**2, chip // SIDE % SIDE, chip % SIDE]

    def device_of(half, piece, first, second):
        owner = half * (1 - core) + (1 - half) * core
        x = (spot[0] + jnp.where(owner == 0, piece, first)) % SIDE
        y = (spot[1] + jnp.where(owner == 0, second, piece)) % SIDE
        z = (spot[2] + jnp.where(owner == 0, first, second)) % SIDE
        return ((x * SIDE + y) * SIDE + z) * 2 + owner

    row = lax.broadcasted_iota(jnp.int32, (528, 1), 0)
    feature = row % HEAD
    high, low = feature // 32 % 4, feature // 8 % 4
    device = device_of(feature // 128, high, high, low)
    goal = jnp.where(row < 512, row // HEAD * HEAD + device % 32 * 8 + feature % 8, -2)
    column = lax.broadcasted_iota(jnp.int32, (1, 1024), 1)
    device = device_of(column // 512, column // 128 % 4, column // 32 % 4, column // 8 % 4)
    part = column % 8
    have = jnp.where(part < 4, device * 4 + part, -1)
    gain = jnp.where(row >= 512, row - 508, -1)
    select_ref[...] = jnp.where(
        (goal == have) | ((gain == part) & (part < 6)), 1.0, 0.0
    ).astype(BF)
    natural_ref[...] = jnp.where(
        goal[:HEAD] == lax.broadcasted_iota(jnp.int32, (1, HEAD), 1), 1.0, 0.0
    ).astype(BF)


def normalise(values, gain):
    inverse = lax.rsqrt(jnp.mean(values * values, axis=-1, keepdims=True) + EPSILON)
    return (values * inverse * gain).astype(BF)


def normalise_back(values, gain, grad):
    inverse = lax.rsqrt(jnp.mean(values * values, axis=-1, keepdims=True) + EPSILON)
    unit = values * inverse
    gain_grad = jnp.sum(grad * unit, axis=0, keepdims=True)
    scaled = grad * gain
    return inverse * (scaled - unit * jnp.mean(scaled * unit, axis=-1, keepdims=True)), gain_grad


def own_mask():
    row = lax.broadcasted_iota(jnp.int32, (HEADS * TILE, TILE), 0) % TILE
    column = lax.broadcasted_iota(jnp.int32, (HEADS * TILE, TILE), 1)
    return column <= row


def folded(wide, own):
    return jnp.concatenate(
        [jnp.where(own, wide[:, WIN:], wide[:, :TILE]), wide[:, TILE:WIN]], axis=1
    )


def unfolded(narrow, own):
    edge = narrow[:, :TILE]
    none = jnp.zeros_like(edge)
    return jnp.concatenate(
        [jnp.where(own, none, edge), narrow[:, TILE:], jnp.where(own, edge, none)], axis=1
    )


def payload_kernel(place_ref, *refs):
    sources, (payload_ref, *places, sems) = refs[:8], refs[8:]
    copies = [
        pltpu.make_async_copy(source, goal, sems.at[k])
        for k, (source, goal) in enumerate(zip(sources, places))
    ]
    for one in copies:
        one.start()
    for one in copies:
        one.wait()
    query_ref, out_ref, keyval_ref, gate_ref, up_ref, down_ref, gain_one_ref, gain_two_ref = places
    width = gain_one_ref.shape[1]
    row = lax.broadcasted_iota(jnp.int32, (8, query_ref.shape[1]), 0)
    lane = lax.broadcasted_iota(jnp.int32, (8, query_ref.shape[1]), 1) - place_ref[0] * width
    gains = jnp.zeros(row.shape, F32)
    for k, ref in ((4, gain_one_ref), (5, gain_two_ref)):
        values = ref[...].astype(F32)
        for i in range(width):
            gains = jnp.where((row == k) & (lane == i), values[:, i : i + 1], gains)
    keyval = jnp.concatenate([keyval_ref[...].astype(F32), gains[4:]], axis=0)
    payload_ref[0] = query_ref[...]
    payload_ref[1] = out_ref[...]
    payload_ref[2] = keyval.astype(BF)
    for k, ref in ((3, gate_ref), (5, up_ref), (7, down_ref)):
        payload_ref[k : k + 2] = ref[...].reshape(2, 8, -1)


def pack_kernel(r0, r1, r2, r3, goal_ref):
    groups, rows, width = r0.shape
    for k, ref in enumerate((r0, r1, r2, r3)):
        goal_ref[:, k] = ref[...]


def pack_two_kernel(r0, r1, r2, r3, attn_ref, units_ref):
    for k, ref in enumerate((r0, r1, r2, r3)):
        attn_ref[:, :, k] = ref[:3]
        units_ref[:, :, k] = ref[3:]


def nothing_kernel(*refs):
    pass


def head_rows(half, owner):
    for head in range(HEADS):
        first = head * HEAD + half * 128
        if owner == 0:
            yield pl.ds(first, 128), head, pl.ds(0, 128)
        else:
            for piece in range(SIDE):
                yield pl.ds(first + piece * 32, 32), piece, pl.ds(head * 32, 32)


def forward_kernel(
    place_ref, tokens_ref, before_ref, select_ref, a0, a1, a2, a3, b0, b1, b2, b3,
    residual_ref, normed_two_ref, normed_ref, query_ref, keyval_ref, attended_ref, probs_ref,
    weight_query_ref, weight_out_ref, weight_keyval_ref, gains_ref,
):
    count = tokens_ref.shape[0]
    halves = ((a0, a1, a2, a3), (b0, b1, b2, b3))
    for half in range(2):
        for owner in range(2):

            @pl.when((place_ref[0] + half) % 2 == owner)
            def _():
                for here, piece, there in head_rows(half, owner):
                    weight_query_ref[here, :] = halves[half][piece][0, there, :]
                    weight_out_ref[here, :] = halves[half][piece][1, there, :]

    mixed = jnp.concatenate([one[2] for half in halves for one in half], axis=0)
    sorted_rows = times_plain(select_ref[...], mixed)
    weight_keyval_ref[...] = sorted_rows[:512].astype(BF)
    gains_ref[...] = sorted_rows[512:520]
    gain_one = sorted_rows[512:513]
    gain_two = sorted_rows[513:514]
    inputs = tokens_ref[...].astype(F32)
    normed = normalise(inputs, gain_one)
    normed_ref[...] = normed
    normed_before = normalise(before_ref[...].astype(F32), gain_one)
    weight_keyval = weight_keyval_ref[...]
    keyval_ref[:WIN, :] = times_rows(normed_before, weight_keyval).astype(BF)
    keyval_ref[WIN:, :] = times_rows(normed, weight_keyval).astype(BF)
    for head in range(HEADS):
        query_ref[head] = times_rows(
            normed, weight_query_ref[pl.ds(head * HEAD, HEAD), :]
        ).astype(BF)
    own = own_mask()
    first_key = jnp.where(place_ref[0] == 0, WIN, 0)

    @pl.loop(0, count // TILE)
    def _(tile):
        start = pl.multiple_of(tile * TILE, TILE)
        queries = query_ref[:, pl.ds(start, TILE), :].reshape(HEADS * TILE, HEAD)
        scores = times_rows(queries, keyval_ref[pl.ds(start, SPAN), :HEAD]) * SCALE
        spot = start + lax.broadcasted_iota(jnp.int32, (1, SPAN), 1)
        scores = folded(jnp.where(spot >= first_key, scores, MASKED), own)
        raised = jnp.exp(scores - jnp.max(scores, axis=1, keepdims=True))
        probs = (raised / jnp.sum(raised, axis=1, keepdims=True)).astype(BF)
        probs_ref[pl.ds(pl.multiple_of(tile * HEADS * TILE, TILE), HEADS * TILE), :] = probs
        mixed = times_plain(unfolded(probs, own), keyval_ref[pl.ds(start, SPAN), HEAD:]).astype(BF)
        for head in range(HEADS):
            attended_ref[pl.ds(start, TILE), pl.ds(head * HEAD, HEAD)] = mixed[
                head * TILE : (head + 1) * TILE
            ]

    residual = inputs + times_plain(attended_ref[...], weight_out_ref[...])
    residual_ref[...] = residual
    normed_two_ref[...] = normalise(residual, gain_two)


GELU_A = math.sqrt(2.0 / math.pi)
GELU_B = 0.044715


def ffn_kernel(normed_ref, grad_ref, w0, w1, w2, w3, branch_ref, normed_grad_ref, both_grad_ref, hidden_ref):
    normed = normed_ref[...]
    grad = grad_ref[...]
    branch, normed_grad = None, None
    for k, ref in enumerate((w0, w1, w2, w3)):
        units = ref[0:4].reshape(512, -1)
        down = ref[4:6].reshape(256, -1)
        both = times_rows(normed, units)
        gate, up = both[:, :256], both[:, 256:]
        hidden_grad = times_rows(grad, down)
        square = gate * gate
        bend = jnp.tanh(GELU_A * gate * (1.0 + GELU_B * square))
        half = 0.5 * (1.0 + bend)
        active = gate * half
        slope = half + 0.5 * gate * (1.0 - bend * bend) * (GELU_A + (3.0 * GELU_A * GELU_B) * square)
        hidden = (active * up).astype(BF)
        both_grad = jnp.concatenate(
            [(hidden_grad * up * slope).astype(BF), (hidden_grad * active).astype(BF)], axis=1
        )
        hidden_ref[k] = hidden
        both_grad_ref[k] = both_grad
        branch_term = times_plain(hidden, down)
        normed_term = times_plain(both_grad, units)
        branch = branch_term if k == 0 else branch + branch_term
        normed_grad = normed_term if k == 0 else normed_grad + normed_term
    branch_ref[...] = branch.astype(branch_ref.dtype).reshape(branch_ref.shape)
    normed_grad_ref[...] = normed_grad.astype(normed_grad_ref.dtype).reshape(normed_grad_ref.shape)


def ffn_other_kernel(normed_ref, grad_ref, w0, w1, w2, w3, sums_ref, both_grad_ref, hidden_ref):
    ffn_kernel(
        normed_ref, grad_ref, w0, w1, w2, w3, sums_ref.at[0], sums_ref.at[1], both_grad_ref, hidden_ref
    )


def ffn_terms_kernel(normed_ref, grad_ref, both_ref, hidden_ref, normed_other_ref, grad_other_ref, both_other_ref, hidden_other_ref, *goals):
    for k, goal in enumerate(goals):
        terms = times_cols(both_ref[k], normed_ref[...]) + times_cols(both_other_ref[k], normed_other_ref[...])
        goal[0:4] = terms.astype(goal.dtype).reshape(4, 128, -1)
        terms = times_cols(hidden_ref[k], grad_ref[...]) + times_cols(hidden_other_ref[k], grad_other_ref[...])
        goal[4:6] = terms.astype(goal.dtype).reshape(2, 128, -1)


def middle_kernel(
    residual_ref, branch_ref, normed_grad_ref, sums_ref, cotangent_ref, gains_ref, weight_out_ref, query_ref, keyval_ref, probs_ref, natural_ref,
    output_ref, residual_grad_ref, low_ref, query_grad_ref, own_ref, sent_ref, gain_ref,
    rows_ref, window_ref,
):
    count = residual_ref.shape[0]
    residual = residual_ref[...]
    output_ref[...] = (residual + branch_ref[...] + sums_ref[0].astype(F32)).astype(BF)
    normed_grad = normed_grad_ref[...] + sums_ref[1].astype(F32)
    part, gain_grad = normalise_back(residual, gains_ref[1:2, :], normed_grad)
    gain_ref[...] = jnp.broadcast_to(gain_grad, gain_ref.shape)
    residual_grad = cotangent_ref[...].astype(F32) + part
    residual_grad_ref[...] = residual_grad
    low = residual_grad.astype(BF)
    low_ref[...] = low
    for head in range(HEADS):
        rows_ref[head] = times_rows(low, weight_out_ref[pl.ds(head * HEAD, HEAD), :]).astype(BF)
    window_ref[...] = jnp.zeros_like(window_ref)
    own = own_mask()

    @pl.loop(0, count // TILE)
    def _(tile):
        start = pl.multiple_of(tile * TILE, TILE)
        span = pl.ds(start, SPAN)
        queries = query_ref[:, pl.ds(start, TILE), :].reshape(HEADS * TILE, HEAD)
        rows = rows_ref[:, pl.ds(start, TILE), :].reshape(HEADS * TILE, HEAD)
        low_probs = probs_ref[pl.ds(pl.multiple_of(tile * HEADS * TILE, TILE), HEADS * TILE), :]
        probs = low_probs.astype(F32)
        prob_grad = folded(times_rows(rows, keyval_ref[span, HEAD:]), own)
        centre = jnp.sum(probs * prob_grad, axis=1, keepdims=True) / jnp.sum(
            probs, axis=1, keepdims=True
        )
        score_grad = unfolded((probs * (prob_grad - centre)).astype(BF), own)
        mixed = (times_plain(score_grad, keyval_ref[span, :HEAD]) * SCALE).astype(BF)
        for head in range(HEADS):
            query_grad_ref[pl.ds(start, TILE), pl.ds(head * HEAD, HEAD)] = mixed[
                head * TILE : (head + 1) * TILE
            ]
        window_ref[span, :HEAD] += times_cols(score_grad, queries) * SCALE
        window_ref[span, HEAD:] += times_cols(unfolded(low_probs, own), rows)

    own_ref[...] = window_ref[WIN:, :]
    natural = natural_ref[...]
    sent_ref[:, :HEAD] = times_plain(window_ref[:WIN, :HEAD].astype(BF), natural).astype(BF)
    sent_ref[:, HEAD:] = times_plain(window_ref[:WIN, HEAD:].astype(BF), natural).astype(BF)


def weights_kernel(
    normed_ref, low_ref, attended_ref, query_grad_ref, weight_query_ref, normed_grad_ref, query_ref, out_ref
):
    query_grad = query_grad_ref[...]
    normed_grad_ref[...] = times_plain(query_grad, weight_query_ref[...])
    query_ref[...] = times_cols(query_grad, normed_ref[...]).astype(BF)
    out_ref[...] = times_cols(attended_ref[...], low_ref[...]).astype(BF)


def last_kernel(
    tokens_ref, normed_ref, own_ref, came_ref, natural_ref, select_ref, weight_keyval_ref, gains_ref,
    partial_ref, residual_grad_ref, gain_two_ref, query_ref, out_ref, place_ref,
    input_grad_ref, mine_ref, *other_refs,
):
    natural = natural_ref[...]
    keyval = jnp.concatenate(
        [
            own_ref[:, :HEAD] + times_rows(came_ref[:, :HEAD], natural),
            own_ref[:, HEAD:] + times_rows(came_ref[:, HEAD:], natural),
        ],
        axis=1,
    ).astype(BF)
    grad = partial_ref[...] + times_plain(keyval, weight_keyval_ref[...])
    part, gain_grad = normalise_back(tokens_ref[...].astype(F32), gains_ref[0:1, :], grad)
    input_grad_ref[...] = residual_grad_ref[...] + part
    row = lax.broadcasted_iota(jnp.int32, (16, gain_grad.shape[1]), 0)
    gain_rows = jnp.where(
        row == 0, gain_grad, jnp.where(row == 1, gain_two_ref[0:1, :], 0.0)
    ).astype(BF)
    rows = jnp.concatenate([times_cols(keyval, normed_ref[...]).astype(BF), gain_rows], axis=0)
    mixed = times_cols(select_ref[...], rows).astype(BF)
    for half in range(2):

        def goal(group, piece):
            if half == 0:
                return mine_ref.at[piece, group]
            return other_refs[2 * group + piece // 2].at[piece % 2]

        for piece in range(SIDE):
            goal(2, piece)[...] = mixed[(half * SIDE + piece) * 128 : (half * SIDE + piece + 1) * 128]
        for owner in range(2):

            @pl.when((place_ref[0] + half) % 2 == owner)
            def _():
                for here, piece, there in head_rows(half, owner):
                    goal(0, piece)[there, :] = query_ref[here, :]
                    goal(1, piece)[there, :] = out_ref[here, :]


def meet_kernel(mine_ref, *refs):
    for last, goal in enumerate(refs[6:]):
        for k in range(3):
            came = refs[2 * k + last // 2][last % 2]
            goal[k] = (mine_ref[last, k].astype(F32) + came.astype(F32)).astype(goal.dtype)


def meet(mine, came, after=()):
    _, groups, rows, width = mine.shape
    return run(
        meet_kernel,
        [shape((groups, rows, width), F32 if k == 0 else BF) for k in range(SIDE)],
        mine,
        *came,
        after=after,
    )


def summed(refs):
    total = refs[0][...]
    for one in refs[1:]:
        total = total + one[...].astype(F32)
    return total


def middle_sum_kernel(*refs):
    total = summed(refs[:SIDE])
    groups, rows, width = total.shape
    blocks = total.reshape(groups, SIDE, SIDE, 8, width)
    for k, goal in enumerate(refs[SIDE:]):
        goal[...] = blocks[:, :, k].reshape(groups, 4 * 8, width).astype(goal.dtype)


def middle_sum(held, came, after=()):
    groups, rows, width = held.shape
    return run(
        middle_sum_kernel,
        [shape((groups, rows // SIDE, width), F32 if k == 0 else BF) for k in range(SIDE)],
        held, *came,
        after=after,
        grid=(groups // 3,),
        in_specs=[pl.BlockSpec((3, rows, width), lambda i: (i, 0, 0))] * SIDE,
        out_specs=[pl.BlockSpec((3, rows // SIDE, width), lambda i: (i, 0, 0))] * SIDE,
    )


def first_sum_kernel(*refs):
    for first, groups, parts in ((0, 3, refs[:SIDE]), (3, 6, refs[SIDE : 2 * SIDE])):
        total = summed(parts)
        for k, goal in enumerate(refs[2 * SIDE :]):
            goal[first : first + groups] = total[:, 8 * k : 8 * k + 8].astype(goal.dtype)


def end_kernel(place_ref, r0, r1, r2, r3, query_ref, keyval_ref, out_ref, gate_ref, up_ref, down_ref, one_ref, two_ref):
    total = summed((r0, r1, r2, r3))
    query_ref[...] = total[0]
    out_ref[...] = total[1]
    keyval_ref[...] = total[2, :4]
    for k, goal in ((3, gate_ref), (5, up_ref), (7, down_ref)):
        goal[...] = total[k : k + 2].reshape(goal.shape)
    width = one_ref.shape[0]
    full = total.shape[-1]
    rows = pltpu.roll(total[2], lax.rem(full - place_ref[0] * width, full), 1)
    one_ref[...] = rows[4, :width]
    two_ref[...] = rows[5, :width]


def local(tokens, gain_attn, gain_ffn, w_query, w_keyval, w_out, w_gate, w_up, w_down, cotangent):
    row_count, model_width = tokens.shape
    place = lax.axis_index(AXES)

    before = shifted(tokens, 1)
    cotangent_other = to_sibling(cotangent)
    spot = place.reshape(1)
    scalar = pl.BlockSpec(memory_space=pltpu.SMEM)
    shards = (w_query, w_out, w_keyval, w_gate, w_up, w_down, gain_attn[None], gain_ffn[None])
    payload, = run(
        payload_kernel,
        [shape((9, 8, model_width), BF)],
        spot, *shards,
        in_specs=[scalar] + [OUTSIDE] * 8,
        limit=60,
        scratch_shapes=[pltpu.VMEM(one.shape, BF) for one in shards] + [pltpu.SemaphoreType.DMA((8,))],
    )
    select, natural = run(
        select_kernel,
        [shape((528, 1024), BF), shape((HEAD, HEAD), BF)],
        spot,
        in_specs=[scalar],
    )
    payload, = run(
        pack_kernel,
        [shape((9, SIDE, 8, model_width), BF)],
        *gather_stage(payload, 0),
        after=(natural,),
    )
    attn, units = run(
        pack_two_kernel,
        [shape((3, SIDE, SIDE, 8, model_width), BF), shape((6, SIDE, SIDE, 8, model_width), BF)],
        *gather_stage(payload, 1),
        after=(before,),
    )
    attn = gather_stage(attn.reshape(3, 128, model_width), 2)
    units = gather_stage(units.reshape(6, 128, model_width), 2)
    attn += [to_sibling(one) for one in attn]

    (
        residual, normed_two, normed, queries, keyvals, attended, probs, weight_query, weight_out, weight_keyval, gains
    ) = run(
        forward_kernel,
        (
            shape((row_count, model_width), F32),
            shape((row_count, model_width), BF),
            shape((row_count, model_width), BF),
            shape((HEADS, row_count, HEAD), BF),
            shape((2 * row_count, 2 * HEAD), BF),
            shape((row_count, HEADS * HEAD), BF),
            shape((HEADS * row_count, WIN), BF),
            shape((HEADS * HEAD, model_width), BF),
            shape((HEADS * HEAD, model_width), BF),
            shape((2 * HEAD, model_width), BF),
            shape((8, model_width), F32),
        ),
        spot, tokens, before, select, *attn,
        in_specs=[scalar] + [WHOLE] * 11,
    )

    normed_other = to_sibling(normed_two)
    kept = [shape((SIDE, row_count, 512), BF), shape((SIDE, row_count, 256), BF)]
    branch, normed_grad, both_grad, hidden = run(
        ffn_kernel,
        [shape((row_count, model_width), F32)] * 2 + kept,
        normed_two, cotangent, *units,
        flops=10**10,
    )
    sums, both_grad_other, hidden_other = run(
        ffn_other_kernel,
        [shape((2, row_count, model_width), BF)] + kept,
        normed_other, cotangent_other, *units,
        after=(normed_grad,),
    )
    sums = to_sibling(sums)
    ffn_pieces = run(
        ffn_terms_kernel,
        [shape((6, 128, model_width), F32 if k == 0 else BF) for k in range(SIDE)],
        normed_two, cotangent, both_grad, hidden, normed_other, cotangent_other, both_grad_other, hidden_other,
    )
    ffn_back = scatter_stage(ffn_pieces, 2)

    output, residual_grad, low, query_grad, keyval_own, keyval_sent, gain_two_grad = run(
        middle_kernel,
        (
            shape((row_count, model_width), BF),
            shape((row_count, model_width), F32),
            shape((row_count, model_width), BF),
            shape((row_count, HEADS * HEAD), BF),
            shape((row_count, 2 * HEAD), F32),
            shape((row_count, 2 * HEAD), BF),
            shape((8, model_width), F32),
        ),
        residual, branch, normed_grad, sums, cotangent, gains, weight_out, queries, keyvals, probs, natural,
        after=(ffn_pieces[1],),
        scratch_shapes=[pltpu.VMEM((HEADS, row_count, HEAD), BF), pltpu.VMEM((2 * row_count, 2 * HEAD), F32)],
    )
    came = shifted(keyval_sent, -1)
    partial, query_term, out_term = run(
        weights_kernel,
        (
            shape((row_count, model_width), F32),
            shape((HEADS * HEAD, model_width), BF),
            shape((HEADS * HEAD, model_width), BF),
        ),
        normed, low, attended, query_grad, weight_query,
    )
    input_grad, mine, *others = run(
        last_kernel,
        (
            shape((row_count, model_width), F32),
            shape((SIDE, 3, 128, model_width), BF),
        )
        + (shape((2, 128, model_width), BF),) * 6,
        tokens, normed, keyval_own, came, natural, select, weight_keyval, gains,
        partial, residual_grad, gain_two_grad, query_term, out_term, spot,
        in_specs=[WHOLE] * 13 + [scalar],
    )
    came = [to_sibling(one) for one in others]
    ffn_pieces = middle_sum(ffn_pieces[0], ffn_back, after=(mine,))
    ffn_back = scatter_stage(ffn_pieces, 1)
    attn_pieces = meet(mine, came, after=(ffn_pieces[1],))
    attn_back = scatter_stage(attn_pieces, 2)
    attn_pieces = middle_sum(attn_pieces[0], attn_back)
    attn_back = scatter_stage(attn_pieces, 1)
    pieces = run(
        first_sum_kernel,
        [shape((9, 8, model_width), F32 if k == 0 else BF) for k in range(SIDE)],
        attn_pieces[0], *attn_back, ffn_pieces[0], *ffn_back,
    )
    query, keyval, out, gate, up, down, gain_one, gain_two = run(
        end_kernel,
        [shape(one.shape, F32) for one in (w_query, w_keyval, w_out, w_gate, w_up, w_down, gain_attn, gain_ffn)],
        spot, pieces[0], *scatter_stage(pieces, 0),
        in_specs=[scalar] + [WHOLE] * SIDE,
    )
    return output, input_grad, query, keyval, out, gate, up, down, gain_one, gain_two


def solution(mesh):
    rows, flat = P(AXES, None), P(AXES)
    return jax.shard_map(
        local,
        mesh=mesh,
        in_specs=(rows, flat, flat, rows, rows, rows, rows, rows, rows, rows),
        out_specs=(rows, rows, rows, rows, rows, rows, rows, rows, flat, flat),
        check_vma=False,
    )
```

```python
import math

import jax
import jax.numpy as jnp
from jax import lax
from jax.experimental import pallas as pl
from jax.experimental.pallas import tpu as pltpu
from jax.sharding import PartitionSpec as P

HEADS = 4
HEAD = 256
WIN = 512
SIDE = 4

EPSILON = 1e-06
MASKED = -1e30
AXES = ("ctx", "hd")
BF = jnp.bfloat16
F32 = jnp.float32

SCALE = 1.0 / math.sqrt(HEAD)
TILE = 128
SPAN = WIN + TILE
MEGA = 1 << 20

GATHER = ((2, 2), (1, 0), (0, 1))
SCATTER = ((1, 0), (2, 2), (0, 1))


def chip_pairs(axis_of_core, steps):
    pairs = []
    for chip in range(SIDE**3):
        spot = [chip // SIDE**2, chip // SIDE % SIDE, chip % SIDE]
        for core in range(2):
            goal = list(spot)
            axis = axis_of_core[core]
            goal[axis] = (goal[axis] + steps) % SIDE
            target = (goal[0] * SIDE + goal[1]) * SIDE + goal[2]
            pairs.append((chip * 2 + core, target * 2 + core))
    return pairs


def to_sibling(value):
    return lax.ppermute(value, "hd", [(0, 1), (1, 0)])


def gather_stage(value, stage):
    return [value] + [
        lax.ppermute(value, AXES, chip_pairs(GATHER[stage], -steps)) for steps in range(1, SIDE)
    ]


def scatter_stage(pieces, stage):
    return [
        lax.ppermute(pieces[steps], AXES, chip_pairs(SCATTER[stage], steps))
        for steps in range(1, SIDE)
    ]


def sent(value, stage, steps):
    return lax.ppermute(value, AXES, chip_pairs(SCATTER[stage], steps))


def shifted(value, steps):
    count = lax.axis_size(AXES)
    initial, last = (max(0, -steps), min(count, count - steps))
    return lax.ppermute(value, AXES, [(source, source + steps) for source in range(initial, last)])


def times_rows(left, right):
    return lax.dot_general(left, right, (((1,), (1,)), ((), ())), preferred_element_type=F32)


def times_cols(left, right):
    return lax.dot_general(left, right, (((0,), (0,)), ((), ())), preferred_element_type=F32)


def times_plain(left, right):
    return jnp.dot(left, right, preferred_element_type=F32)


def shape(dims, kind):
    return jax.ShapeDtypeStruct(dims, kind)


WHOLE = pl.BlockSpec(memory_space=pltpu.VMEM)
ANYWHERE = pl.BlockSpec(memory_space=pl.ANY)
OUTSIDE = pl.BlockSpec(memory_space=pltpu.HBM)


def run(kernel, outs, *operands, after=(), limit=16, flops=1, in_specs=None, **more):
    count = len(operands)

    def body(*refs):
        kernel(*refs[:count], *refs[count + len(after) :])

    return pl.pallas_call(
        body,
        out_shape=outs,
        in_specs=list(in_specs or [WHOLE] * count) + [ANYWHERE] * len(after),
        cost_estimate=pl.CostEstimate(flops=flops, bytes_accessed=1, transcendentals=0),
        compiler_params=pltpu.CompilerParams(vmem_limit_bytes=limit * MEGA),
        **more,
    )(*operands, *after)


def select_kernel(place_ref, select_ref, natural_ref):
    place = place_ref[0]
    core = place % 2
    chip = place // 2
    spot = [chip // SIDE**2, chip // SIDE % SIDE, chip % SIDE]

    def device_of(half, piece, first, second):
        owner = half * (1 - core) + (1 - half) * core
        x = (spot[0] + jnp.where(owner == 0, piece, first)) % SIDE
        y = (spot[1] + jnp.where(owner == 0, first, piece)) % SIDE
        z = (spot[2] + second) % SIDE
        return ((x * SIDE + y) * SIDE + z) * 2 + owner

    row = lax.broadcasted_iota(jnp.int32, (528, 1), 0)
    feature = row % HEAD
    high, low = feature // 32 % 4, feature // 8 % 4
    device = device_of(feature // 128, high, high, low)
    goal = jnp.where(row < 512, row // HEAD * HEAD + device % 32 * 8 + feature % 8, -2)
    column = lax.broadcasted_iota(jnp.int32, (1, 1024), 1)
    device = device_of(column // 512, column // 128 % 4, column // 32 % 4, column // 8 % 4)
    part = column % 8
    have = jnp.where(part < 4, device * 4 + part, -1)
    gain = jnp.where(row >= 512, row - 508, -1)
    select_ref[...] = jnp.where(
        (goal == have) | ((gain == part) & (part < 6)), 1.0, 0.0
    ).astype(BF)
    natural_ref[...] = jnp.where(
        goal[:HEAD] == lax.broadcasted_iota(jnp.int32, (1, HEAD), 1), 1.0, 0.0
    ).astype(BF)


def normalise(values, gain):
    inverse = lax.rsqrt(jnp.mean(values * values, axis=-1, keepdims=True) + EPSILON)
    return (values * inverse * gain).astype(BF)


def normalise_back(values, gain, grad):
    inverse = lax.rsqrt(jnp.mean(values * values, axis=-1, keepdims=True) + EPSILON)
    unit = values * inverse
    gain_grad = jnp.sum(grad * unit, axis=0, keepdims=True)
    scaled = grad * gain
    return inverse * (scaled - unit * jnp.mean(scaled * unit, axis=-1, keepdims=True)), gain_grad


def own_mask():
    row = lax.broadcasted_iota(jnp.int32, (HEADS * TILE, TILE), 0) % TILE
    column = lax.broadcasted_iota(jnp.int32, (HEADS * TILE, TILE), 1)
    return column <= row


def folded(wide, own):
    return jnp.concatenate(
        [jnp.where(own, wide[:, WIN:], wide[:, :TILE]), wide[:, TILE:WIN]], axis=1
    )


def unfolded(narrow, own):
    edge = narrow[:, :TILE]
    none = jnp.zeros_like(edge)
    return jnp.concatenate(
        [jnp.where(own, none, edge), narrow[:, TILE:], jnp.where(own, edge, none)], axis=1
    )


def payload_kernel(place_ref, *refs):
    sources, (payload_ref, *places, sems) = refs[:8], refs[8:]
    copies = [
        pltpu.make_async_copy(source, goal, sems.at[k])
        for k, (source, goal) in enumerate(zip(sources, places))
    ]
    for one in copies:
        one.start()
    for one in copies:
        one.wait()
    query_ref, out_ref, keyval_ref, gate_ref, up_ref, down_ref, gain_one_ref, gain_two_ref = places
    width = gain_one_ref.shape[1]
    row = lax.broadcasted_iota(jnp.int32, (8, query_ref.shape[1]), 0)
    lane = lax.broadcasted_iota(jnp.int32, (8, query_ref.shape[1]), 1) - place_ref[0] * width
    gains = jnp.zeros(row.shape, F32)
    for k, ref in ((4, gain_one_ref), (5, gain_two_ref)):
        values = ref[...].astype(F32)
        for i in range(width):
            gains = jnp.where((row == k) & (lane == i), values[:, i : i + 1], gains)
    keyval = jnp.concatenate([keyval_ref[...].astype(F32), gains[4:]], axis=0)
    payload_ref[0] = query_ref[...]
    payload_ref[1] = out_ref[...]
    payload_ref[2] = keyval.astype(BF)
    for k, ref in ((3, gate_ref), (5, up_ref), (7, down_ref)):
        payload_ref[k : k + 2] = ref[...].reshape(2, 8, -1)


def pack_kernel(r0, r1, r2, r3, goal_ref):
    groups, rows, width = r0.shape
    for k, ref in enumerate((r0, r1, r2, r3)):
        goal_ref[:, k] = ref[...]


def pack_two_kernel(r0, r1, r2, r3, attn_ref, units_ref):
    for k, ref in enumerate((r0, r1, r2, r3)):
        attn_ref[:, k] = ref[:3]
        units_ref[:, k] = ref[3:]


def before_slots(narrow, own, start):
    edge = jnp.where(own, jnp.zeros_like(narrow[:, :TILE]), narrow[:, :TILE])
    return jnp.concatenate([edge, narrow[:, TILE : WIN - start]], axis=1) if start < WIN - TILE else edge


def own_slots(narrow, own, start):
    edge = jnp.where(own, narrow[:, :TILE], jnp.zeros_like(narrow[:, :TILE]))
    return jnp.concatenate([narrow[:, WIN - start :], edge], axis=1) if start > 0 else edge


def head_rows(half, owner):
    for head in range(HEADS):
        first = head * HEAD + half * 128
        if owner == 0:
            yield first, 128, head, pl.ds(0, 128)
        else:
            for piece in range(SIDE):
                yield first + piece * 32, 32, piece, pl.ds(head * 32, 32)


def forward_kernel(
    place_ref, tokens_ref, before_ref, select_ref, a0, a1, a2, a3, b0, b1, b2, b3,
    residual_ref, normed_two_ref, normed_ref, query_ref, keyval_ref, attended_ref, probs_ref,
    weight_query_ref, weight_out_ref, weight_keyval_ref, gains_ref,
):
    count = tokens_ref.shape[0]
    halves = ((a0, a1, a2, a3), (b0, b1, b2, b3))
    for half in range(2):
        for owner in range(2):

            @pl.when((place_ref[0] + half) % 2 == owner)
            def _():
                for first, rows, piece, there in head_rows(half, owner):
                    here = pl.ds(first, rows)
                    weight_query_ref[here, :] = halves[half][piece][0, there, :]
                    weight_out_ref[here, :] = halves[half][piece][1, there, :]

    mixed = jnp.concatenate([one[2] for half in halves for one in half], axis=0)
    sorted_rows = times_plain(select_ref[...], mixed)
    weight_keyval_ref[...] = sorted_rows[:512].astype(BF)
    gains_ref[...] = sorted_rows[512:520]
    gain_one = sorted_rows[512:513]
    gain_two = sorted_rows[513:514]
    inputs = tokens_ref[...].astype(F32)
    normed = normalise(inputs, gain_one)
    normed_ref[...] = normed
    normed_before = normalise(before_ref[...].astype(F32), gain_one)
    weight_keyval = weight_keyval_ref[...]
    keyval_ref[:WIN, :] = times_rows(normed_before, weight_keyval).astype(BF)
    keyval_ref[WIN:, :] = times_rows(normed, weight_keyval).astype(BF)
    for head in range(HEADS):
        query_ref[head] = times_rows(
            normed, weight_query_ref[pl.ds(head * HEAD, HEAD), :]
        ).astype(BF)
    own = own_mask()
    first_key = jnp.where(place_ref[0] == 0, WIN, 0)

    @pl.loop(0, count // TILE)
    def _(tile):
        start = pl.multiple_of(tile * TILE, TILE)
        queries = query_ref[:, pl.ds(start, TILE), :].reshape(HEADS * TILE, HEAD)
        scores = times_rows(queries, keyval_ref[pl.ds(start, SPAN), :HEAD]) * SCALE
        spot = start + lax.broadcasted_iota(jnp.int32, (1, SPAN), 1)
        scores = folded(jnp.where(spot >= first_key, scores, MASKED), own)
        raised = jnp.exp(scores - jnp.max(scores, axis=1, keepdims=True))
        probs = (raised / jnp.sum(raised, axis=1, keepdims=True)).astype(BF)
        probs_ref[pl.ds(pl.multiple_of(tile * HEADS * TILE, TILE), HEADS * TILE), :] = probs
        mixed = times_plain(unfolded(probs, own), keyval_ref[pl.ds(start, SPAN), HEAD:]).astype(BF)
        for head in range(HEADS):
            attended_ref[pl.ds(start, TILE), pl.ds(head * HEAD, HEAD)] = mixed[
                head * TILE : (head + 1) * TILE
            ]

    residual = inputs + times_plain(attended_ref[...], weight_out_ref[...])
    residual_ref[...] = residual
    normed_two_ref[...] = normalise(residual, gain_two)


GELU_A = math.sqrt(2.0 / math.pi)
GELU_B = 0.044715


def ffn_kernel(normed_ref, grad_ref, w0, w1, w2, w3, branch_ref, normed_grad_ref, both_grad_ref, hidden_ref):
    normed = normed_ref[...]
    grad = grad_ref[...]
    branch, normed_grad = None, None
    for k, ref in enumerate((w0, w1, w2, w3)):
        units = ref[0:4].reshape(512, -1)
        down = ref[4:6].reshape(256, -1)
        both = times_rows(normed, units)
        gate, up = both[:, :256], both[:, 256:]
        hidden_grad = times_rows(grad, down)
        square = gate * gate
        bend = jnp.tanh(GELU_A * gate * (1.0 + GELU_B * square))
        half = 0.5 * (1.0 + bend)
        active = gate * half
        slope = half + 0.5 * gate * (1.0 - bend * bend) * (GELU_A + (3.0 * GELU_A * GELU_B) * square)
        hidden = (active * up).astype(BF)
        both_grad = jnp.concatenate(
            [(hidden_grad * up * slope).astype(BF), (hidden_grad * active).astype(BF)], axis=1
        )
        hidden_ref[k] = hidden
        both_grad_ref[k] = both_grad
        branch_term = times_plain(hidden, down)
        normed_term = times_plain(both_grad, units)
        branch = branch_term if k == 0 else branch + branch_term
        normed_grad = normed_term if k == 0 else normed_grad + normed_term
    branch_ref[...] = branch.astype(branch_ref.dtype).reshape(branch_ref.shape)
    normed_grad_ref[...] = normed_grad.astype(normed_grad_ref.dtype).reshape(normed_grad_ref.shape)


def ffn_other_kernel(normed_ref, grad_ref, w0, w1, w2, w3, sums_ref, both_grad_ref, hidden_ref):
    ffn_kernel(
        normed_ref, grad_ref, w0, w1, w2, w3, sums_ref.at[0], sums_ref.at[1], both_grad_ref, hidden_ref
    )


def ffn_terms_kernel(
    normed_ref, grad_ref, both_ref, hidden_ref, normed_other_ref, grad_other_ref, both_other_ref, hidden_other_ref,
    held_ref, right_ref, far_right_ref, far_left_ref, left_ref,
):
    for k, goal in ((2, None), (0, held_ref), (1, right_ref), (3, left_ref)):
        both = times_cols(both_ref[k], normed_ref[...])
        both = (both + times_cols(both_other_ref[k], normed_other_ref[...])).reshape(4, 128, -1)
        down = times_cols(hidden_ref[k], grad_ref[...])
        down = (down + times_cols(hidden_other_ref[k], grad_other_ref[...])).reshape(2, 128, -1)
        if k == 2:
            far_right_ref[...] = both[:3].astype(BF)
            far_left_ref[0:1] = both[3:].astype(BF)
            far_left_ref[1:3] = down.astype(BF)
        else:
            goal[0:4] = both.astype(goal.dtype)
            goal[4:6] = down.astype(goal.dtype)


def relay_kernel(right_ref, left_ref, from_left_ref, from_right_ref, right_goal, left_goal):
    right_goal[0:3] = (right_ref[0:3].astype(F32) + from_left_ref[...].astype(F32)).astype(BF)
    right_goal[3:6] = right_ref[3:6]
    left_goal[0:3] = left_ref[0:3]
    left_goal[3:6] = (left_ref[3:6].astype(F32) + from_right_ref[...].astype(F32)).astype(BF)


def middle_kernel(
    residual_ref, branch_ref, normed_grad_ref, sums_ref, cotangent_ref, gains_ref, weight_out_ref, query_ref, keyval_ref, probs_ref,
    natural_ref, output_ref, residual_grad_ref, low_ref, rows_ref, score_grad_ref, sent_ref, gain_ref, window_ref,
):
    count = residual_ref.shape[0]
    residual = residual_ref[...]
    output_ref[...] = (residual + branch_ref[...] + sums_ref[0].astype(F32)).astype(BF)
    normed_grad = normed_grad_ref[...] + sums_ref[1].astype(F32)
    part, gain_grad = normalise_back(residual, gains_ref[1:2, :], normed_grad)
    gain_ref[...] = jnp.broadcast_to(gain_grad, gain_ref.shape)
    residual_grad = cotangent_ref[...].astype(F32) + part
    residual_grad_ref[...] = residual_grad
    low = residual_grad.astype(BF)
    low_ref[...] = low
    for head in range(HEADS):
        rows_ref[head] = times_rows(low, weight_out_ref[pl.ds(head * HEAD, HEAD), :]).astype(BF)
    own = own_mask()
    for tile in range(count // TILE):
        start = tile * TILE
        span = pl.ds(start, SPAN)
        here = pl.ds(tile * HEADS * TILE, HEADS * TILE)
        queries = query_ref[:, pl.ds(start, TILE), :].reshape(HEADS * TILE, HEAD)
        rows = rows_ref[:, pl.ds(start, TILE), :].reshape(HEADS * TILE, HEAD)
        low_probs = probs_ref[here, :]
        probs = low_probs.astype(F32)
        prob_grad = folded(times_rows(rows, keyval_ref[span, HEAD:]), own)
        centre = jnp.sum(probs * prob_grad, axis=1, keepdims=True) / jnp.sum(
            probs, axis=1, keepdims=True
        )
        score_grad = (probs * (prob_grad - centre)).astype(BF)
        score_grad_ref[here, :] = score_grad
        earlier = pl.ds(start, WIN - start)
        key_term = times_cols(before_slots(score_grad, own, start), queries)
        value_term = times_cols(before_slots(low_probs, own, start), rows)
        if tile == 0:
            window_ref[earlier, :HEAD] = key_term
            window_ref[earlier, HEAD:] = value_term
        else:
            window_ref[earlier, :HEAD] += key_term
            window_ref[earlier, HEAD:] += value_term
    natural = natural_ref[...]
    sent_ref[:, :HEAD] = times_plain((window_ref[:, :HEAD] * SCALE).astype(BF), natural).astype(BF)
    sent_ref[:, HEAD:] = times_plain(window_ref[:, HEAD:].astype(BF), natural).astype(BF)


def own_kernel(rows_ref, score_grad_ref, query_ref, keyval_ref, probs_ref, query_grad_ref, own_ref):
    count = query_grad_ref.shape[0]
    own = own_mask()
    for tile in reversed(range(count // TILE)):
        start = tile * TILE
        span = pl.ds(start, SPAN)
        here = pl.ds(tile * HEADS * TILE, HEADS * TILE)
        queries = query_ref[:, pl.ds(start, TILE), :].reshape(HEADS * TILE, HEAD)
        rows = rows_ref[:, pl.ds(start, TILE), :].reshape(HEADS * TILE, HEAD)
        score_grad = score_grad_ref[here, :]
        mixed = (times_plain(unfolded(score_grad, own), keyval_ref[span, :HEAD]) * SCALE).astype(BF)
        for head in range(HEADS):
            query_grad_ref[pl.ds(start, TILE), pl.ds(head * HEAD, HEAD)] = mixed[
                head * TILE : (head + 1) * TILE
            ]
        mine = pl.ds(0, start + TILE)
        key_term = times_cols(own_slots(score_grad, own, start), queries) * SCALE
        value_term = times_cols(own_slots(probs_ref[here, :], own, start), rows)
        if start + TILE == count:
            own_ref[mine, :HEAD] = key_term
            own_ref[mine, HEAD:] = value_term
        else:
            own_ref[mine, :HEAD] += key_term
            own_ref[mine, HEAD:] += value_term


def weights_kernel(
    place_ref, normed_ref, low_ref, attended_ref, query_grad_ref, weight_query_ref,
    normed_grad_ref, mine_ref, *other_refs,
):
    query_grad = query_grad_ref[...]
    normed_grad_ref[...] = times_plain(query_grad, weight_query_ref[...])
    for group, term in (
        (0, times_cols(query_grad, normed_ref[...]).astype(BF)),
        (1, times_cols(attended_ref[...], low_ref[...]).astype(BF)),
    ):
        for half in range(2):
            for owner in range(2):

                @pl.when((place_ref[0] + half) % 2 == owner)
                def _():
                    for first, rows, piece, there in head_rows(half, owner):
                        goal = mine_ref.at[piece, group]
                        if half == 1:
                            goal = other_refs[2 * group + piece // 2].at[piece % 2]
                        goal[there, :] = term[first : first + rows]


def last_kernel(
    tokens_ref, normed_ref, own_ref, came_ref, natural_ref, select_ref, weight_keyval_ref, gains_ref,
    partial_ref, residual_grad_ref, gain_two_ref,
    input_grad_ref, mine_ref, other_ref,
):
    natural = natural_ref[...]
    keyval = jnp.concatenate(
        [
            own_ref[:, :HEAD] + times_rows(came_ref[:, :HEAD], natural),
            own_ref[:, HEAD:] + times_rows(came_ref[:, HEAD:], natural),
        ],
        axis=1,
    ).astype(BF)
    grad = partial_ref[...] + times_plain(keyval, weight_keyval_ref[...])
    part, gain_grad = normalise_back(tokens_ref[...].astype(F32), gains_ref[0:1, :], grad)
    input_grad_ref[...] = residual_grad_ref[...] + part
    row = lax.broadcasted_iota(jnp.int32, (16, gain_grad.shape[1]), 0)
    gain_rows = jnp.where(
        row == 0, gain_grad, jnp.where(row == 1, gain_two_ref[0:1, :], 0.0)
    ).astype(BF)
    rows = jnp.concatenate([times_cols(keyval, normed_ref[...]).astype(BF), gain_rows], axis=0)
    mixed = times_cols(select_ref[...], rows).astype(BF)
    for piece in range(SIDE):
        mine_ref[piece] = mixed[piece * 128 : (piece + 1) * 128]
        other_ref[piece] = mixed[512 + piece * 128 : 512 + (piece + 1) * 128]


def meet_kernel(mine_ref, mine_keyval_ref, *refs):
    for last, goal in enumerate(refs[5:]):
        for k in range(3):
            mine = mine_ref[last, k] if k < 2 else mine_keyval_ref[last]
            came = refs[2 * k + last // 2][last % 2] if k < 2 else refs[4][last]
            goal[k] = (mine.astype(F32) + came.astype(F32)).astype(goal.dtype)


def meet(mine, mine_keyval, came, after=()):
    _, rows, width = mine_keyval.shape
    return run(
        meet_kernel,
        [shape((3, rows, width), F32 if k == 0 else BF) for k in range(SIDE)],
        mine,
        mine_keyval,
        *came,
        after=after,
    )


def summed(refs):
    total = refs[0][...]
    for one in refs[1:]:
        total = total + one[...].astype(F32)
    return total


def middle_sum_kernel(*refs):
    total = summed(refs[:-SIDE])
    groups, rows, width = total.shape
    blocks = total.reshape(groups, SIDE, SIDE, 8, width)
    for k, goal in enumerate(refs[-SIDE:]):
        goal[...] = blocks[:, :, k].reshape(groups, 4 * 8, width).astype(goal.dtype)


def middle_sum(held, came, after=()):
    groups, rows, width = held.shape
    return run(
        middle_sum_kernel,
        [shape((groups, rows // SIDE, width), F32 if k == 0 else BF) for k in range(SIDE)],
        held, *came,
        after=after,
        grid=(groups // 3,),
        in_specs=[pl.BlockSpec((3, rows, width), lambda i: (i, 0, 0))] * (1 + len(came)),
        out_specs=[pl.BlockSpec((3, rows // SIDE, width), lambda i: (i, 0, 0))] * SIDE,
    )


def first_sum_kernel(*refs):
    for first, groups, parts in ((0, 3, refs[:SIDE]), (3, 6, refs[SIDE : 2 * SIDE])):
        total = summed(parts)
        for k, goal in enumerate(refs[2 * SIDE :]):
            goal[first : first + groups] = total[:, 8 * k : 8 * k + 8].astype(goal.dtype)


def end_kernel(place_ref, r0, r1, r2, r3, query_ref, keyval_ref, out_ref, gate_ref, up_ref, down_ref, one_ref, two_ref):
    total = summed((r0, r1, r2, r3))
    query_ref[...] = total[0]
    out_ref[...] = total[1]
    keyval_ref[...] = total[2, :4]
    for k, goal in ((3, gate_ref), (5, up_ref), (7, down_ref)):
        goal[...] = total[k : k + 2].reshape(goal.shape)
    width = one_ref.shape[0]
    full = total.shape[-1]
    rows = pltpu.roll(total[2], lax.rem(full - place_ref[0] * width, full), 1)
    one_ref[...] = rows[4, :width]
    two_ref[...] = rows[5, :width]


def local(tokens, gain_attn, gain_ffn, w_query, w_keyval, w_out, w_gate, w_up, w_down, cotangent):
    row_count, model_width = tokens.shape
    place = lax.axis_index(AXES)

    cotangent_other = to_sibling(cotangent)
    spot = place.reshape(1)
    scalar = pl.BlockSpec(memory_space=pltpu.SMEM)
    shards = (w_query, w_out, w_keyval, w_gate, w_up, w_down, gain_attn[None], gain_ffn[None])
    payload, = run(
        payload_kernel,
        [shape((9, 8, model_width), BF)],
        spot, *shards,
        in_specs=[scalar] + [OUTSIDE] * 8,
        limit=60,
        scratch_shapes=[pltpu.VMEM(one.shape, BF) for one in shards] + [pltpu.SemaphoreType.DMA((8,))],
    )
    before = shifted(tokens, 1)
    select, natural = run(
        select_kernel,
        [shape((528, 1024), BF), shape((HEAD, HEAD), BF)],
        spot,
        in_specs=[scalar],
    )
    payload, = run(
        pack_kernel,
        [shape((9, SIDE, 8, model_width), BF)],
        *gather_stage(payload, 0),
        flops=4 * 10**9,
    )
    attn, units = run(
        pack_two_kernel,
        [shape((3, SIDE, SIDE, 8, model_width), BF), shape((6, SIDE, SIDE, 8, model_width), BF)],
        *gather_stage(payload, 1),
        after=(before, natural),
    )
    attn = gather_stage(attn.reshape(3, 128, model_width), 2)
    units = gather_stage(units.reshape(6, 128, model_width), 2)
    attn += [to_sibling(one) for one in attn]

    (
        residual, normed_two, normed, queries, keyvals, attended, probs, weight_query, weight_out, weight_keyval, gains
    ) = run(
        forward_kernel,
        (
            shape((row_count, model_width), F32),
            shape((row_count, model_width), BF),
            shape((row_count, model_width), BF),
            shape((HEADS, row_count, HEAD), BF),
            shape((2 * row_count, 2 * HEAD), BF),
            shape((row_count, HEADS * HEAD), BF),
            shape((HEADS * row_count, WIN), BF),
            shape((HEADS * HEAD, model_width), BF),
            shape((HEADS * HEAD, model_width), BF),
            shape((2 * HEAD, model_width), BF),
            shape((8, model_width), F32),
        ),
        spot, tokens, before, select, *attn,
        in_specs=[scalar] + [WHOLE] * 11,
    )

    normed_other = to_sibling(normed_two)
    kept = [shape((SIDE, row_count, 512), BF), shape((SIDE, row_count, 256), BF)]
    branch, normed_grad, both_grad, hidden = run(
        ffn_kernel,
        [shape((row_count, model_width), F32)] * 2 + kept,
        normed_two, cotangent, *units,
        flops=10**10,
    )
    sums, both_grad_other, hidden_other = run(
        ffn_other_kernel,
        [shape((2, row_count, model_width), BF)] + kept,
        normed_other, cotangent_other, *units,
        after=(normed_grad,),
    )
    sums = to_sibling(sums)
    full, part = (6, 128, model_width), (3, 128, model_width)
    held, right, far_right, far_left, left = run(
        ffn_terms_kernel,
        [shape(full, F32), shape(full, BF), shape(part, BF), shape(part, BF), shape(full, BF)],
        normed_two, cotangent, both_grad, hidden, normed_other, cotangent_other, both_grad_other, hidden_other,
    )
    from_left, from_right = sent(far_right, 2, 1), sent(far_left, 2, -1)

    output, residual_grad, low, rows, score_grad, keyval_sent, gain_two_grad = run(
        middle_kernel,
        (
            shape((row_count, model_width), BF),
            shape((row_count, model_width), F32),
            shape((row_count, model_width), BF),
            shape((HEADS, row_count, HEAD), BF),
            shape((HEADS * row_count, WIN), BF),
            shape((row_count, 2 * HEAD), BF),
            shape((8, model_width), F32),
        ),
        residual, branch, normed_grad, sums, cotangent, gains, weight_out, queries, keyvals, probs, natural,
        after=(far_left,),
        scratch_shapes=[pltpu.VMEM((row_count, 2 * HEAD), F32)],
    )
    came = shifted(keyval_sent, -1)
    query_grad, keyval_own = run(
        own_kernel,
        (shape((row_count, HEADS * HEAD), BF), shape((row_count, 2 * HEAD), F32)),
        rows, score_grad, queries, keyvals, probs,
    )
    right, left = run(
        relay_kernel, [shape(full, BF)] * 2, right, left, from_left, from_right, after=(query_grad,)
    )
    ffn_back = [sent(right, 2, 1), sent(left, 2, -1)]
    block = shape((2, 128, model_width), BF)
    partial, mine, *others = run(
        weights_kernel,
        (shape((row_count, model_width), F32), shape((SIDE, 2, 128, model_width), BF)) + (block,) * 4,
        spot, normed, low, attended, query_grad, weight_query,
        after=(right,),
        in_specs=[scalar] + [WHOLE] * 5,
    )
    input_grad, mine_keyval, other_keyval = run(
        last_kernel,
        (shape((row_count, model_width), F32),) + (shape((SIDE, 128, model_width), BF),) * 2,
        tokens, normed, keyval_own, came, natural, select, weight_keyval, gains,
        partial, residual_grad, gain_two_grad,
        flops=2 * 10**9,
    )
    others.append(other_keyval)
    came = [to_sibling(one) for one in others]
    ffn_pieces = middle_sum(held, ffn_back, after=(mine_keyval,))
    ffn_back = scatter_stage(ffn_pieces, 1)
    attn_pieces = meet(mine, mine_keyval, came, after=(ffn_pieces[1],))
    attn_back = scatter_stage(attn_pieces, 2)
    attn_pieces = middle_sum(attn_pieces[0], attn_back)
    attn_back = scatter_stage(attn_pieces, 1)
    pieces = run(
        first_sum_kernel,
        [shape((9, 8, model_width), F32 if k == 0 else BF) for k in range(SIDE)],
        attn_pieces[0], *attn_back, ffn_pieces[0], *ffn_back,
    )
    query, keyval, out, gate, up, down, gain_one, gain_two = run(
        end_kernel,
        [shape(one.shape, F32) for one in (w_query, w_keyval, w_out, w_gate, w_up, w_down, gain_attn, gain_ffn)],
        spot, pieces[0], *scatter_stage(pieces, 0),
        in_specs=[scalar] + [WHOLE] * SIDE,
    )
    return output, input_grad, query, keyval, out, gate, up, down, gain_one, gain_two


def solution(mesh):
    rows, flat = P(AXES, None), P(AXES)
    return jax.shard_map(
        local,
        mesh=mesh,
        in_specs=(rows, flat, flat, rows, rows, rows, rows, rows, rows, rows),
        out_specs=(rows, rows, rows, rows, rows, rows, rows, rows, flat, flat),
        check_vma=False,
    )
```

```python
import math

import jax
import jax.numpy as jnp
from jax import lax
from jax.experimental import pallas as pl
from jax.experimental.pallas import tpu as pltpu
from jax.sharding import PartitionSpec as P

HEADS = 4
HEAD = 256
WIN = 512
SIDE = 4

EPSILON = 1e-06
MASKED = -1e30
AXES = ("ctx", "hd")
BF = jnp.bfloat16
F32 = jnp.float32

SCALE = 1.0 / math.sqrt(HEAD)
TILE = 128
SPAN = WIN + TILE
MEGA = 1 << 20

GATHER = ((2, 2), (1, 0), (0, 1))
SCATTER = ((1, 0), (2, 2), (0, 1))
SCATTER_ATTN = ((2, 2), (1, 0), (0, 1))


def chip_pairs(axis_of_core, steps):
    pairs = []
    for chip in range(SIDE**3):
        spot = [chip // SIDE**2, chip // SIDE % SIDE, chip % SIDE]
        for core in range(2):
            goal = list(spot)
            axis = axis_of_core[core]
            goal[axis] = (goal[axis] + steps) % SIDE
            target = (goal[0] * SIDE + goal[1]) * SIDE + goal[2]
            pairs.append((chip * 2 + core, target * 2 + core))
    return pairs


def to_sibling(value):
    return lax.ppermute(value, "hd", [(0, 1), (1, 0)])


def gather_stage(value, stage):
    return [value] + [
        lax.ppermute(value, AXES, chip_pairs(GATHER[stage], -steps)) for steps in range(1, SIDE)
    ]


def scatter_stage(pieces, axis_of_core):
    return [
        lax.ppermute(pieces[steps], AXES, chip_pairs(axis_of_core, steps))
        for steps in range(1, SIDE)
    ]


def sent(value, stage, steps):
    return lax.ppermute(value, AXES, chip_pairs(SCATTER[stage], steps))


def shifted(value, steps):
    count = lax.axis_size(AXES)
    initial, last = (max(0, -steps), min(count, count - steps))
    return lax.ppermute(value, AXES, [(source, source + steps) for source in range(initial, last)])


def times_rows(left, right):
    return lax.dot_general(left, right, (((1,), (1,)), ((), ())), preferred_element_type=F32)


def times_cols(left, right):
    return lax.dot_general(left, right, (((0,), (0,)), ((), ())), preferred_element_type=F32)


def times_plain(left, right):
    return jnp.dot(left, right, preferred_element_type=F32)


def shape(dims, kind):
    return jax.ShapeDtypeStruct(dims, kind)


WHOLE = pl.BlockSpec(memory_space=pltpu.VMEM)
ANYWHERE = pl.BlockSpec(memory_space=pl.ANY)
OUTSIDE = pl.BlockSpec(memory_space=pltpu.HBM)


def run(kernel, outs, *operands, after=(), limit=16, flops=1, in_specs=None, **more):
    count = len(operands)

    def body(*refs):
        kernel(*refs[:count], *refs[count + len(after) :])

    return pl.pallas_call(
        body,
        out_shape=outs,
        in_specs=list(in_specs or [WHOLE] * count) + [ANYWHERE] * len(after),
        cost_estimate=pl.CostEstimate(flops=flops, bytes_accessed=1, transcendentals=0),
        compiler_params=pltpu.CompilerParams(vmem_limit_bytes=limit * MEGA),
        **more,
    )(*operands, *after)


def select_kernel(place_ref, select_ref, natural_ref):
    place = place_ref[0]
    core = place % 2
    chip = place // 2
    spot = [chip // SIDE**2, chip // SIDE % SIDE, chip % SIDE]

    def device_of(half, piece, first, second):
        owner = half * (1 - core) + (1 - half) * core
        x = (spot[0] + jnp.where(owner == 0, piece, first)) % SIDE
        y = (spot[1] + jnp.where(owner == 0, first, piece)) % SIDE
        z = (spot[2] + second) % SIDE
        return ((x * SIDE + y) * SIDE + z) * 2 + owner

    row = lax.broadcasted_iota(jnp.int32, (528, 1), 0)
    feature = row % HEAD
    high, low = feature // 32 % 4, feature // 8 % 4
    device = device_of(feature // 128, high, high, low)
    goal = jnp.where(row < 512, row // HEAD * HEAD + device % 32 * 8 + feature % 8, -2)
    column = lax.broadcasted_iota(jnp.int32, (1, 1024), 1)
    device = device_of(column // 512, column // 128 % 4, column // 32 % 4, column // 8 % 4)
    part = column % 8
    have = jnp.where(part < 4, device * 4 + part, -1)
    gain = jnp.where(row >= 512, row - 508, -1)
    select_ref[...] = jnp.where(
        (goal == have) | ((gain == part) & (part < 6)), 1.0, 0.0
    ).astype(BF)
    natural_ref[...] = jnp.where(
        goal[:HEAD] == lax.broadcasted_iota(jnp.int32, (1, HEAD), 1), 1.0, 0.0
    ).astype(BF)


def normalise(values, gain):
    inverse = lax.rsqrt(jnp.mean(values * values, axis=-1, keepdims=True) + EPSILON)
    return (values * inverse * gain).astype(BF)


def normalise_back(values, gain, grad):
    inverse = lax.rsqrt(jnp.mean(values * values, axis=-1, keepdims=True) + EPSILON)
    unit = values * inverse
    gain_grad = jnp.sum(grad * unit, axis=0, keepdims=True)
    scaled = grad * gain
    return inverse * (scaled - unit * jnp.mean(scaled * unit, axis=-1, keepdims=True)), gain_grad


def own_mask():
    row = lax.broadcasted_iota(jnp.int32, (HEADS * TILE, TILE), 0) % TILE
    column = lax.broadcasted_iota(jnp.int32, (HEADS * TILE, TILE), 1)
    return column <= row


def folded(wide, own):
    return jnp.concatenate(
        [jnp.where(own, wide[:, WIN:], wide[:, :TILE]), wide[:, TILE:WIN]], axis=1
    )


def unfolded(narrow, own):
    edge = narrow[:, :TILE]
    none = jnp.zeros_like(edge)
    return jnp.concatenate(
        [jnp.where(own, none, edge), narrow[:, TILE:], jnp.where(own, edge, none)], axis=1
    )


def payload_kernel(place_ref, *refs):
    sources, (payload_ref, *places, sems) = refs[:8], refs[8:]
    copies = [
        pltpu.make_async_copy(source, goal, sems.at[k])
        for k, (source, goal) in enumerate(zip(sources, places))
    ]
    for one in copies:
        one.start()
    for one in copies:
        one.wait()
    query_ref, out_ref, keyval_ref, gate_ref, up_ref, down_ref, gain_one_ref, gain_two_ref = places
    width = gain_one_ref.shape[1]
    row = lax.broadcasted_iota(jnp.int32, (8, query_ref.shape[1]), 0)
    lane = lax.broadcasted_iota(jnp.int32, (8, query_ref.shape[1]), 1) - place_ref[0] * width
    gains = jnp.zeros(row.shape, F32)
    for k, ref in ((4, gain_one_ref), (5, gain_two_ref)):
        values = ref[...].astype(F32)
        for i in range(width):
            gains = jnp.where((row == k) & (lane == i), values[:, i : i + 1], gains)
    keyval = jnp.concatenate([keyval_ref[...].astype(F32), gains[4:]], axis=0)
    payload_ref[0] = query_ref[...]
    payload_ref[1] = out_ref[...]
    payload_ref[2] = keyval.astype(BF)
    for k, ref in ((3, gate_ref), (5, up_ref), (7, down_ref)):
        payload_ref[k : k + 2] = ref[...].reshape(2, 8, -1)


def pack_kernel(r0, r1, r2, r3, goal_ref):
    groups, rows, width = r0.shape
    for k, ref in enumerate((r0, r1, r2, r3)):
        goal_ref[:, k] = ref[...]


def pack_two_kernel(r0, r1, r2, r3, attn_ref, units_ref):
    for k, ref in enumerate((r0, r1, r2, r3)):
        attn_ref[:, k] = ref[:3]
        units_ref[:, k] = ref[3:]


def before_slots(narrow, own, start):
    edge = jnp.where(own, jnp.zeros_like(narrow[:, :TILE]), narrow[:, :TILE])
    return jnp.concatenate([edge, narrow[:, TILE : WIN - start]], axis=1) if start < WIN - TILE else edge


def own_slots(narrow, own, start):
    edge = jnp.where(own, narrow[:, :TILE], jnp.zeros_like(narrow[:, :TILE]))
    return jnp.concatenate([narrow[:, WIN - start :], edge], axis=1) if start > 0 else edge


def head_rows(half, owner):
    for head in range(HEADS):
        first = head * HEAD + half * 128
        if owner == 0:
            yield first, 128, head, pl.ds(0, 128)
        else:
            for piece in range(SIDE):
                yield first + piece * 32, 32, piece, pl.ds(head * 32, 32)


def forward_kernel(
    place_ref, tokens_ref, before_ref, select_ref, a0, a1, a2, a3, b0, b1, b2, b3,
    residual_ref, normed_two_ref, normed_ref, query_ref, keyval_ref, attended_ref, probs_ref,
    weight_query_ref, weight_out_ref, weight_keyval_ref, gains_ref,
):
    count = tokens_ref.shape[0]
    halves = ((a0, a1, a2, a3), (b0, b1, b2, b3))
    for half in range(2):
        for owner in range(2):

            @pl.when((place_ref[0] + half) % 2 == owner)
            def _():
                for first, rows, piece, there in head_rows(half, owner):
                    here = pl.ds(first, rows)
                    weight_query_ref[here, :] = halves[half][piece][0, there, :]
                    weight_out_ref[here, :] = halves[half][piece][1, there, :]

    mixed = jnp.concatenate([one[2] for half in halves for one in half], axis=0)
    sorted_rows = times_plain(select_ref[...], mixed)
    weight_keyval_ref[...] = sorted_rows[:512].astype(BF)
    gains_ref[...] = sorted_rows[512:520]
    gain_one = sorted_rows[512:513]
    gain_two = sorted_rows[513:514]
    inputs = tokens_ref[...].astype(F32)
    normed = normalise(inputs, gain_one)
    normed_ref[...] = normed
    normed_before = normalise(before_ref[...].astype(F32), gain_one)
    weight_keyval = weight_keyval_ref[...]
    keyval_ref[:WIN, :] = times_rows(normed_before, weight_keyval).astype(BF)
    keyval_ref[WIN:, :] = times_rows(normed, weight_keyval).astype(BF)
    for head in range(HEADS):
        query_ref[head] = times_rows(
            normed, weight_query_ref[pl.ds(head * HEAD, HEAD), :]
        ).astype(BF)
    own = own_mask()
    first_key = jnp.where(place_ref[0] == 0, WIN, 0)

    @pl.loop(0, count // TILE)
    def _(tile):
        start = pl.multiple_of(tile * TILE, TILE)
        queries = query_ref[:, pl.ds(start, TILE), :].reshape(HEADS * TILE, HEAD)
        scores = times_rows(queries, keyval_ref[pl.ds(start, SPAN), :HEAD]) * SCALE
        spot = start + lax.broadcasted_iota(jnp.int32, (1, SPAN), 1)
        scores = folded(jnp.where(spot >= first_key, scores, MASKED), own)
        raised = jnp.exp(scores - jnp.max(scores, axis=1, keepdims=True))
        probs = (raised / jnp.sum(raised, axis=1, keepdims=True)).astype(BF)
        probs_ref[pl.ds(pl.multiple_of(tile * HEADS * TILE, TILE), HEADS * TILE), :] = probs
        mixed = times_plain(unfolded(probs, own), keyval_ref[pl.ds(start, SPAN), HEAD:]).astype(BF)
        for head in range(HEADS):
            attended_ref[pl.ds(start, TILE), pl.ds(head * HEAD, HEAD)] = mixed[
                head * TILE : (head + 1) * TILE
            ]

    residual = inputs + times_plain(attended_ref[...], weight_out_ref[...])
    residual_ref[...] = residual
    normed_two_ref[...] = normalise(residual, gain_two)


GELU_A = math.sqrt(2.0 / math.pi)
GELU_B = 0.044715


def ffn_products(normed, grad, ref):
    return times_rows(normed, ref[0:4].reshape(512, -1)), times_rows(grad, ref[4:6].reshape(256, -1))


def ffn_units(both, hidden_grad):
    gate, up = both[:, :256], both[:, 256:]
    square = gate * gate
    bend = jnp.tanh(GELU_A * gate * (1.0 + GELU_B * square))
    half = 0.5 * (1.0 + bend)
    active = gate * half
    slope = half + 0.5 * gate * (1.0 - bend * bend) * (GELU_A + (3.0 * GELU_A * GELU_B) * square)
    both_grad = jnp.concatenate(
        [(hidden_grad * up * slope).astype(BF), (hidden_grad * active).astype(BF)], axis=1
    )
    return (active * up).astype(BF), both_grad


def ffn_sums(normed_ref, grad_ref, weights, both_grad_ref, hidden_ref, branch=None, normed_grad=None):
    normed = normed_ref[...]
    grad = grad_ref[...]
    ahead = ffn_products(normed, grad, weights[0])
    for k, ref in enumerate(weights):
        now = ahead
        if k + 1 < len(weights):
            ahead = ffn_products(normed, grad, weights[k + 1])
        hidden, both_grad = ffn_units(*now)
        hidden_ref[k] = hidden
        both_grad_ref[k] = both_grad
        branch_term = times_plain(hidden, ref[4:6].reshape(256, -1))
        normed_term = times_plain(both_grad, ref[0:4].reshape(512, -1))
        branch = branch_term if branch is None else branch + branch_term
        normed_grad = normed_term if normed_grad is None else normed_grad + normed_term
    return branch, normed_grad


def ffn_kernel(normed_ref, grad_ref, w0, w1, w2, branch_ref, normed_grad_ref, both_grad_ref, hidden_ref):
    branch_ref[...], normed_grad_ref[...] = ffn_sums(
        normed_ref, grad_ref, (w0, w1, w2), both_grad_ref, hidden_ref
    )


def ffn_last_kernel(
    normed_ref, grad_ref, normed_other_ref, grad_other_ref, w0, branch_in_ref, normed_grad_in_ref, branch_other_ref, normed_grad_other_ref,
    branch_ref, normed_grad_ref, both_grad_ref, hidden_ref, sums_ref, both_grad_other_ref, hidden_other_ref,
):
    branch, normed_grad = ffn_sums(
        normed_other_ref, grad_other_ref, (w0,), both_grad_other_ref, hidden_other_ref,
        branch_other_ref[...], normed_grad_other_ref[...],
    )
    sums_ref[0] = branch.astype(BF)
    sums_ref[1] = normed_grad.astype(BF)
    branch_ref[...], normed_grad_ref[...] = ffn_sums(
        normed_ref, grad_ref, (w0,), both_grad_ref, hidden_ref, branch_in_ref[...], normed_grad_in_ref[...]
    )


def ffn_terms_kernel(
    normed_ref, grad_ref, both_ref, hidden_ref, both_late_ref, hidden_late_ref,
    normed_other_ref, grad_other_ref, both_other_ref, hidden_other_ref, both_late_other_ref, hidden_late_other_ref,
    held_ref, right_ref, far_right_ref, far_left_ref, left_ref,
):
    for k, goal in ((2, None), (0, held_ref), (1, right_ref), (3, left_ref)):
        if k == 1:
            parts = (both_late_ref[0], hidden_late_ref[0], both_late_other_ref[0], hidden_late_other_ref[0])
        else:
            parts = [ref[max(0, k - 1)] for ref in (both_ref, hidden_ref, both_other_ref, hidden_other_ref)]
        both = times_cols(parts[0], normed_ref[...]) + times_cols(parts[2], normed_other_ref[...])
        down = times_cols(parts[1], grad_ref[...]) + times_cols(parts[3], grad_other_ref[...])
        both, down = both.reshape(4, 128, -1), down.reshape(2, 128, -1)
        if k == 2:
            far_right_ref[...] = both[:3].astype(BF)
            far_left_ref[0:1] = both[3:].astype(BF)
            far_left_ref[1:3] = down.astype(BF)
        else:
            goal[0:4] = both.astype(goal.dtype)
            goal[4:6] = down.astype(goal.dtype)


def relay_kernel(right_ref, left_ref, from_left_ref, from_right_ref, right_goal, left_goal):
    right_goal[0:3] = (right_ref[0:3].astype(F32) + from_left_ref[...].astype(F32)).astype(BF)
    right_goal[3:6] = right_ref[3:6]
    left_goal[0:3] = left_ref[0:3]
    left_goal[3:6] = (left_ref[3:6].astype(F32) + from_right_ref[...].astype(F32)).astype(BF)


def middle_kernel(
    residual_ref, branch_ref, normed_grad_ref, sums_ref, cotangent_ref, gains_ref, weight_out_ref, query_ref, keyval_ref, probs_ref,
    natural_ref, output_ref, residual_grad_ref, low_ref, rows_ref, score_grad_ref, sent_ref, gain_ref, window_ref,
):
    count = residual_ref.shape[0]
    residual = residual_ref[...]
    output_ref[...] = (residual + branch_ref[...] + sums_ref[0].astype(F32)).astype(BF)
    normed_grad = normed_grad_ref[...] + sums_ref[1].astype(F32)
    part, gain_grad = normalise_back(residual, gains_ref[1:2, :], normed_grad)
    gain_ref[...] = jnp.broadcast_to(gain_grad, gain_ref.shape)
    residual_grad = cotangent_ref[...].astype(F32) + part
    residual_grad_ref[...] = residual_grad
    low = residual_grad.astype(BF)
    low_ref[...] = low
    for head in range(HEADS):
        rows_ref[head] = times_rows(low, weight_out_ref[pl.ds(head * HEAD, HEAD), :]).astype(BF)
    own = own_mask()
    for tile in range(count // TILE):
        start = tile * TILE
        span = pl.ds(start, SPAN)
        here = pl.ds(tile * HEADS * TILE, HEADS * TILE)
        queries = query_ref[:, pl.ds(start, TILE), :].reshape(HEADS * TILE, HEAD)
        rows = rows_ref[:, pl.ds(start, TILE), :].reshape(HEADS * TILE, HEAD)
        low_probs = probs_ref[here, :]
        probs = low_probs.astype(F32)
        prob_grad = folded(times_rows(rows, keyval_ref[span, HEAD:]), own)
        centre = jnp.sum(probs * prob_grad, axis=1, keepdims=True) / jnp.sum(
            probs, axis=1, keepdims=True
        )
        score_grad = (probs * (prob_grad - centre)).astype(BF)
        score_grad_ref[here, :] = score_grad
        earlier = pl.ds(start, WIN - start)
        key_term = times_cols(before_slots(score_grad, own, start), queries)
        value_term = times_cols(before_slots(low_probs, own, start), rows)
        if tile == 0:
            window_ref[earlier, :HEAD] = key_term
            window_ref[earlier, HEAD:] = value_term
        else:
            window_ref[earlier, :HEAD] += key_term
            window_ref[earlier, HEAD:] += value_term
    natural = natural_ref[...]
    sent_ref[:, :HEAD] = times_plain((window_ref[:, :HEAD] * SCALE).astype(BF), natural).astype(BF)
    sent_ref[:, HEAD:] = times_plain(window_ref[:, HEAD:].astype(BF), natural).astype(BF)


def own_kernel(rows_ref, score_grad_ref, query_ref, keyval_ref, probs_ref, query_grad_ref, own_ref):
    count = query_grad_ref.shape[0]
    own = own_mask()
    for tile in reversed(range(count // TILE)):
        start = tile * TILE
        span = pl.ds(start, SPAN)
        here = pl.ds(tile * HEADS * TILE, HEADS * TILE)
        queries = query_ref[:, pl.ds(start, TILE), :].reshape(HEADS * TILE, HEAD)
        rows = rows_ref[:, pl.ds(start, TILE), :].reshape(HEADS * TILE, HEAD)
        score_grad = score_grad_ref[here, :]
        mixed = (times_plain(unfolded(score_grad, own), keyval_ref[span, :HEAD]) * SCALE).astype(BF)
        for head in range(HEADS):
            query_grad_ref[pl.ds(start, TILE), pl.ds(head * HEAD, HEAD)] = mixed[
                head * TILE : (head + 1) * TILE
            ]
        mine = pl.ds(0, start + TILE)
        key_term = times_cols(own_slots(score_grad, own, start), queries) * SCALE
        value_term = times_cols(own_slots(probs_ref[here, :], own, start), rows)
        if start + TILE == count:
            own_ref[mine, :HEAD] = key_term
            own_ref[mine, HEAD:] = value_term
        else:
            own_ref[mine, :HEAD] += key_term
            own_ref[mine, HEAD:] += value_term


def weights_kernel(
    place_ref, normed_ref, low_ref, attended_ref, query_grad_ref, weight_query_ref,
    normed_grad_ref, mine_ref, *other_refs,
):
    query_grad = query_grad_ref[...]
    normed_grad_ref[...] = times_plain(query_grad, weight_query_ref[...])
    for group, term in (
        (0, times_cols(query_grad, normed_ref[...]).astype(BF)),
        (1, times_cols(attended_ref[...], low_ref[...]).astype(BF)),
    ):
        for half in range(2):
            for owner in range(2):

                @pl.when((place_ref[0] + half) % 2 == owner)
                def _():
                    for first, rows, piece, there in head_rows(half, owner):
                        goal = mine_ref.at[piece, group]
                        if half == 1:
                            goal = other_refs[group].at[piece]
                        goal[there, :] = term[first : first + rows]


def last_kernel(
    tokens_ref, normed_ref, own_ref, came_ref, natural_ref, select_ref, weight_keyval_ref, gains_ref,
    partial_ref, residual_grad_ref, gain_two_ref,
    input_grad_ref, mine_ref, other_ref,
):
    natural = natural_ref[...]
    keyval = jnp.concatenate(
        [
            own_ref[:, :HEAD] + times_rows(came_ref[:, :HEAD], natural),
            own_ref[:, HEAD:] + times_rows(came_ref[:, HEAD:], natural),
        ],
        axis=1,
    ).astype(BF)
    grad = partial_ref[...] + times_plain(keyval, weight_keyval_ref[...])
    part, gain_grad = normalise_back(tokens_ref[...].astype(F32), gains_ref[0:1, :], grad)
    input_grad_ref[...] = residual_grad_ref[...] + part
    row = lax.broadcasted_iota(jnp.int32, (16, gain_grad.shape[1]), 0)
    gain_rows = jnp.where(
        row == 0, gain_grad, jnp.where(row == 1, gain_two_ref[0:1, :], 0.0)
    ).astype(BF)
    rows = jnp.concatenate([times_cols(keyval, normed_ref[...]).astype(BF), gain_rows], axis=0)
    mixed = times_cols(select_ref[...], rows).astype(BF)
    for piece in range(SIDE):
        mine_ref[piece] = mixed[piece * 128 : (piece + 1) * 128]
        other_ref[piece] = mixed[512 + piece * 128 : 512 + (piece + 1) * 128]


def meet_kernel(mine_ref, mine_keyval_ref, *refs):
    for last, goal in enumerate(refs[3:]):
        for k in range(3):
            mine = mine_ref[last, k] if k < 2 else mine_keyval_ref[last]
            goal[k] = (mine.astype(F32) + refs[k][last].astype(F32)).astype(goal.dtype)


def meet(mine, mine_keyval, came, after=()):
    _, rows, width = mine_keyval.shape
    return run(
        meet_kernel,
        [shape((3, rows, width), F32 if k == 0 else BF) for k in range(SIDE)],
        mine,
        mine_keyval,
        *came,
        after=after,
    )


def summed(refs):
    total = refs[0][...]
    for one in refs[1:]:
        total = total + one[...].astype(F32)
    return total


def middle_sum_kernel(*refs):
    total = summed(refs[:-SIDE])
    groups, rows, width = total.shape
    blocks = total.reshape(groups, SIDE, SIDE, 8, width)
    for k, goal in enumerate(refs[-SIDE:]):
        goal[...] = blocks[:, :, k].reshape(groups, 4 * 8, width).astype(goal.dtype)


def middle_sum(held, came, after=()):
    groups, rows, width = held.shape
    return run(
        middle_sum_kernel,
        [shape((groups, rows // SIDE, width), F32 if k == 0 else BF) for k in range(SIDE)],
        held, *came,
        after=after,
        grid=(groups // 3,),
        in_specs=[pl.BlockSpec((3, rows, width), lambda i: (i, 0, 0))] * (1 + len(came)),
        out_specs=[pl.BlockSpec((3, rows // SIDE, width), lambda i: (i, 0, 0))] * SIDE,
    )


def cut_kernel(*refs):
    total = summed(refs[:SIDE])
    rows = total.shape[1] // SIDE
    for k, goal in enumerate(refs[SIDE:]):
        goal[...] = total[:, k * rows : (k + 1) * rows].astype(goal.dtype)


def cut(pieces, came, after=()):
    groups, rows, width = pieces[0].shape
    outs = [shape((groups, rows // SIDE, width), F32 if k == 0 else BF) for k in range(SIDE)]
    return run(cut_kernel, outs, pieces[0], *came, after=after)


def end_kernel(
    place_ref, r0, r1, r2, r3, f0, f1, f2, f3, query_ref, keyval_ref, out_ref, gate_ref, up_ref, down_ref, one_ref, two_ref
):
    total = summed((r0, r1, r2, r3))
    units = summed((f0, f1, f2, f3))
    query_ref[...] = total[0]
    out_ref[...] = total[1]
    keyval_ref[...] = total[2, :4]
    for k, goal in ((0, gate_ref), (2, up_ref), (4, down_ref)):
        goal[...] = units[k : k + 2].reshape(goal.shape)
    width = one_ref.shape[0]
    full = total.shape[-1]
    rows = pltpu.roll(total[2], lax.rem(full - place_ref[0] * width, full), 1)
    one_ref[...] = rows[4, :width]
    two_ref[...] = rows[5, :width]


def local(tokens, gain_attn, gain_ffn, w_query, w_keyval, w_out, w_gate, w_up, w_down, cotangent):
    row_count, model_width = tokens.shape
    place = lax.axis_index(AXES)

    cotangent_other = to_sibling(cotangent)
    spot = place.reshape(1)
    scalar = pl.BlockSpec(memory_space=pltpu.SMEM)
    shards = (w_query, w_out, w_keyval, w_gate, w_up, w_down, gain_attn[None], gain_ffn[None])
    payload, = run(
        payload_kernel,
        [shape((9, 8, model_width), BF)],
        spot, *shards,
        in_specs=[scalar] + [OUTSIDE] * 8,
        limit=60,
        scratch_shapes=[pltpu.VMEM(one.shape, BF) for one in shards] + [pltpu.SemaphoreType.DMA((8,))],
    )
    before = shifted(tokens, 1)
    select, natural = run(
        select_kernel,
        [shape((528, 1024), BF), shape((HEAD, HEAD), BF)],
        spot,
        in_specs=[scalar],
    )
    payload, = run(
        pack_kernel,
        [shape((9, SIDE, 8, model_width), BF)],
        *gather_stage(payload, 0),
        flops=4 * 10**9,
    )
    attn, units = run(
        pack_two_kernel,
        [shape((3, SIDE, SIDE, 8, model_width), BF), shape((6, SIDE, SIDE, 8, model_width), BF)],
        *gather_stage(payload, 1),
        after=(before, natural),
    )
    attn = gather_stage(attn.reshape(3, 128, model_width), 2)
    units = gather_stage(units.reshape(6, 128, model_width), 2)
    attn += [to_sibling(one) for one in attn]

    (
        residual, normed_two, normed, queries, keyvals, attended, probs, weight_query, weight_out, weight_keyval, gains
    ) = run(
        forward_kernel,
        (
            shape((row_count, model_width), F32),
            shape((row_count, model_width), BF),
            shape((row_count, model_width), BF),
            shape((HEADS, row_count, HEAD), BF),
            shape((2 * row_count, 2 * HEAD), BF),
            shape((row_count, HEADS * HEAD), BF),
            shape((HEADS * row_count, WIN), BF),
            shape((HEADS * HEAD, model_width), BF),
            shape((HEADS * HEAD, model_width), BF),
            shape((2 * HEAD, model_width), BF),
            shape((8, model_width), F32),
        ),
        spot, tokens, before, select, *attn,
        in_specs=[scalar] + [WHOLE] * 11,
    )

    normed_other = to_sibling(normed_two)
    def kept(count):
        return [shape((count, row_count, 512), BF), shape((count, row_count, 256), BF)]

    branch, normed_grad, both_grad, hidden = run(
        ffn_kernel,
        [shape((row_count, model_width), F32)] * 2 + kept(3),
        normed_two, cotangent, units[0], units[2], units[3],
        flops=10**10,
    )
    branch_other, normed_grad_other, both_grad_other, hidden_other = run(
        ffn_kernel,
        [shape((row_count, model_width), F32)] * 2 + kept(3),
        normed_other, cotangent_other, units[0], units[2], units[3],
        after=(normed_grad,),
    )
    branch, normed_grad, both_late, hidden_late, sums, both_late_other, hidden_late_other = run(
        ffn_last_kernel,
        [shape((row_count, model_width), F32)] * 2 + kept(1) + [shape((2, row_count, model_width), BF)] + kept(1),
        normed_two, cotangent, normed_other, cotangent_other, units[1], branch, normed_grad, branch_other, normed_grad_other,
    )
    sums = to_sibling(sums)
    full, part = (6, 128, model_width), (3, 128, model_width)
    held, right, far_right, far_left, left = run(
        ffn_terms_kernel,
        [shape(full, F32), shape(full, BF), shape(part, BF), shape(part, BF), shape(full, BF)],
        normed_two, cotangent, both_grad, hidden, both_late, hidden_late,
        normed_other, cotangent_other, both_grad_other, hidden_other, both_late_other, hidden_late_other,
    )
    from_left, from_right = sent(far_right, 2, 1), sent(far_left, 2, -1)

    output, residual_grad, low, rows, score_grad, keyval_sent, gain_two_grad = run(
        middle_kernel,
        (
            shape((row_count, model_width), BF),
            shape((row_count, model_width), F32),
            shape((row_count, model_width), BF),
            shape((HEADS, row_count, HEAD), BF),
            shape((HEADS * row_count, WIN), BF),
            shape((row_count, 2 * HEAD), BF),
            shape((8, model_width), F32),
        ),
        residual, branch, normed_grad, sums, cotangent, gains, weight_out, queries, keyvals, probs, natural,
        after=(far_left,),
        scratch_shapes=[pltpu.VMEM((row_count, 2 * HEAD), F32)],
    )
    came = shifted(keyval_sent, -1)
    query_grad, keyval_own = run(
        own_kernel,
        (shape((row_count, HEADS * HEAD), BF), shape((row_count, 2 * HEAD), F32)),
        rows, score_grad, queries, keyvals, probs,
    )
    right, left = run(
        relay_kernel, [shape(full, BF)] * 2, right, left, from_left, from_right, after=(query_grad,)
    )
    ffn_back = [sent(right, 2, 1), sent(left, 2, -1)]
    partial, mine, *others = run(
        weights_kernel,
        (shape((row_count, model_width), F32), shape((SIDE, 2, 128, model_width), BF))
        + (shape((SIDE, 128, model_width), BF),) * 2,
        spot, normed, low, attended, query_grad, weight_query,
        after=(right,),
        in_specs=[scalar] + [WHOLE] * 5,
    )
    input_grad, mine_keyval, other_keyval = run(
        last_kernel,
        (shape((row_count, model_width), F32),) + (shape((SIDE, 128, model_width), BF),) * 2,
        tokens, normed, keyval_own, came, natural, select, weight_keyval, gains,
        partial, residual_grad, gain_two_grad,
        flops=2 * 10**9,
    )
    others.append(other_keyval)
    came = [to_sibling(one) for one in others]
    ffn_pieces = middle_sum(held, ffn_back, after=(mine_keyval,))
    ffn_back = scatter_stage(ffn_pieces, SCATTER[1])
    pieces = meet(mine, mine_keyval, came, after=(ffn_pieces[1],))
    pieces = cut(pieces, scatter_stage(pieces, SCATTER_ATTN[2]))
    back = scatter_stage(pieces, SCATTER_ATTN[1])
    ffn_pieces = cut(ffn_pieces, ffn_back, after=(pieces[1],))
    ffn_back = scatter_stage(ffn_pieces, SCATTER[0])
    pieces = cut(pieces, back, after=(ffn_pieces[1],))
    back = scatter_stage(pieces, SCATTER_ATTN[0])
    query, keyval, out, gate, up, down, gain_one, gain_two = run(
        end_kernel,
        [shape(one.shape, F32) for one in (w_query, w_keyval, w_out, w_gate, w_up, w_down, gain_attn, gain_ffn)],
        spot, pieces[0], *back, ffn_pieces[0], *ffn_back,
        in_specs=[scalar] + [WHOLE] * (2 * SIDE),
    )
    return output, input_grad, query, keyval, out, gate, up, down, gain_one, gain_two


def solution(mesh):
    rows, flat = P(AXES, None), P(AXES)
    return jax.shard_map(
        local,
        mesh=mesh,
        in_specs=(rows, flat, flat, rows, rows, rows, rows, rows, rows, rows),
        out_specs=(rows, rows, rows, rows, rows, rows, rows, rows, flat, flat),
        check_vma=False,
    )
```

```python
import math

import jax
import jax.numpy as jnp
from jax import lax
from jax.experimental import pallas as pl
from jax.experimental.pallas import tpu as pltpu
from jax.sharding import PartitionSpec as P

HEADS = 4
HEAD = 256
WIN = 512
SIDE = 4

EPSILON = 1e-06
MASKED = -1e30
AXES = ("ctx", "hd")
BF = jnp.bfloat16
F32 = jnp.float32

SCALE = 1.0 / math.sqrt(HEAD)
TILE = 128
SPAN = WIN + TILE
MEGA = 1 << 20

GATHER = ((2, 2), (1, 0), (0, 1))
SCATTER = ((1, 0), (2, 2), (0, 1))
SCATTER_ATTN = ((2, 2), (1, 0), (0, 1))


def chip_pairs(axis_of_core, steps):
    pairs = []
    for chip in range(SIDE**3):
        spot = [chip // SIDE**2, chip // SIDE % SIDE, chip % SIDE]
        for core in range(2):
            goal = list(spot)
            axis = axis_of_core[core]
            goal[axis] = (goal[axis] + steps) % SIDE
            target = (goal[0] * SIDE + goal[1]) * SIDE + goal[2]
            pairs.append((chip * 2 + core, target * 2 + core))
    return pairs


def to_sibling(value):
    return lax.ppermute(value, "hd", [(0, 1), (1, 0)])


def gather_stage(value, stage):
    return [value] + [
        lax.ppermute(value, AXES, chip_pairs(GATHER[stage], -steps)) for steps in range(1, SIDE)
    ]


def scatter_stage(pieces, axis_of_core):
    return [
        lax.ppermute(pieces[steps], AXES, chip_pairs(axis_of_core, steps))
        for steps in range(1, SIDE)
    ]


def sent(value, stage, steps):
    return lax.ppermute(value, AXES, chip_pairs(SCATTER[stage], steps))


def shifted(value, steps):
    count = lax.axis_size(AXES)
    initial, last = (max(0, -steps), min(count, count - steps))
    return lax.ppermute(value, AXES, [(source, source + steps) for source in range(initial, last)])


def times_rows(left, right):
    return lax.dot_general(left, right, (((1,), (1,)), ((), ())), preferred_element_type=F32)


def times_cols(left, right):
    return lax.dot_general(left, right, (((0,), (0,)), ((), ())), preferred_element_type=F32)


def times_plain(left, right):
    return jnp.dot(left, right, preferred_element_type=F32)


def shape(dims, kind):
    return jax.ShapeDtypeStruct(dims, kind)


WHOLE = pl.BlockSpec(memory_space=pltpu.VMEM)
ANYWHERE = pl.BlockSpec(memory_space=pl.ANY)
OUTSIDE = pl.BlockSpec(memory_space=pltpu.HBM)


def run(kernel, outs, *operands, after=(), limit=16, flops=1, in_specs=None, **more):
    count = len(operands)

    def body(*refs):
        kernel(*refs[:count], *refs[count + len(after) :])

    return pl.pallas_call(
        body,
        out_shape=outs,
        in_specs=list(in_specs or [WHOLE] * count) + [ANYWHERE] * len(after),
        cost_estimate=pl.CostEstimate(flops=flops, bytes_accessed=1, transcendentals=0),
        compiler_params=pltpu.CompilerParams(vmem_limit_bytes=limit * MEGA),
        **more,
    )(*operands, *after)


def select_kernel(place_ref, select_ref, natural_ref):
    place = place_ref[0]
    core = place % 2
    chip = place // 2
    spot = [chip // SIDE**2, chip // SIDE % SIDE, chip % SIDE]

    def device_of(half, piece, first, second):
        owner = half * (1 - core) + (1 - half) * core
        x = (spot[0] + jnp.where(owner == 0, piece, first)) % SIDE
        y = (spot[1] + jnp.where(owner == 0, first, piece)) % SIDE
        z = (spot[2] + second) % SIDE
        return ((x * SIDE + y) * SIDE + z) * 2 + owner

    row = lax.broadcasted_iota(jnp.int32, (528, 1), 0)
    feature = row % HEAD
    high, low = feature // 32 % 4, feature // 8 % 4
    device = device_of(feature // 128, high, high, low)
    goal = jnp.where(row < 512, row // HEAD * HEAD + device % 32 * 8 + feature % 8, -2)
    column = lax.broadcasted_iota(jnp.int32, (1, 1024), 1)
    device = device_of(column // 512, column // 128 % 4, column // 32 % 4, column // 8 % 4)
    part = column % 8
    have = jnp.where(part < 4, device * 4 + part, -1)
    gain = jnp.where(row >= 512, row - 508, -1)
    select_ref[...] = jnp.where(
        (goal == have) | ((gain == part) & (part < 6)), 1.0, 0.0
    ).astype(BF)
    natural_ref[...] = jnp.where(
        goal[:HEAD] == lax.broadcasted_iota(jnp.int32, (1, HEAD), 1), 1.0, 0.0
    ).astype(BF)


def normalise(values, gain):
    inverse = lax.rsqrt(jnp.mean(values * values, axis=-1, keepdims=True) + EPSILON)
    return (values * inverse * gain).astype(BF)


def normalise_back(values, gain, grad):
    inverse = lax.rsqrt(jnp.mean(values * values, axis=-1, keepdims=True) + EPSILON)
    unit = values * inverse
    gain_grad = jnp.sum(grad * unit, axis=0, keepdims=True)
    scaled = grad * gain
    return inverse * (scaled - unit * jnp.mean(scaled * unit, axis=-1, keepdims=True)), gain_grad


def own_mask():
    row = lax.broadcasted_iota(jnp.int32, (HEADS * TILE, TILE), 0) % TILE
    column = lax.broadcasted_iota(jnp.int32, (HEADS * TILE, TILE), 1)
    return column <= row


def folded(wide, own):
    return jnp.concatenate(
        [jnp.where(own, wide[:, WIN:], wide[:, :TILE]), wide[:, TILE:WIN]], axis=1
    )


def unfolded(narrow, own):
    edge = narrow[:, :TILE]
    none = jnp.zeros_like(edge)
    return jnp.concatenate(
        [jnp.where(own, none, edge), narrow[:, TILE:], jnp.where(own, edge, none)], axis=1
    )


def payload_kernel(place_ref, *refs):
    sources, (payload_ref, *places, sems) = refs[:8], refs[8:]
    copies = [
        pltpu.make_async_copy(source, goal, sems.at[k])
        for k, (source, goal) in enumerate(zip(sources, places))
    ]
    for one in copies:
        one.start()
    for one in copies:
        one.wait()
    query_ref, out_ref, keyval_ref, gate_ref, up_ref, down_ref, gain_one_ref, gain_two_ref = places
    width = gain_one_ref.shape[1]
    row = lax.broadcasted_iota(jnp.int32, (8, query_ref.shape[1]), 0)
    lane = lax.broadcasted_iota(jnp.int32, (8, query_ref.shape[1]), 1) - place_ref[0] * width
    gains = jnp.zeros(row.shape, F32)
    for k, ref in ((4, gain_one_ref), (5, gain_two_ref)):
        values = ref[...].astype(F32)
        for i in range(width):
            gains = jnp.where((row == k) & (lane == i), values[:, i : i + 1], gains)
    keyval = jnp.concatenate([keyval_ref[...].astype(F32), gains[4:]], axis=0)
    payload_ref[0] = query_ref[...]
    payload_ref[1] = out_ref[...]
    payload_ref[2] = keyval.astype(BF)
    for k, ref in ((3, gate_ref), (5, up_ref), (7, down_ref)):
        payload_ref[k : k + 2] = ref[...].reshape(2, 8, -1)


def pack_kernel(r0, r1, r2, r3, goal_ref):
    groups, rows, width = r0.shape
    for k, ref in enumerate((r0, r1, r2, r3)):
        goal_ref[:, k] = ref[...]


def choose_kernel(place_ref, own_ref, hop_ref, goal_ref):
    edge = place_ref[0] % (2 * SIDE) == 2 * SIDE - 1

    @pl.when(edge)
    def _():
        goal_ref[...] = hop_ref[...]

    @pl.when(jnp.logical_not(edge))
    def _():
        goal_ref[...] = own_ref[...]


def pack_two_kernel(r0, r1, r2, r3, attn_ref, units_ref):
    for k, ref in enumerate((r0, r1, r2, r3)):
        attn_ref[:, k] = ref[:3]
        units_ref[:, k] = ref[3:]


def before_slots(narrow, own, start):
    edge = jnp.where(own, jnp.zeros_like(narrow[:, :TILE]), narrow[:, :TILE])
    return jnp.concatenate([edge, narrow[:, TILE : WIN - start]], axis=1) if start < WIN - TILE else edge


def own_slots(narrow, own, start):
    edge = jnp.where(own, narrow[:, :TILE], jnp.zeros_like(narrow[:, :TILE]))
    return jnp.concatenate([narrow[:, WIN - start :], edge], axis=1) if start > 0 else edge


def head_rows(half, owner):
    for head in range(HEADS):
        first = head * HEAD + half * 128
        if owner == 0:
            yield first, 128, head, pl.ds(0, 128)
        else:
            for piece in range(SIDE):
                yield first + piece * 32, 32, piece, pl.ds(head * 32, 32)


def forward_kernel(
    place_ref, tokens_ref, before_ref, select_ref, a0, a1, a2, a3, b0, b1, b2, b3,
    residual_ref, normed_two_ref, normed_ref, query_ref, keyval_ref, attended_ref, probs_ref,
    weight_query_ref, weight_out_ref, weight_keyval_ref, gains_ref,
):
    count = tokens_ref.shape[0]
    halves = ((a0, a1, a2, a3), (b0, b1, b2, b3))
    for half in range(2):
        for owner in range(2):

            @pl.when((place_ref[0] + half) % 2 == owner)
            def _():
                for first, rows, piece, there in head_rows(half, owner):
                    here = pl.ds(first, rows)
                    weight_query_ref[here, :] = halves[half][piece][0, there, :]
                    weight_out_ref[here, :] = halves[half][piece][1, there, :]

    mixed = jnp.concatenate([one[2] for half in halves for one in half], axis=0)
    sorted_rows = times_plain(select_ref[...], mixed)
    weight_keyval_ref[...] = sorted_rows[:512].astype(BF)
    gains_ref[...] = sorted_rows[512:520]
    gain_one = sorted_rows[512:513]
    gain_two = sorted_rows[513:514]
    inputs = tokens_ref[...].astype(F32)
    normed = normalise(inputs, gain_one)
    normed_ref[...] = normed
    normed_before = normalise(before_ref[...].astype(F32), gain_one)
    weight_keyval = weight_keyval_ref[...]
    keyval_ref[:WIN, :] = times_rows(normed_before, weight_keyval).astype(BF)
    keyval_ref[WIN:, :] = times_rows(normed, weight_keyval).astype(BF)
    for head in range(HEADS):
        query_ref[head] = times_rows(
            normed, weight_query_ref[pl.ds(head * HEAD, HEAD), :]
        ).astype(BF)
    own = own_mask()
    first_key = jnp.where(place_ref[0] == 0, WIN, 0)

    @pl.loop(0, count // TILE)
    def _(tile):
        start = pl.multiple_of(tile * TILE, TILE)
        queries = query_ref[:, pl.ds(start, TILE), :].reshape(HEADS * TILE, HEAD)
        scores = times_rows(queries, keyval_ref[pl.ds(start, SPAN), :HEAD]) * SCALE
        spot = start + lax.broadcasted_iota(jnp.int32, (1, SPAN), 1)
        scores = folded(jnp.where(spot >= first_key, scores, MASKED), own)
        raised = jnp.exp(scores - jnp.max(scores, axis=1, keepdims=True))
        probs = (raised / jnp.sum(raised, axis=1, keepdims=True)).astype(BF)
        probs_ref[pl.ds(pl.multiple_of(tile * HEADS * TILE, TILE), HEADS * TILE), :] = probs
        mixed = times_plain(unfolded(probs, own), keyval_ref[pl.ds(start, SPAN), HEAD:]).astype(BF)
        for head in range(HEADS):
            attended_ref[pl.ds(start, TILE), pl.ds(head * HEAD, HEAD)] = mixed[
                head * TILE : (head + 1) * TILE
            ]

    residual = inputs + times_plain(attended_ref[...], weight_out_ref[...])
    residual_ref[...] = residual
    normed_two_ref[...] = normalise(residual, gain_two)


GELU_A = math.sqrt(2.0 / math.pi)
GELU_B = 0.044715


def ffn_products(normed, grad, ref):
    return times_rows(normed, ref[0:4].reshape(512, -1)), times_rows(grad, ref[4:6].reshape(256, -1))


def ffn_units(both, hidden_grad):
    gate, up = both[:, :256], both[:, 256:]
    square = gate * gate
    bend = jnp.tanh(GELU_A * gate * (1.0 + GELU_B * square))
    half = 0.5 * (1.0 + bend)
    active = gate * half
    slope = half + 0.5 * gate * (1.0 - bend * bend) * (GELU_A + (3.0 * GELU_A * GELU_B) * square)
    both_grad = jnp.concatenate(
        [(hidden_grad * up * slope).astype(BF), (hidden_grad * active).astype(BF)], axis=1
    )
    return (active * up).astype(BF), both_grad


def ffn_sums(normed_ref, grad_ref, weights, both_grad_ref, hidden_ref, branch=None, normed_grad=None):
    normed = normed_ref[...]
    grad = grad_ref[...]
    ahead = ffn_products(normed, grad, weights[0])
    for k, ref in enumerate(weights):
        now = ahead
        if k + 1 < len(weights):
            ahead = ffn_products(normed, grad, weights[k + 1])
        hidden, both_grad = ffn_units(*now)
        hidden_ref[k] = hidden
        both_grad_ref[k] = both_grad
        branch_term = times_plain(hidden, ref[4:6].reshape(256, -1))
        normed_term = times_plain(both_grad, ref[0:4].reshape(512, -1))
        branch = branch_term if branch is None else branch + branch_term
        normed_grad = normed_term if normed_grad is None else normed_grad + normed_term
    return branch, normed_grad


def ffn_kernel(normed_ref, grad_ref, w0, w1, w2, branch_ref, normed_grad_ref, both_grad_ref, hidden_ref):
    branch_ref[...], normed_grad_ref[...] = ffn_sums(
        normed_ref, grad_ref, (w0, w1, w2), both_grad_ref, hidden_ref
    )


def ffn_last_kernel(
    normed_ref, grad_ref, normed_other_ref, grad_other_ref, w0, branch_in_ref, normed_grad_in_ref, branch_other_ref, normed_grad_other_ref,
    branch_ref, normed_grad_ref, both_grad_ref, hidden_ref, sums_ref, both_grad_other_ref, hidden_other_ref,
):
    branch, normed_grad = ffn_sums(
        normed_other_ref, grad_other_ref, (w0,), both_grad_other_ref, hidden_other_ref,
        branch_other_ref[...], normed_grad_other_ref[...],
    )
    sums_ref[0] = branch.astype(BF)
    sums_ref[1] = normed_grad.astype(BF)
    branch_ref[...], normed_grad_ref[...] = ffn_sums(
        normed_ref, grad_ref, (w0,), both_grad_ref, hidden_ref, branch_in_ref[...], normed_grad_in_ref[...]
    )


def ffn_terms_kernel(
    normed_ref, grad_ref, both_ref, hidden_ref, both_late_ref, hidden_late_ref,
    normed_other_ref, grad_other_ref, both_other_ref, hidden_other_ref, both_late_other_ref, hidden_late_other_ref,
    held_ref, right_ref, far_right_ref, far_left_ref, left_ref,
):
    for k, goal in ((2, None), (0, held_ref), (1, right_ref), (3, left_ref)):
        if k == 1:
            parts = (both_late_ref[0], hidden_late_ref[0], both_late_other_ref[0], hidden_late_other_ref[0])
        else:
            parts = [ref[max(0, k - 1)] for ref in (both_ref, hidden_ref, both_other_ref, hidden_other_ref)]
        both = times_cols(parts[0], normed_ref[...]) + times_cols(parts[2], normed_other_ref[...])
        down = times_cols(parts[1], grad_ref[...]) + times_cols(parts[3], grad_other_ref[...])
        both, down = both.reshape(4, 128, -1), down.reshape(2, 128, -1)
        if k == 2:
            far_right_ref[...] = both[:3].astype(BF)
            far_left_ref[0:1] = both[3:].astype(BF)
            far_left_ref[1:3] = down.astype(BF)
        else:
            goal[0:4] = both.astype(goal.dtype)
            goal[4:6] = down.astype(goal.dtype)


def relay_kernel(right_ref, left_ref, from_left_ref, from_right_ref, right_goal, left_goal):
    right_goal[0:3] = (right_ref[0:3].astype(F32) + from_left_ref[...].astype(F32)).astype(BF)
    right_goal[3:6] = right_ref[3:6]
    left_goal[0:3] = left_ref[0:3]
    left_goal[3:6] = (left_ref[3:6].astype(F32) + from_right_ref[...].astype(F32)).astype(BF)


def middle_kernel(
    residual_ref, branch_ref, normed_grad_ref, sums_ref, cotangent_ref, gains_ref, weight_out_ref, query_ref, keyval_ref, probs_ref,
    natural_ref, output_ref, residual_grad_ref, low_ref, rows_ref, score_grad_ref, sent_ref, gain_ref, window_ref,
):
    count = residual_ref.shape[0]
    residual = residual_ref[...]
    output_ref[...] = (residual + branch_ref[...] + sums_ref[0].astype(F32)).astype(BF)
    normed_grad = normed_grad_ref[...] + sums_ref[1].astype(F32)
    part, gain_grad = normalise_back(residual, gains_ref[1:2, :], normed_grad)
    gain_ref[...] = jnp.broadcast_to(gain_grad, gain_ref.shape)
    residual_grad = cotangent_ref[...].astype(F32) + part
    residual_grad_ref[...] = residual_grad
    low = residual_grad.astype(BF)
    low_ref[...] = low
    for head in range(HEADS):
        rows_ref[head] = times_rows(low, weight_out_ref[pl.ds(head * HEAD, HEAD), :]).astype(BF)
    own = own_mask()
    for tile in range(count // TILE):
        start = tile * TILE
        span = pl.ds(start, SPAN)
        here = pl.ds(tile * HEADS * TILE, HEADS * TILE)
        queries = query_ref[:, pl.ds(start, TILE), :].reshape(HEADS * TILE, HEAD)
        rows = rows_ref[:, pl.ds(start, TILE), :].reshape(HEADS * TILE, HEAD)
        low_probs = probs_ref[here, :]
        probs = low_probs.astype(F32)
        prob_grad = folded(times_rows(rows, keyval_ref[span, HEAD:]), own)
        centre = jnp.sum(probs * prob_grad, axis=1, keepdims=True) / jnp.sum(
            probs, axis=1, keepdims=True
        )
        score_grad = (probs * (prob_grad - centre)).astype(BF)
        score_grad_ref[here, :] = score_grad
        earlier = pl.ds(start, WIN - start)
        key_term = times_cols(before_slots(score_grad, own, start), queries)
        value_term = times_cols(before_slots(low_probs, own, start), rows)
        if tile == 0:
            window_ref[earlier, :HEAD] = key_term
            window_ref[earlier, HEAD:] = value_term
        else:
            window_ref[earlier, :HEAD] += key_term
            window_ref[earlier, HEAD:] += value_term
    natural = natural_ref[...]
    sent_ref[:, :HEAD] = times_plain((window_ref[:, :HEAD] * SCALE).astype(BF), natural).astype(BF)
    sent_ref[:, HEAD:] = times_plain(window_ref[:, HEAD:].astype(BF), natural).astype(BF)


def own_kernel(rows_ref, score_grad_ref, query_ref, keyval_ref, probs_ref, query_grad_ref, own_ref):
    count = query_grad_ref.shape[0]
    own = own_mask()
    for tile in reversed(range(count // TILE)):
        start = tile * TILE
        span = pl.ds(start, SPAN)
        here = pl.ds(tile * HEADS * TILE, HEADS * TILE)
        queries = query_ref[:, pl.ds(start, TILE), :].reshape(HEADS * TILE, HEAD)
        rows = rows_ref[:, pl.ds(start, TILE), :].reshape(HEADS * TILE, HEAD)
        score_grad = score_grad_ref[here, :]
        mixed = (times_plain(unfolded(score_grad, own), keyval_ref[span, :HEAD]) * SCALE).astype(BF)
        for head in range(HEADS):
            query_grad_ref[pl.ds(start, TILE), pl.ds(head * HEAD, HEAD)] = mixed[
                head * TILE : (head + 1) * TILE
            ]
        mine = pl.ds(0, start + TILE)
        key_term = times_cols(own_slots(score_grad, own, start), queries) * SCALE
        value_term = times_cols(own_slots(probs_ref[here, :], own, start), rows)
        if start + TILE == count:
            own_ref[mine, :HEAD] = key_term
            own_ref[mine, HEAD:] = value_term
        else:
            own_ref[mine, :HEAD] += key_term
            own_ref[mine, HEAD:] += value_term


def weights_kernel(
    place_ref, normed_ref, low_ref, attended_ref, query_grad_ref, weight_query_ref,
    normed_grad_ref, mine_ref, *other_refs,
):
    query_grad = query_grad_ref[...]
    normed_grad_ref[...] = times_plain(query_grad, weight_query_ref[...])
    for group, term in (
        (0, times_cols(query_grad, normed_ref[...]).astype(BF)),
        (1, times_cols(attended_ref[...], low_ref[...]).astype(BF)),
    ):
        for half in range(2):
            for owner in range(2):

                @pl.when((place_ref[0] + half) % 2 == owner)
                def _():
                    for first, rows, piece, there in head_rows(half, owner):
                        goal = mine_ref.at[piece, group]
                        if half == 1:
                            goal = other_refs[group].at[piece]
                        goal[there, :] = term[first : first + rows]


def last_kernel(
    tokens_ref, normed_ref, own_ref, came_ref, natural_ref, select_ref, weight_keyval_ref, gains_ref,
    partial_ref, residual_grad_ref, gain_two_ref,
    input_grad_ref, mine_ref, other_ref,
):
    natural = natural_ref[...]
    keyval = jnp.concatenate(
        [
            own_ref[:, :HEAD] + times_rows(came_ref[:, :HEAD], natural),
            own_ref[:, HEAD:] + times_rows(came_ref[:, HEAD:], natural),
        ],
        axis=1,
    ).astype(BF)
    grad = partial_ref[...] + times_plain(keyval, weight_keyval_ref[...])
    part, gain_grad = normalise_back(tokens_ref[...].astype(F32), gains_ref[0:1, :], grad)
    input_grad_ref[...] = residual_grad_ref[...] + part
    row = lax.broadcasted_iota(jnp.int32, (16, gain_grad.shape[1]), 0)
    gain_rows = jnp.where(
        row == 0, gain_grad, jnp.where(row == 1, gain_two_ref[0:1, :], 0.0)
    ).astype(BF)
    rows = jnp.concatenate([times_cols(keyval, normed_ref[...]).astype(BF), gain_rows], axis=0)
    mixed = times_cols(select_ref[...], rows).astype(BF)
    for piece in range(SIDE):
        mine_ref[piece] = mixed[piece * 128 : (piece + 1) * 128]
        other_ref[piece] = mixed[512 + piece * 128 : 512 + (piece + 1) * 128]


def meet_kernel(mine_ref, mine_keyval_ref, *refs):
    for last, goal in enumerate(refs[3:]):
        for k in range(3):
            mine = mine_ref[last, k] if k < 2 else mine_keyval_ref[last]
            goal[k] = (mine.astype(F32) + refs[k][last].astype(F32)).astype(goal.dtype)


def meet(mine, mine_keyval, came, after=()):
    _, rows, width = mine_keyval.shape
    return run(
        meet_kernel,
        [shape((3, rows, width), F32 if k == 0 else BF) for k in range(SIDE)],
        mine,
        mine_keyval,
        *came,
        after=after,
    )


def summed(refs):
    total = refs[0][...]
    for one in refs[1:]:
        total = total + one[...].astype(F32)
    return total


def middle_sum_kernel(*refs):
    total = summed(refs[:-SIDE])
    groups, rows, width = total.shape
    blocks = total.reshape(groups, SIDE, SIDE, 8, width)
    for k, goal in enumerate(refs[-SIDE:]):
        goal[...] = blocks[:, :, k].reshape(groups, 4 * 8, width).astype(goal.dtype)


def middle_sum(held, came, after=()):
    groups, rows, width = held.shape
    return run(
        middle_sum_kernel,
        [shape((groups, rows // SIDE, width), F32 if k == 0 else BF) for k in range(SIDE)],
        held, *came,
        after=after,
        grid=(groups // 3,),
        in_specs=[pl.BlockSpec((3, rows, width), lambda i: (i, 0, 0))] * (1 + len(came)),
        out_specs=[pl.BlockSpec((3, rows // SIDE, width), lambda i: (i, 0, 0))] * SIDE,
    )


def cut_kernel(*refs):
    total = summed(refs[:SIDE])
    rows = total.shape[1] // SIDE
    for k, goal in enumerate(refs[SIDE:]):
        goal[...] = total[:, k * rows : (k + 1) * rows].astype(goal.dtype)


def cut(pieces, came, after=()):
    groups, rows, width = pieces[0].shape
    outs = [shape((groups, rows // SIDE, width), F32 if k == 0 else BF) for k in range(SIDE)]
    return run(cut_kernel, outs, pieces[0], *came, after=after)


def end_kernel(
    place_ref, r0, r1, r2, r3, f0, f1, f2, f3, query_ref, keyval_ref, out_ref, gate_ref, up_ref, down_ref, one_ref, two_ref
):
    total = summed((r0, r1, r2, r3))
    units = summed((f0, f1, f2, f3))
    query_ref[...] = total[0]
    out_ref[...] = total[1]
    keyval_ref[...] = total[2, :4]
    for k, goal in ((0, gate_ref), (2, up_ref), (4, down_ref)):
        goal[...] = units[k : k + 2].reshape(goal.shape)
    width = one_ref.shape[0]
    full = total.shape[-1]
    rows = pltpu.roll(total[2], lax.rem(full - place_ref[0] * width, full), 1)
    one_ref[...] = rows[4, :width]
    two_ref[...] = rows[5, :width]


def local(tokens, gain_attn, gain_ffn, w_query, w_keyval, w_out, w_gate, w_up, w_down, cotangent):
    row_count, model_width = tokens.shape
    place = lax.axis_index(AXES)

    cotangent_other = to_sibling(cotangent)
    spot = place.reshape(1)
    scalar = pl.BlockSpec(memory_space=pltpu.SMEM)
    shards = (w_query, w_out, w_keyval, w_gate, w_up, w_down, gain_attn[None], gain_ffn[None])
    payload, = run(
        payload_kernel,
        [shape((9, 8, model_width), BF)],
        spot, *shards,
        in_specs=[scalar] + [OUTSIDE] * 8,
        limit=60,
        scratch_shapes=[pltpu.VMEM(one.shape, BF) for one in shards] + [pltpu.SemaphoreType.DMA((8,))],
    )
    hop = [((chip * SIDE + 3) * 2 + 1, (chip * SIDE + 7) * 2 + 1) for chip in range(SIDE**2 - 1)]
    ring = [(2 * chip, 2 * chip + 1) for chip in range(SIDE**3)]
    ring += [(2 * chip + 1, 2 * (chip // SIDE * SIDE + (chip + 1) % SIDE)) for chip in range(SIDE**3)]
    chosen, = run(
        choose_kernel,
        [shape(tokens.shape, BF)],
        place.reshape(1), tokens, lax.ppermute(tokens, AXES, hop),
        in_specs=[pl.BlockSpec(memory_space=pltpu.SMEM), WHOLE, WHOLE],
    )
    before = lax.ppermute(chosen, AXES, ring)
    select, natural = run(
        select_kernel,
        [shape((528, 1024), BF), shape((HEAD, HEAD), BF)],
        spot,
        in_specs=[scalar],
    )
    payload, = run(
        pack_kernel,
        [shape((9, SIDE, 8, model_width), BF)],
        *gather_stage(payload, 0),
        flops=4 * 10**9,
    )
    attn, units = run(
        pack_two_kernel,
        [shape((3, SIDE, SIDE, 8, model_width), BF), shape((6, SIDE, SIDE, 8, model_width), BF)],
        *gather_stage(payload, 1),
        after=(chosen, natural),
    )
    attn = gather_stage(attn.reshape(3, 128, model_width), 2)
    units = gather_stage(units.reshape(6, 128, model_width), 2)
    attn += [to_sibling(one) for one in attn]

    (
        residual, normed_two, normed, queries, keyvals, attended, probs, weight_query, weight_out, weight_keyval, gains
    ) = run(
        forward_kernel,
        (
            shape((row_count, model_width), F32),
            shape((row_count, model_width), BF),
            shape((row_count, model_width), BF),
            shape((HEADS, row_count, HEAD), BF),
            shape((2 * row_count, 2 * HEAD), BF),
            shape((row_count, HEADS * HEAD), BF),
            shape((HEADS * row_count, WIN), BF),
            shape((HEADS * HEAD, model_width), BF),
            shape((HEADS * HEAD, model_width), BF),
            shape((2 * HEAD, model_width), BF),
            shape((8, model_width), F32),
        ),
        spot, tokens, before, select, *attn,
        in_specs=[scalar] + [WHOLE] * 11,
    )

    normed_other = to_sibling(normed_two)
    def kept(count):
        return [shape((count, row_count, 512), BF), shape((count, row_count, 256), BF)]

    branch, normed_grad, both_grad, hidden = run(
        ffn_kernel,
        [shape((row_count, model_width), F32)] * 2 + kept(3),
        normed_two, cotangent, units[0], units[2], units[3],
        flops=10**10,
    )
    branch_other, normed_grad_other, both_grad_other, hidden_other = run(
        ffn_kernel,
        [shape((row_count, model_width), F32)] * 2 + kept(3),
        normed_other, cotangent_other, units[0], units[2], units[3],
        after=(normed_grad,),
    )
    branch, normed_grad, both_late, hidden_late, sums, both_late_other, hidden_late_other = run(
        ffn_last_kernel,
        [shape((row_count, model_width), F32)] * 2 + kept(1) + [shape((2, row_count, model_width), BF)] + kept(1),
        normed_two, cotangent, normed_other, cotangent_other, units[1], branch, normed_grad, branch_other, normed_grad_other,
    )
    sums = to_sibling(sums)
    full, part = (6, 128, model_width), (3, 128, model_width)
    held, right, far_right, far_left, left = run(
        ffn_terms_kernel,
        [shape(full, F32), shape(full, BF), shape(part, BF), shape(part, BF), shape(full, BF)],
        normed_two, cotangent, both_grad, hidden, both_late, hidden_late,
        normed_other, cotangent_other, both_grad_other, hidden_other, both_late_other, hidden_late_other,
    )
    from_left, from_right = sent(far_right, 2, 1), sent(far_left, 2, -1)

    output, residual_grad, low, rows, score_grad, keyval_sent, gain_two_grad = run(
        middle_kernel,
        (
            shape((row_count, model_width), BF),
            shape((row_count, model_width), F32),
            shape((row_count, model_width), BF),
            shape((HEADS, row_count, HEAD), BF),
            shape((HEADS * row_count, WIN), BF),
            shape((row_count, 2 * HEAD), BF),
            shape((8, model_width), F32),
        ),
        residual, branch, normed_grad, sums, cotangent, gains, weight_out, queries, keyvals, probs, natural,
        after=(far_left,),
        scratch_shapes=[pltpu.VMEM((row_count, 2 * HEAD), F32)],
    )
    came = shifted(keyval_sent, -1)
    query_grad, keyval_own = run(
        own_kernel,
        (shape((row_count, HEADS * HEAD), BF), shape((row_count, 2 * HEAD), F32)),
        rows, score_grad, queries, keyvals, probs,
    )
    right, left = run(
        relay_kernel, [shape(full, BF)] * 2, right, left, from_left, from_right, after=(query_grad,)
    )
    ffn_back = [sent(right, 2, 1), sent(left, 2, -1)]
    partial, mine, *others = run(
        weights_kernel,
        (shape((row_count, model_width), F32), shape((SIDE, 2, 128, model_width), BF))
        + (shape((SIDE, 128, model_width), BF),) * 2,
        spot, normed, low, attended, query_grad, weight_query,
        after=(right,),
        in_specs=[scalar] + [WHOLE] * 5,
    )
    input_grad, mine_keyval, other_keyval = run(
        last_kernel,
        (shape((row_count, model_width), F32),) + (shape((SIDE, 128, model_width), BF),) * 2,
        tokens, normed, keyval_own, came, natural, select, weight_keyval, gains,
        partial, residual_grad, gain_two_grad,
        flops=2 * 10**9,
    )
    others.append(other_keyval)
    came = [to_sibling(one) for one in others]
    ffn_pieces = middle_sum(held, ffn_back, after=(mine_keyval,))
    ffn_back = scatter_stage(ffn_pieces, SCATTER[1])
    pieces = meet(mine, mine_keyval, came, after=(ffn_pieces[1],))
    pieces = cut(pieces, scatter_stage(pieces, SCATTER_ATTN[2]))
    back = scatter_stage(pieces, SCATTER_ATTN[1])
    ffn_pieces = cut(ffn_pieces, ffn_back, after=(pieces[1],))
    ffn_back = scatter_stage(ffn_pieces, SCATTER[0])
    pieces = cut(pieces, back, after=(ffn_pieces[1],))
    back = scatter_stage(pieces, SCATTER_ATTN[0])
    query, keyval, out, gate, up, down, gain_one, gain_two = run(
        end_kernel,
        [shape(one.shape, F32) for one in (w_query, w_keyval, w_out, w_gate, w_up, w_down, gain_attn, gain_ffn)],
        spot, pieces[0], *back, ffn_pieces[0], *ffn_back,
        in_specs=[scalar] + [WHOLE] * (2 * SIDE),
    )
    return output, input_grad, query, keyval, out, gate, up, down, gain_one, gain_two


def solution(mesh):
    rows, flat = P(AXES, None), P(AXES)
    return jax.shard_map(
        local,
        mesh=mesh,
        in_specs=(rows, flat, flat, rows, rows, rows, rows, rows, rows, rows),
        out_specs=(rows, rows, rows, rows, rows, rows, rows, rows, flat, flat),
        check_vma=False,
    )
```

```python
import math

import jax
import jax.numpy as jnp
from jax import lax
from jax.experimental import pallas as pl
from jax.experimental.pallas import tpu as pltpu
from jax.sharding import PartitionSpec as P

HEADS = 4
HEAD = 256
WIN = 512
SIDE = 4

EPSILON = 1e-06
MASKED = -1e30
AXES = ("ctx", "hd")
BF = jnp.bfloat16
F32 = jnp.float32

SCALE = 1.0 / math.sqrt(HEAD)
TILE = 128
SPAN = WIN + TILE
MEGA = 1 << 20

GATHER = ((2, 2), (1, 0), (0, 1))
SCATTER = ((1, 0), (2, 2), (0, 1))
SCATTER_ATTN = ((2, 2), (1, 0), (0, 1))


def chip_pairs(axis_of_core, steps):
    pairs = []
    for chip in range(SIDE**3):
        spot = [chip // SIDE**2, chip // SIDE % SIDE, chip % SIDE]
        for core in range(2):
            goal = list(spot)
            axis = axis_of_core[core]
            goal[axis] = (goal[axis] + steps) % SIDE
            target = (goal[0] * SIDE + goal[1]) * SIDE + goal[2]
            pairs.append((chip * 2 + core, target * 2 + core))
    return pairs


def to_sibling(value):
    return lax.ppermute(value, "hd", [(0, 1), (1, 0)])


def gather_stage(value, stage):
    return [value] + [
        lax.ppermute(value, AXES, chip_pairs(GATHER[stage], -steps)) for steps in range(1, SIDE)
    ]


def scatter_stage(pieces, axis_of_core):
    return [
        lax.ppermute(pieces[steps], AXES, chip_pairs(axis_of_core, steps))
        for steps in range(1, SIDE)
    ]


def sent(value, stage, steps):
    return lax.ppermute(value, AXES, chip_pairs(SCATTER[stage], steps))


def shifted(value, steps):
    count = lax.axis_size(AXES)
    initial, last = (max(0, -steps), min(count, count - steps))
    return lax.ppermute(value, AXES, [(source, source + steps) for source in range(initial, last)])


def times_rows(left, right):
    return lax.dot_general(left, right, (((1,), (1,)), ((), ())), preferred_element_type=F32)


def times_cols(left, right):
    return lax.dot_general(left, right, (((0,), (0,)), ((), ())), preferred_element_type=F32)


def times_plain(left, right):
    return jnp.dot(left, right, preferred_element_type=F32)


def shape(dims, kind):
    return jax.ShapeDtypeStruct(dims, kind)


WHOLE = pl.BlockSpec(memory_space=pltpu.VMEM)
ANYWHERE = pl.BlockSpec(memory_space=pl.ANY)
OUTSIDE = pl.BlockSpec(memory_space=pltpu.HBM)


def run(kernel, outs, *operands, after=(), limit=16, flops=1, in_specs=None, **more):
    count = len(operands)

    def body(*refs):
        kernel(*refs[:count], *refs[count + len(after) :])

    return pl.pallas_call(
        body,
        out_shape=outs,
        in_specs=list(in_specs or [WHOLE] * count) + [ANYWHERE] * len(after),
        cost_estimate=pl.CostEstimate(flops=flops, bytes_accessed=1, transcendentals=0),
        compiler_params=pltpu.CompilerParams(vmem_limit_bytes=limit * MEGA),
        **more,
    )(*operands, *after)


def select_kernel(place_ref, select_ref, natural_ref):
    place = place_ref[0]
    core = place % 2
    chip = place // 2
    spot = [chip // SIDE**2, chip // SIDE % SIDE, chip % SIDE]

    def device_of(half, piece, first, second):
        owner = half * (1 - core) + (1 - half) * core
        x = (spot[0] + jnp.where(owner == 0, piece, first)) % SIDE
        y = (spot[1] + jnp.where(owner == 0, first, piece)) % SIDE
        z = (spot[2] + second) % SIDE
        return ((x * SIDE + y) * SIDE + z) * 2 + owner

    row = lax.broadcasted_iota(jnp.int32, (528, 1), 0)
    feature = row % HEAD
    high, low = feature // 32 % 4, feature // 8 % 4
    device = device_of(feature // 128, high, high, low)
    goal = jnp.where(row < 512, row // HEAD * HEAD + device % 32 * 8 + feature % 8, -2)
    column = lax.broadcasted_iota(jnp.int32, (1, 1024), 1)
    device = device_of(column // 512, column // 128 % 4, column // 32 % 4, column // 8 % 4)
    part = column % 8
    have = jnp.where(part < 4, device * 4 + part, -1)
    gain = jnp.where(row >= 512, row - 508, -1)
    select_ref[...] = jnp.where(
        (goal == have) | ((gain == part) & (part < 6)), 1.0, 0.0
    ).astype(BF)
    natural_ref[...] = jnp.where(
        goal[:HEAD] == lax.broadcasted_iota(jnp.int32, (1, HEAD), 1), 1.0, 0.0
    ).astype(BF)


def normalise(values, gain):
    inverse = lax.rsqrt(jnp.mean(values * values, axis=-1, keepdims=True) + EPSILON)
    return (values * inverse * gain).astype(BF)


def normalise_back(values, gain, grad):
    inverse = lax.rsqrt(jnp.mean(values * values, axis=-1, keepdims=True) + EPSILON)
    unit = values * inverse
    gain_grad = jnp.sum(grad * unit, axis=0, keepdims=True)
    scaled = grad * gain
    return inverse * (scaled - unit * jnp.mean(scaled * unit, axis=-1, keepdims=True)), gain_grad


def own_mask():
    row = lax.broadcasted_iota(jnp.int32, (HEADS * TILE, TILE), 0) % TILE
    column = lax.broadcasted_iota(jnp.int32, (HEADS * TILE, TILE), 1)
    return column <= row


def folded(wide, own):
    return jnp.concatenate(
        [jnp.where(own, wide[:, WIN:], wide[:, :TILE]), wide[:, TILE:WIN]], axis=1
    )


def unfolded(narrow, own):
    edge = narrow[:, :TILE]
    none = jnp.zeros_like(edge)
    return jnp.concatenate(
        [jnp.where(own, none, edge), narrow[:, TILE:], jnp.where(own, edge, none)], axis=1
    )


def payload_kernel(place_ref, *refs):
    sources, (payload_ref, *places, sems) = refs[:8], refs[8:]
    copies = [
        pltpu.make_async_copy(source, goal, sems.at[k])
        for k, (source, goal) in enumerate(zip(sources, places))
    ]
    for one in copies:
        one.start()
    for one in copies:
        one.wait()
    query_ref, out_ref, keyval_ref, gate_ref, up_ref, down_ref, gain_one_ref, gain_two_ref = places
    width = gain_one_ref.shape[1]
    row = lax.broadcasted_iota(jnp.int32, (8, query_ref.shape[1]), 0)
    lane = lax.broadcasted_iota(jnp.int32, (8, query_ref.shape[1]), 1) - place_ref[0] * width
    gains = jnp.zeros(row.shape, F32)
    for k, ref in ((4, gain_one_ref), (5, gain_two_ref)):
        values = ref[...].astype(F32)
        for i in range(width):
            gains = jnp.where((row == k) & (lane == i), values[:, i : i + 1], gains)
    keyval = jnp.concatenate([keyval_ref[...].astype(F32), gains[4:]], axis=0)
    payload_ref[0] = query_ref[...]
    payload_ref[1] = out_ref[...]
    payload_ref[2] = keyval.astype(BF)
    for k, ref in ((3, gate_ref), (5, up_ref), (7, down_ref)):
        payload_ref[k : k + 2] = ref[...].reshape(2, 8, -1)


def pack_kernel(r0, r1, r2, r3, goal_ref):
    groups, rows, width = r0.shape
    for k, ref in enumerate((r0, r1, r2, r3)):
        goal_ref[:, k] = ref[...]


def choose_kernel(place_ref, own_ref, hop_ref, goal_ref):
    edge = place_ref[0] % (2 * SIDE) == 2 * SIDE - 1

    @pl.when(edge)
    def _():
        goal_ref[...] = hop_ref[...]

    @pl.when(jnp.logical_not(edge))
    def _():
        goal_ref[...] = own_ref[...]


def pack_two_kernel(r0, r1, r2, r3, attn_ref, units_ref):
    for k, ref in enumerate((r0, r1, r2, r3)):
        attn_ref[:, k] = ref[:3]
        units_ref[:, k] = ref[3:]


def before_slots(narrow, own, start):
    edge = jnp.where(own, jnp.zeros_like(narrow[:, :TILE]), narrow[:, :TILE])
    return jnp.concatenate([edge, narrow[:, TILE : WIN - start]], axis=1) if start < WIN - TILE else edge


def own_slots(narrow, own, start):
    edge = jnp.where(own, narrow[:, :TILE], jnp.zeros_like(narrow[:, :TILE]))
    return jnp.concatenate([narrow[:, WIN - start :], edge], axis=1) if start > 0 else edge


def head_rows(half, owner):
    for head in range(HEADS):
        first = head * HEAD + half * 128
        if owner == 0:
            yield first, 128, head, pl.ds(0, 128)
        else:
            for piece in range(SIDE):
                yield first + piece * 32, 32, piece, pl.ds(head * 32, 32)


def forward_kernel(
    place_ref, tokens_ref, before_ref, select_ref, a0, a1, a2, a3, b0, b1, b2, b3,
    residual_ref, normed_two_ref, normed_ref, query_ref, keyval_ref, attended_ref, probs_ref,
    weight_query_ref, weight_out_ref, weight_keyval_ref, gains_ref,
):
    count = tokens_ref.shape[0]
    halves = ((a0, a1, a2, a3), (b0, b1, b2, b3))
    for half in range(2):
        for owner in range(2):

            @pl.when((place_ref[0] + half) % 2 == owner)
            def _():
                for first, rows, piece, there in head_rows(half, owner):
                    here = pl.ds(first, rows)
                    weight_query_ref[here, :] = halves[half][piece][0, there, :]
                    weight_out_ref[here, :] = halves[half][piece][1, there, :]

    mixed = jnp.concatenate([one[2] for half in halves for one in half], axis=0)
    sorted_rows = times_plain(select_ref[...], mixed)
    weight_keyval_ref[...] = sorted_rows[:512].astype(BF)
    gains_ref[...] = sorted_rows[512:520]
    gain_one = sorted_rows[512:513]
    gain_two = sorted_rows[513:514]
    inputs = tokens_ref[...].astype(F32)
    normed = normalise(inputs, gain_one)
    normed_ref[...] = normed
    normed_before = normalise(before_ref[...].astype(F32), gain_one)
    weight_keyval = weight_keyval_ref[...]
    keyval_ref[:WIN, :] = times_rows(normed_before, weight_keyval).astype(BF)
    keyval_ref[WIN:, :] = times_rows(normed, weight_keyval).astype(BF)
    for head in range(HEADS):
        query_ref[head] = times_rows(
            normed, weight_query_ref[pl.ds(head * HEAD, HEAD), :]
        ).astype(BF) * BF(SCALE)
    own = own_mask()
    first_key = jnp.where(place_ref[0] == 0, WIN, 0)

    def scores_of(tile):
        queries = query_ref[:, pl.ds(tile * TILE, TILE), :].reshape(HEADS * TILE, HEAD)
        return times_rows(queries, keyval_ref[pl.ds(tile * TILE, SPAN), :HEAD])

    ahead = scores_of(0)
    for tile in range(count // TILE):
        start = tile * TILE
        scores = folded(ahead, own)
        if start + TILE < count:
            ahead = scores_of(tile + 1)
        slot = start + lax.broadcasted_iota(jnp.int32, (1, WIN), 1)
        hidden = jnp.where(slot >= first_key, 0.0, MASKED)
        scores = jnp.concatenate(
            [scores[:, :TILE] + jnp.where(own, 0.0, hidden[:, :TILE]), scores[:, TILE:] + hidden[:, TILE:]],
            axis=1,
        )
        raised = jnp.exp(scores - jnp.max(scores, axis=1, keepdims=True))
        probs = (raised * (1.0 / jnp.sum(raised, axis=1, keepdims=True))).astype(BF)
        probs_ref[pl.ds(tile * HEADS * TILE, HEADS * TILE), :] = probs
        mixed = times_plain(unfolded(probs, own), keyval_ref[pl.ds(start, SPAN), HEAD:]).astype(BF)
        for head in range(HEADS):
            attended_ref[pl.ds(start, TILE), pl.ds(head * HEAD, HEAD)] = mixed[
                head * TILE : (head + 1) * TILE
            ]

    residual = inputs + times_plain(attended_ref[...], weight_out_ref[...])
    residual_ref[...] = residual
    normed_two_ref[...] = normalise(residual, gain_two)


GELU_A = math.sqrt(2.0 / math.pi)
GELU_B = 0.044715


def ffn_products(normed, grad, ref):
    return times_rows(normed, ref[0:4].reshape(512, -1)), times_rows(grad, ref[4:6].reshape(256, -1))


def ffn_units(both, hidden_grad):
    gate, up = both[:, :256], both[:, 256:]
    square = gate * gate
    bend = jnp.tanh(GELU_A * gate * (1.0 + GELU_B * square))
    half = 0.5 * (1.0 + bend)
    active = gate * half
    slope = half + 0.5 * gate * (1.0 - bend * bend) * (GELU_A + (3.0 * GELU_A * GELU_B) * square)
    both_grad = jnp.concatenate(
        [(hidden_grad * up * slope).astype(BF), (hidden_grad * active).astype(BF)], axis=1
    )
    return (active * up).astype(BF), both_grad


def ffn_sums(normed_ref, grad_ref, weights, both_grad_ref, hidden_ref, branch=None, normed_grad=None):
    normed = normed_ref[...]
    grad = grad_ref[...]
    ahead = ffn_products(normed, grad, weights[0])
    for k, ref in enumerate(weights):
        now = ahead
        if k + 1 < len(weights):
            ahead = ffn_products(normed, grad, weights[k + 1])
        hidden, both_grad = ffn_units(*now)
        hidden_ref[k] = hidden
        both_grad_ref[k] = both_grad
        branch_term = times_plain(hidden, ref[4:6].reshape(256, -1))
        normed_term = times_plain(both_grad, ref[0:4].reshape(512, -1))
        branch = branch_term if branch is None else branch + branch_term
        normed_grad = normed_term if normed_grad is None else normed_grad + normed_term
    return branch, normed_grad


def ffn_kernel(normed_ref, grad_ref, w0, w1, w2, branch_ref, normed_grad_ref, both_grad_ref, hidden_ref):
    branch_ref[...], normed_grad_ref[...] = ffn_sums(
        normed_ref, grad_ref, (w0, w1, w2), both_grad_ref, hidden_ref
    )


def ffn_last_kernel(
    normed_ref, grad_ref, normed_other_ref, grad_other_ref, w0, branch_in_ref, normed_grad_in_ref, branch_other_ref, normed_grad_other_ref,
    branch_ref, normed_grad_ref, both_grad_ref, hidden_ref, sums_ref, both_grad_other_ref, hidden_other_ref,
):
    branch, normed_grad = ffn_sums(
        normed_other_ref, grad_other_ref, (w0,), both_grad_other_ref, hidden_other_ref,
        branch_other_ref[...], normed_grad_other_ref[...],
    )
    sums_ref[0] = branch.astype(BF)
    sums_ref[1] = normed_grad.astype(BF)
    branch_ref[...], normed_grad_ref[...] = ffn_sums(
        normed_ref, grad_ref, (w0,), both_grad_ref, hidden_ref, branch_in_ref[...], normed_grad_in_ref[...]
    )


def ffn_terms_kernel(
    normed_ref, grad_ref, both_ref, hidden_ref, both_late_ref, hidden_late_ref,
    normed_other_ref, grad_other_ref, both_other_ref, hidden_other_ref, both_late_other_ref, hidden_late_other_ref,
    held_ref, right_ref, far_right_ref, far_left_ref, left_ref,
):
    for k, goal in ((2, None), (0, held_ref), (1, right_ref), (3, left_ref)):
        if k == 2:
            parts = (both_late_ref[0], hidden_late_ref[0], both_late_other_ref[0], hidden_late_other_ref[0])
        else:
            parts = [ref[min(k, 2)] for ref in (both_ref, hidden_ref, both_other_ref, hidden_other_ref)]
        both = times_cols(parts[0], normed_ref[...]) + times_cols(parts[2], normed_other_ref[...])
        down = times_cols(parts[1], grad_ref[...]) + times_cols(parts[3], grad_other_ref[...])
        both, down = both.reshape(4, 128, -1), down.reshape(2, 128, -1)
        if k == 2:
            far_right_ref[...] = both[:3].astype(BF)
            far_left_ref[0:1] = both[3:].astype(BF)
            far_left_ref[1:3] = down.astype(BF)
        else:
            goal[0:4] = both.astype(goal.dtype)
            goal[4:6] = down.astype(goal.dtype)


def relay_kernel(right_ref, left_ref, from_left_ref, from_right_ref, right_goal, left_goal):
    right_goal[0:3] = (right_ref[0:3].astype(F32) + from_left_ref[...].astype(F32)).astype(BF)
    right_goal[3:6] = right_ref[3:6]
    left_goal[0:3] = left_ref[0:3]
    left_goal[3:6] = (left_ref[3:6].astype(F32) + from_right_ref[...].astype(F32)).astype(BF)


def middle_kernel(
    residual_ref, branch_ref, normed_grad_ref, sums_ref, cotangent_ref, gains_ref, weight_out_ref, query_ref, keyval_ref, probs_ref,
    natural_ref, output_ref, residual_grad_ref, low_ref, rows_ref, score_grad_ref, sent_ref, gain_ref, window_ref,
):
    count = residual_ref.shape[0]
    residual = residual_ref[...]
    output_ref[...] = (residual + branch_ref[...] + sums_ref[0].astype(F32)).astype(BF)
    normed_grad = normed_grad_ref[...] + sums_ref[1].astype(F32)
    part, gain_grad = normalise_back(residual, gains_ref[1:2, :], normed_grad)
    gain_ref[...] = jnp.broadcast_to(gain_grad, gain_ref.shape)
    residual_grad = cotangent_ref[...].astype(F32) + part
    residual_grad_ref[...] = residual_grad
    low = residual_grad.astype(BF)
    low_ref[...] = low
    for head in range(HEADS):
        rows_ref[head] = times_rows(low, weight_out_ref[pl.ds(head * HEAD, HEAD), :]).astype(BF)
    own = own_mask()

    def rows_of(tile):
        return rows_ref[:, pl.ds(tile * TILE, TILE), :].reshape(HEADS * TILE, HEAD)

    def grads_of(tile):
        return times_rows(rows_of(tile), keyval_ref[pl.ds(tile * TILE, SPAN), HEAD:])

    ahead = grads_of(0)
    for tile in range(count // TILE):
        start = tile * TILE
        here = pl.ds(tile * HEADS * TILE, HEADS * TILE)
        queries = query_ref[:, pl.ds(start, TILE), :].reshape(HEADS * TILE, HEAD)
        rows = rows_of(tile)
        low_probs = probs_ref[here, :]
        probs = low_probs.astype(F32)
        prob_grad = folded(ahead, own)
        if start + TILE < count:
            ahead = grads_of(tile + 1)
        centre = jnp.sum(probs * prob_grad, axis=1, keepdims=True) / jnp.sum(
            probs, axis=1, keepdims=True
        )
        score_grad = (probs * (prob_grad - centre)).astype(BF)
        score_grad_ref[here, :] = score_grad
        earlier = pl.ds(start, WIN - start)
        key_term = times_cols(before_slots(score_grad, own, start), queries)
        value_term = times_cols(before_slots(low_probs, own, start), rows)
        if tile == 0:
            window_ref[earlier, :HEAD] = key_term
            window_ref[earlier, HEAD:] = value_term
        else:
            window_ref[earlier, :HEAD] += key_term
            window_ref[earlier, HEAD:] += value_term
    natural = natural_ref[...]
    sent_ref[:, :HEAD] = times_plain(window_ref[:, :HEAD].astype(BF), natural).astype(BF)
    sent_ref[:, HEAD:] = times_plain(window_ref[:, HEAD:].astype(BF), natural).astype(BF)


def own_kernel(rows_ref, score_grad_ref, query_ref, keyval_ref, probs_ref, query_grad_ref, own_ref):
    count = query_grad_ref.shape[0]
    own = own_mask()
    for tile in reversed(range(count // TILE)):
        start = tile * TILE
        span = pl.ds(start, SPAN)
        here = pl.ds(tile * HEADS * TILE, HEADS * TILE)
        queries = query_ref[:, pl.ds(start, TILE), :].reshape(HEADS * TILE, HEAD)
        rows = rows_ref[:, pl.ds(start, TILE), :].reshape(HEADS * TILE, HEAD)
        score_grad = score_grad_ref[here, :]
        mixed = (times_plain(unfolded(score_grad, own), keyval_ref[span, :HEAD]) * SCALE).astype(BF)
        for head in range(HEADS):
            query_grad_ref[pl.ds(start, TILE), pl.ds(head * HEAD, HEAD)] = mixed[
                head * TILE : (head + 1) * TILE
            ]
        mine = pl.ds(0, start + TILE)
        key_term = times_cols(own_slots(score_grad, own, start), queries)
        value_term = times_cols(own_slots(probs_ref[here, :], own, start), rows)
        if start + TILE == count:
            own_ref[mine, :HEAD] = key_term
            own_ref[mine, HEAD:] = value_term
        else:
            own_ref[mine, :HEAD] += key_term
            own_ref[mine, HEAD:] += value_term


def weights_kernel(
    place_ref, normed_ref, low_ref, attended_ref, query_grad_ref, weight_query_ref,
    normed_grad_ref, mine_ref, *other_refs,
):
    query_grad = query_grad_ref[...]
    normed_grad_ref[...] = times_plain(query_grad, weight_query_ref[...])
    for group, term in (
        (0, times_cols(query_grad, normed_ref[...]).astype(BF)),
        (1, times_cols(attended_ref[...], low_ref[...]).astype(BF)),
    ):
        for half in range(2):
            for owner in range(2):

                @pl.when((place_ref[0] + half) % 2 == owner)
                def _():
                    for first, rows, piece, there in head_rows(half, owner):
                        goal = mine_ref.at[piece, group]
                        if half == 1:
                            goal = other_refs[group].at[piece]
                        goal[there, :] = term[first : first + rows]


def last_kernel(
    tokens_ref, normed_ref, own_ref, came_ref, natural_ref, select_ref, weight_keyval_ref, gains_ref,
    partial_ref, residual_grad_ref, gain_two_ref,
    input_grad_ref, mine_ref, other_ref,
):
    natural = natural_ref[...]
    keyval = jnp.concatenate(
        [
            own_ref[:, :HEAD] + times_rows(came_ref[:, :HEAD], natural),
            own_ref[:, HEAD:] + times_rows(came_ref[:, HEAD:], natural),
        ],
        axis=1,
    ).astype(BF)
    grad = partial_ref[...] + times_plain(keyval, weight_keyval_ref[...])
    part, gain_grad = normalise_back(tokens_ref[...].astype(F32), gains_ref[0:1, :], grad)
    input_grad_ref[...] = residual_grad_ref[...] + part
    row = lax.broadcasted_iota(jnp.int32, (16, gain_grad.shape[1]), 0)
    gain_rows = jnp.where(
        row == 0, gain_grad, jnp.where(row == 1, gain_two_ref[0:1, :], 0.0)
    ).astype(BF)
    rows = jnp.concatenate([times_cols(keyval, normed_ref[...]).astype(BF), gain_rows], axis=0)
    mixed = times_cols(select_ref[...], rows).astype(BF)
    for piece in range(SIDE):
        mine_ref[piece] = mixed[piece * 128 : (piece + 1) * 128]
        other_ref[piece] = mixed[512 + piece * 128 : 512 + (piece + 1) * 128]


def meet_kernel(mine_ref, mine_keyval_ref, *refs):
    for last, goal in enumerate(refs[3:]):
        for k in range(3):
            mine = mine_ref[last, k] if k < 2 else mine_keyval_ref[last]
            goal[k] = (mine.astype(F32) + refs[k][last].astype(F32)).astype(goal.dtype)


def meet(mine, mine_keyval, came, after=()):
    _, rows, width = mine_keyval.shape
    return run(
        meet_kernel,
        [shape((3, rows, width), F32 if k == 0 else BF) for k in range(SIDE)],
        mine,
        mine_keyval,
        *came,
        after=after,
    )


def summed(refs):
    total = refs[0][...]
    for one in refs[1:]:
        total = total + one[...].astype(F32)
    return total


def middle_sum_kernel(*refs):
    total = summed(refs[:-SIDE])
    groups, rows, width = total.shape
    blocks = total.reshape(groups, SIDE, SIDE, 8, width)
    for k, goal in enumerate(refs[-SIDE:]):
        goal[...] = blocks[:, :, k].reshape(groups, 4 * 8, width).astype(goal.dtype)


def middle_sum(held, came, after=()):
    groups, rows, width = held.shape
    return run(
        middle_sum_kernel,
        [shape((groups, rows // SIDE, width), F32 if k == 0 else BF) for k in range(SIDE)],
        held, *came,
        after=after,
        grid=(groups // 3,),
        in_specs=[pl.BlockSpec((3, rows, width), lambda i: (i, 0, 0))] * (1 + len(came)),
        out_specs=[pl.BlockSpec((3, rows // SIDE, width), lambda i: (i, 0, 0))] * SIDE,
    )


def cut_kernel(*refs):
    total = summed(refs[:SIDE])
    rows = total.shape[1] // SIDE
    for k, goal in enumerate(refs[SIDE:]):
        goal[...] = total[:, k * rows : (k + 1) * rows].astype(goal.dtype)


def cut(pieces, came, after=()):
    groups, rows, width = pieces[0].shape
    outs = [shape((groups, rows // SIDE, width), F32 if k == 0 else BF) for k in range(SIDE)]
    return run(cut_kernel, outs, pieces[0], *came, after=after)


def end_kernel(
    place_ref, r0, r1, r2, r3, f0, f1, f2, f3, query_ref, keyval_ref, out_ref, gate_ref, up_ref, down_ref, one_ref, two_ref
):
    total = summed((r0, r1, r2, r3))
    units = summed((f0, f1, f2, f3))
    query_ref[...] = total[0]
    out_ref[...] = total[1]
    keyval_ref[...] = total[2, :4]
    for k, goal in ((0, gate_ref), (2, up_ref), (4, down_ref)):
        goal[...] = units[k : k + 2].reshape(goal.shape)
    width = one_ref.shape[0]
    full = total.shape[-1]
    rows = pltpu.roll(total[2], lax.rem(full - place_ref[0] * width, full), 1)
    one_ref[...] = rows[4, :width]
    two_ref[...] = rows[5, :width]


def local(tokens, gain_attn, gain_ffn, w_query, w_keyval, w_out, w_gate, w_up, w_down, cotangent):
    row_count, model_width = tokens.shape
    place = lax.axis_index(AXES)

    cotangent_other = to_sibling(cotangent)
    spot = place.reshape(1)
    scalar = pl.BlockSpec(memory_space=pltpu.SMEM)
    shards = (w_query, w_out, w_keyval, w_gate, w_up, w_down, gain_attn[None], gain_ffn[None])
    payload, = run(
        payload_kernel,
        [shape((9, 8, model_width), BF)],
        spot, *shards,
        in_specs=[scalar] + [OUTSIDE] * 8,
        limit=60,
        scratch_shapes=[pltpu.VMEM(one.shape, BF) for one in shards] + [pltpu.SemaphoreType.DMA((8,))],
    )
    hop = [((chip * SIDE + 3) * 2 + 1, (chip * SIDE + 7) * 2 + 1) for chip in range(SIDE**2 - 1)]
    ring = [(2 * chip, 2 * chip + 1) for chip in range(SIDE**3)]
    ring += [(2 * chip + 1, 2 * (chip // SIDE * SIDE + (chip + 1) % SIDE)) for chip in range(SIDE**3)]
    chosen, = run(
        choose_kernel,
        [shape(tokens.shape, BF)],
        place.reshape(1), tokens, lax.ppermute(tokens, AXES, hop),
        in_specs=[pl.BlockSpec(memory_space=pltpu.SMEM), WHOLE, WHOLE],
    )
    before = lax.ppermute(chosen, AXES, ring)
    select, natural = run(
        select_kernel,
        [shape((528, 1024), BF), shape((HEAD, HEAD), BF)],
        spot,
        in_specs=[scalar],
    )
    payload, = run(
        pack_kernel,
        [shape((9, SIDE, 8, model_width), BF)],
        *gather_stage(payload, 0),
        flops=4 * 10**9,
    )
    attn, units = run(
        pack_two_kernel,
        [shape((3, SIDE, SIDE, 8, model_width), BF), shape((6, SIDE, SIDE, 8, model_width), BF)],
        *gather_stage(payload, 1),
        after=(chosen, natural),
    )
    attn = gather_stage(attn.reshape(3, 128, model_width), 2)
    units = gather_stage(units.reshape(6, 128, model_width), 2)
    attn += [to_sibling(one) for one in attn]

    (
        residual, normed_two, normed, queries, keyvals, attended, probs, weight_query, weight_out, weight_keyval, gains
    ) = run(
        forward_kernel,
        (
            shape((row_count, model_width), F32),
            shape((row_count, model_width), BF),
            shape((row_count, model_width), BF),
            shape((HEADS, row_count, HEAD), BF),
            shape((2 * row_count, 2 * HEAD), BF),
            shape((row_count, HEADS * HEAD), BF),
            shape((HEADS * row_count, WIN), BF),
            shape((HEADS * HEAD, model_width), BF),
            shape((HEADS * HEAD, model_width), BF),
            shape((2 * HEAD, model_width), BF),
            shape((8, model_width), F32),
        ),
        spot, tokens, before, select, *attn,
        in_specs=[scalar] + [WHOLE] * 11,
    )

    normed_other = to_sibling(normed_two)
    def kept(count):
        return [shape((count, row_count, 512), BF), shape((count, row_count, 256), BF)]

    branch, normed_grad, both_grad, hidden = run(
        ffn_kernel,
        [shape((row_count, model_width), F32)] * 2 + kept(3),
        normed_two, cotangent, units[0], units[1], units[3],
        flops=10**10,
    )
    branch_other, normed_grad_other, both_grad_other, hidden_other = run(
        ffn_kernel,
        [shape((row_count, model_width), F32)] * 2 + kept(3),
        normed_other, cotangent_other, units[0], units[1], units[3],
        after=(normed_grad,),
    )
    branch, normed_grad, both_late, hidden_late, sums, both_late_other, hidden_late_other = run(
        ffn_last_kernel,
        [shape((row_count, model_width), F32)] * 2 + kept(1) + [shape((2, row_count, model_width), BF)] + kept(1),
        normed_two, cotangent, normed_other, cotangent_other, units[2], branch, normed_grad, branch_other, normed_grad_other,
    )
    sums = to_sibling(sums)
    full, part = (6, 128, model_width), (3, 128, model_width)
    held, right, far_right, far_left, left = run(
        ffn_terms_kernel,
        [shape(full, F32), shape(full, BF), shape(part, BF), shape(part, BF), shape(full, BF)],
        normed_two, cotangent, both_grad, hidden, both_late, hidden_late,
        normed_other, cotangent_other, both_grad_other, hidden_other, both_late_other, hidden_late_other,
    )
    from_left, from_right = sent(far_right, 2, 1), sent(far_left, 2, -1)

    output, residual_grad, low, rows, score_grad, keyval_sent, gain_two_grad = run(
        middle_kernel,
        (
            shape((row_count, model_width), BF),
            shape((row_count, model_width), F32),
            shape((row_count, model_width), BF),
            shape((HEADS, row_count, HEAD), BF),
            shape((HEADS * row_count, WIN), BF),
            shape((row_count, 2 * HEAD), BF),
            shape((8, model_width), F32),
        ),
        residual, branch, normed_grad, sums, cotangent, gains, weight_out, queries, keyvals, probs, natural,
        after=(far_left,),
        scratch_shapes=[pltpu.VMEM((row_count, 2 * HEAD), F32)],
    )
    came = shifted(keyval_sent, -1)
    query_grad, keyval_own = run(
        own_kernel,
        (shape((row_count, HEADS * HEAD), BF), shape((row_count, 2 * HEAD), F32)),
        rows, score_grad, queries, keyvals, probs,
    )
    right, left = run(
        relay_kernel, [shape(full, BF)] * 2, right, left, from_left, from_right, after=(query_grad,)
    )
    ffn_back = [sent(right, 2, 1), sent(left, 2, -1)]
    partial, mine, *others = run(
        weights_kernel,
        (shape((row_count, model_width), F32), shape((SIDE, 2, 128, model_width), BF))
        + (shape((SIDE, 128, model_width), BF),) * 2,
        spot, normed, low, attended, query_grad, weight_query,
        after=(right,),
        in_specs=[scalar] + [WHOLE] * 5,
    )
    input_grad, mine_keyval, other_keyval = run(
        last_kernel,
        (shape((row_count, model_width), F32),) + (shape((SIDE, 128, model_width), BF),) * 2,
        tokens, normed, keyval_own, came, natural, select, weight_keyval, gains,
        partial, residual_grad, gain_two_grad,
        flops=2 * 10**9,
    )
    others.append(other_keyval)
    came = [to_sibling(one) for one in others]
    ffn_pieces = middle_sum(held, ffn_back, after=(mine_keyval,))
    ffn_back = scatter_stage(ffn_pieces, SCATTER[1])
    pieces = meet(mine, mine_keyval, came, after=(ffn_pieces[1],))
    pieces = cut(pieces, scatter_stage(pieces, SCATTER_ATTN[2]))
    back = scatter_stage(pieces, SCATTER_ATTN[1])
    ffn_pieces = cut(ffn_pieces, ffn_back, after=(pieces[1],))
    ffn_back = scatter_stage(ffn_pieces, SCATTER[0])
    pieces = cut(pieces, back, after=(ffn_pieces[1],))
    back = scatter_stage(pieces, SCATTER_ATTN[0])
    query, keyval, out, gate, up, down, gain_one, gain_two = run(
        end_kernel,
        [shape(one.shape, F32) for one in (w_query, w_keyval, w_out, w_gate, w_up, w_down, gain_attn, gain_ffn)],
        spot, pieces[0], *back, ffn_pieces[0], *ffn_back,
        in_specs=[scalar] + [WHOLE] * (2 * SIDE),
    )
    return output, input_grad, query, keyval, out, gate, up, down, gain_one, gain_two


def solution(mesh):
    rows, flat = P(AXES, None), P(AXES)
    return jax.shard_map(
        local,
        mesh=mesh,
        in_specs=(rows, flat, flat, rows, rows, rows, rows, rows, rows, rows),
        out_specs=(rows, rows, rows, rows, rows, rows, rows, rows, flat, flat),
        check_vma=False,
    )
```

```python
import math

import jax
import jax.numpy as jnp
from jax import lax
from jax.experimental import pallas as pl
from jax.experimental.pallas import tpu as pltpu
from jax.sharding import PartitionSpec as P

HEADS = 4
HEAD = 256
WIN = 512
SIDE = 4

EPSILON = 1e-06
MASKED = -1e30
AXES = ("ctx", "hd")
BF = jnp.bfloat16
F32 = jnp.float32

SCALE = 1.0 / math.sqrt(HEAD)
TILE = 128
SPAN = WIN + TILE
MEGA = 1 << 20

GATHER = ((2, 2), (1, 0), (0, 1))
SCATTER = ((1, 0), (2, 2), (0, 1))
SCATTER_ATTN = ((2, 2), (1, 0), (0, 1))


def chip_pairs(axis_of_core, steps):
    pairs = []
    for chip in range(SIDE**3):
        spot = [chip // SIDE**2, chip // SIDE % SIDE, chip % SIDE]
        for core in range(2):
            goal = list(spot)
            axis = axis_of_core[core]
            goal[axis] = (goal[axis] + steps) % SIDE
            target = (goal[0] * SIDE + goal[1]) * SIDE + goal[2]
            pairs.append((chip * 2 + core, target * 2 + core))
    return pairs


def to_sibling(value):
    return lax.ppermute(value, "hd", [(0, 1), (1, 0)])


def gather_stage(value, stage):
    return [value] + [
        lax.ppermute(value, AXES, chip_pairs(GATHER[stage], -steps)) for steps in range(1, SIDE)
    ]


def scatter_stage(pieces, axis_of_core):
    return [
        lax.ppermute(pieces[steps], AXES, chip_pairs(axis_of_core, steps))
        for steps in range(1, SIDE)
    ]


def sent(value, stage, steps):
    return lax.ppermute(value, AXES, chip_pairs(SCATTER[stage], steps))


def shifted(value, steps):
    count = lax.axis_size(AXES)
    initial, last = (max(0, -steps), min(count, count - steps))
    return lax.ppermute(value, AXES, [(source, source + steps) for source in range(initial, last)])


def times_rows(left, right):
    return lax.dot_general(left, right, (((1,), (1,)), ((), ())), preferred_element_type=F32)


def times_cols(left, right):
    return lax.dot_general(left, right, (((0,), (0,)), ((), ())), preferred_element_type=F32)


def times_plain(left, right):
    return jnp.dot(left, right, preferred_element_type=F32)


def shape(dims, kind):
    return jax.ShapeDtypeStruct(dims, kind)


WHOLE = pl.BlockSpec(memory_space=pltpu.VMEM)
ANYWHERE = pl.BlockSpec(memory_space=pl.ANY)
OUTSIDE = pl.BlockSpec(memory_space=pltpu.HBM)


def run(kernel, outs, *operands, after=(), limit=16, flops=1, in_specs=None, **more):
    count = len(operands)

    def body(*refs):
        kernel(*refs[:count], *refs[count + len(after) :])

    return pl.pallas_call(
        body,
        out_shape=outs,
        in_specs=list(in_specs or [WHOLE] * count) + [ANYWHERE] * len(after),
        cost_estimate=pl.CostEstimate(flops=flops, bytes_accessed=1, transcendentals=0),
        compiler_params=pltpu.CompilerParams(vmem_limit_bytes=limit * MEGA),
        **more,
    )(*operands, *after)


def select_kernel(place_ref, select_ref, natural_ref):
    place = place_ref[0]
    core = place % 2
    chip = place // 2
    spot = [chip // SIDE**2, chip // SIDE % SIDE, chip % SIDE]

    def device_of(half, piece, first, second):
        owner = half * (1 - core) + (1 - half) * core
        x = (spot[0] + jnp.where(owner == 0, piece, first)) % SIDE
        y = (spot[1] + jnp.where(owner == 0, first, piece)) % SIDE
        z = (spot[2] + second) % SIDE
        return ((x * SIDE + y) * SIDE + z) * 2 + owner

    row = lax.broadcasted_iota(jnp.int32, (528, 1), 0)
    feature = row % HEAD
    high, low = feature // 32 % 4, feature // 8 % 4
    device = device_of(feature // 128, high, high, low)
    goal = jnp.where(row < 512, row // HEAD * HEAD + device % 32 * 8 + feature % 8, -2)
    column = lax.broadcasted_iota(jnp.int32, (1, 1024), 1)
    device = device_of(column // 512, column // 128 % 4, column // 32 % 4, column // 8 % 4)
    part = column % 8
    have = jnp.where(part < 4, device * 4 + part, -1)
    gain = jnp.where(row >= 512, row - 508, -1)
    select_ref[...] = jnp.where(
        (goal == have) | ((gain == part) & (part < 6)), 1.0, 0.0
    ).astype(BF)
    natural_ref[...] = jnp.where(
        goal[:HEAD] == lax.broadcasted_iota(jnp.int32, (1, HEAD), 1), 1.0, 0.0
    ).astype(BF)


def normalise(values, gain):
    inverse = lax.rsqrt(jnp.mean(values * values, axis=-1, keepdims=True) + EPSILON)
    return (values * inverse * gain).astype(BF)


def normalise_back(values, gain, grad):
    inverse = lax.rsqrt(jnp.mean(values * values, axis=-1, keepdims=True) + EPSILON)
    unit = values * inverse
    gain_grad = jnp.sum(grad * unit, axis=0, keepdims=True)
    scaled = grad * gain
    return inverse * (scaled - unit * jnp.mean(scaled * unit, axis=-1, keepdims=True)), gain_grad


def own_mask():
    row = lax.broadcasted_iota(jnp.int32, (HEADS * TILE, TILE), 0) % TILE
    column = lax.broadcasted_iota(jnp.int32, (HEADS * TILE, TILE), 1)
    return column <= row


def folded(wide, own):
    return jnp.concatenate(
        [jnp.where(own, wide[:, WIN:], wide[:, :TILE]), wide[:, TILE:WIN]], axis=1
    )


def unfolded(narrow, own):
    edge = narrow[:, :TILE]
    none = jnp.zeros_like(edge)
    return jnp.concatenate(
        [jnp.where(own, none, edge), narrow[:, TILE:], jnp.where(own, edge, none)], axis=1
    )


def payload_kernel(place_ref, *refs):
    sources, (payload_ref, *places, sems) = refs[:8], refs[8:]
    copies = [
        pltpu.make_async_copy(source, goal, sems.at[k])
        for k, (source, goal) in enumerate(zip(sources, places))
    ]
    for one in copies:
        one.start()
    for one in copies:
        one.wait()
    query_ref, out_ref, keyval_ref, gate_ref, up_ref, down_ref, gain_one_ref, gain_two_ref = places
    width = gain_one_ref.shape[1]
    row = lax.broadcasted_iota(jnp.int32, (8, query_ref.shape[1]), 0)
    lane = lax.broadcasted_iota(jnp.int32, (8, query_ref.shape[1]), 1) - place_ref[0] * width
    gains = jnp.zeros(row.shape, F32)
    for k, ref in ((4, gain_one_ref), (5, gain_two_ref)):
        values = ref[...].astype(F32)
        for i in range(width):
            gains = jnp.where((row == k) & (lane == i), values[:, i : i + 1], gains)
    keyval = jnp.concatenate([keyval_ref[...].astype(F32), gains[4:]], axis=0)
    payload_ref[0] = query_ref[...]
    payload_ref[1] = out_ref[...]
    payload_ref[2] = keyval.astype(BF)
    for k, ref in ((3, gate_ref), (5, up_ref), (7, down_ref)):
        payload_ref[k : k + 2] = ref[...].reshape(2, 8, -1)


def pack_kernel(r0, r1, r2, r3, goal_ref):
    groups, rows, width = r0.shape
    for k, ref in enumerate((r0, r1, r2, r3)):
        goal_ref[:, k] = ref[...]


def choose_kernel(place_ref, own_ref, hop_ref, goal_ref):
    edge = place_ref[0] % (2 * SIDE) == 2 * SIDE - 1

    @pl.when(edge)
    def _():
        goal_ref[...] = hop_ref[...]

    @pl.when(jnp.logical_not(edge))
    def _():
        goal_ref[...] = own_ref[...]


def pack_two_kernel(r0, r1, r2, r3, attn_ref, units_ref):
    for k, ref in enumerate((r0, r1, r2, r3)):
        attn_ref[:, k] = ref[:3]
        units_ref[:, k] = ref[3:]


def before_slots(narrow, own, start):
    edge = jnp.where(own, jnp.zeros_like(narrow[:, :TILE]), narrow[:, :TILE])
    return jnp.concatenate([edge, narrow[:, TILE : WIN - start]], axis=1) if start < WIN - TILE else edge


def own_slots(narrow, own, start):
    edge = jnp.where(own, narrow[:, :TILE], jnp.zeros_like(narrow[:, :TILE]))
    return jnp.concatenate([narrow[:, WIN - start :], edge], axis=1) if start > 0 else edge


def head_rows(half, owner):
    for head in range(HEADS):
        first = head * HEAD + half * 128
        if owner == 0:
            yield first, 128, head, pl.ds(0, 128)
        else:
            for piece in range(SIDE):
                yield first + piece * 32, 32, piece, pl.ds(head * 32, 32)


def forward_kernel(
    place_ref, tokens_ref, before_ref, select_ref, a0, a1, a2, a3, b0, b1, b2, b3,
    residual_ref, normed_two_ref, normed_ref, query_ref, keyval_ref, attended_ref, probs_ref,
    weight_query_ref, weight_out_ref, weight_keyval_ref, gains_ref,
):
    count = tokens_ref.shape[0]
    halves = ((a0, a1, a2, a3), (b0, b1, b2, b3))
    for half in range(2):
        for owner in range(2):

            @pl.when((place_ref[0] + half) % 2 == owner)
            def _():
                for first, rows, piece, there in head_rows(half, owner):
                    here = pl.ds(first, rows)
                    weight_query_ref[here, :] = halves[half][piece][0, there, :]
                    weight_out_ref[here, :] = halves[half][piece][1, there, :]

    mixed = jnp.concatenate([one[2] for half in halves for one in half], axis=0)
    sorted_rows = times_plain(select_ref[...], mixed)
    weight_keyval_ref[...] = sorted_rows[:512].astype(BF)
    gains_ref[...] = sorted_rows[512:520]
    gain_one = sorted_rows[512:513]
    gain_two = sorted_rows[513:514]
    inputs = tokens_ref[...].astype(F32)
    normed = normalise(inputs, gain_one)
    normed_ref[...] = normed
    normed_before = normalise(before_ref[...].astype(F32), gain_one)
    weight_keyval = weight_keyval_ref[...]
    keyval_ref[:WIN, :] = times_rows(normed_before, weight_keyval).astype(BF)
    keyval_ref[WIN:, :] = times_rows(normed, weight_keyval).astype(BF)
    for head in range(HEADS):
        query_ref[head] = times_rows(
            normed, weight_query_ref[pl.ds(head * HEAD, HEAD), :]
        ).astype(BF) * BF(SCALE)
    own = own_mask()
    first_key = jnp.where(place_ref[0] == 0, WIN, 0)

    def scores_of(tile):
        queries = query_ref[:, pl.ds(tile * TILE, TILE), :].reshape(HEADS * TILE, HEAD)
        return times_rows(queries, keyval_ref[pl.ds(tile * TILE, SPAN), :HEAD])

    ahead = scores_of(0)
    for tile in range(count // TILE):
        start = tile * TILE
        scores = folded(ahead, own)
        if start + TILE < count:
            ahead = scores_of(tile + 1)
        slot = start + lax.broadcasted_iota(jnp.int32, (1, WIN), 1)
        hidden = jnp.where(slot >= first_key, 0.0, MASKED)
        scores = jnp.concatenate(
            [scores[:, :TILE] + jnp.where(own, 0.0, hidden[:, :TILE]), scores[:, TILE:] + hidden[:, TILE:]],
            axis=1,
        )
        raised = jnp.exp(scores - jnp.max(scores, axis=1, keepdims=True))
        probs = (raised * (1.0 / jnp.sum(raised, axis=1, keepdims=True))).astype(BF)
        probs_ref[pl.ds(tile * HEADS * TILE, HEADS * TILE), :] = probs
        mixed = times_plain(unfolded(probs, own), keyval_ref[pl.ds(start, SPAN), HEAD:]).astype(BF)
        for head in range(HEADS):
            attended_ref[pl.ds(start, TILE), pl.ds(head * HEAD, HEAD)] = mixed[
                head * TILE : (head + 1) * TILE
            ]

    residual = inputs + times_plain(attended_ref[...], weight_out_ref[...])
    residual_ref[...] = residual
    normed_two_ref[...] = normalise(residual, gain_two)


GELU_A = math.sqrt(2.0 / math.pi)
GELU_B = 0.044715


def ffn_products(normed, grad, ref):
    return times_rows(normed, ref[0:4].reshape(512, -1)), times_rows(grad, ref[4:6].reshape(256, -1))


def ffn_units(both, hidden_grad):
    gate, up = both[:, :256], both[:, 256:]
    square = gate * gate
    bend = jnp.tanh(GELU_A * gate * (1.0 + GELU_B * square))
    half = 0.5 * (1.0 + bend)
    active = gate * half
    slope = half + 0.5 * gate * (1.0 - bend * bend) * (GELU_A + (3.0 * GELU_A * GELU_B) * square)
    both_grad = jnp.concatenate(
        [(hidden_grad * up * slope).astype(BF), (hidden_grad * active).astype(BF)], axis=1
    )
    return (active * up).astype(BF), both_grad


def ffn_sums(normed_ref, grad_ref, weights, both_grad_ref, hidden_ref, branch=None, normed_grad=None):
    normed = normed_ref[...]
    grad = grad_ref[...]
    ahead = ffn_products(normed, grad, weights[0])
    for k, ref in enumerate(weights):
        now = ahead
        if k + 1 < len(weights):
            ahead = ffn_products(normed, grad, weights[k + 1])
        hidden, both_grad = ffn_units(*now)
        hidden_ref[k] = hidden
        both_grad_ref[k] = both_grad
        branch_term = times_plain(hidden, ref[4:6].reshape(256, -1))
        normed_term = times_plain(both_grad, ref[0:4].reshape(512, -1))
        branch = branch_term if branch is None else branch + branch_term
        normed_grad = normed_term if normed_grad is None else normed_grad + normed_term
    return branch, normed_grad


def ffn_kernel(normed_ref, grad_ref, w0, w1, w2, branch_ref, normed_grad_ref, both_grad_ref, hidden_ref):
    branch_ref[...], normed_grad_ref[...] = ffn_sums(
        normed_ref, grad_ref, (w0, w1, w2), both_grad_ref, hidden_ref
    )


def ffn_last_kernel(
    normed_ref, grad_ref, normed_other_ref, grad_other_ref, w0, branch_in_ref, normed_grad_in_ref, branch_other_ref, normed_grad_other_ref,
    branch_ref, normed_grad_ref, both_grad_ref, hidden_ref, sums_ref, both_grad_other_ref, hidden_other_ref,
):
    branch, normed_grad = ffn_sums(
        normed_other_ref, grad_other_ref, (w0,), both_grad_other_ref, hidden_other_ref,
        branch_other_ref[...], normed_grad_other_ref[...],
    )
    sums_ref[0] = branch.astype(BF)
    sums_ref[1] = normed_grad.astype(BF)
    branch_ref[...], normed_grad_ref[...] = ffn_sums(
        normed_ref, grad_ref, (w0,), both_grad_ref, hidden_ref, branch_in_ref[...], normed_grad_in_ref[...]
    )


def ffn_terms_kernel(
    normed_ref, grad_ref, both_ref, hidden_ref, both_late_ref, hidden_late_ref,
    normed_other_ref, grad_other_ref, both_other_ref, hidden_other_ref, both_late_other_ref, hidden_late_other_ref,
    held_ref, right_ref, far_right_ref, far_left_ref, left_ref,
):
    for k, goal in ((2, None), (0, held_ref), (1, right_ref), (3, left_ref)):
        if k == 2:
            parts = (both_late_ref[0], hidden_late_ref[0], both_late_other_ref[0], hidden_late_other_ref[0])
        else:
            parts = [ref[min(k, 2)] for ref in (both_ref, hidden_ref, both_other_ref, hidden_other_ref)]
        both = times_cols(parts[0], normed_ref[...]) + times_cols(parts[2], normed_other_ref[...])
        down = times_cols(parts[1], grad_ref[...]) + times_cols(parts[3], grad_other_ref[...])
        both, down = both.reshape(4, 128, -1), down.reshape(2, 128, -1)
        if k == 2:
            far_right_ref[...] = both[:3].astype(BF)
            far_left_ref[0:1] = both[3:].astype(BF)
            far_left_ref[1:3] = down.astype(BF)
        else:
            goal[0:4] = both.astype(goal.dtype)
            goal[4:6] = down.astype(goal.dtype)


def relay_kernel(right_ref, left_ref, from_left_ref, from_right_ref, right_goal, left_goal):
    right_goal[0:3] = (right_ref[0:3].astype(F32) + from_left_ref[...].astype(F32)).astype(BF)
    right_goal[3:6] = right_ref[3:6]
    left_goal[0:3] = left_ref[0:3]
    left_goal[3:6] = (left_ref[3:6].astype(F32) + from_right_ref[...].astype(F32)).astype(BF)


def middle_kernel(
    residual_ref, branch_ref, normed_grad_ref, sums_ref, cotangent_ref, gains_ref, weight_out_ref, query_ref, keyval_ref, probs_ref,
    natural_ref, output_ref, residual_grad_ref, low_ref, rows_ref, score_grad_ref, sent_ref, gain_ref, window_ref,
):
    count = residual_ref.shape[0]
    residual = residual_ref[...]
    output_ref[...] = (residual + branch_ref[...] + sums_ref[0].astype(F32)).astype(BF)
    normed_grad = normed_grad_ref[...] + sums_ref[1].astype(F32)
    part, gain_grad = normalise_back(residual, gains_ref[1:2, :], normed_grad)
    gain_ref[...] = jnp.broadcast_to(gain_grad, gain_ref.shape)
    residual_grad = cotangent_ref[...].astype(F32) + part
    residual_grad_ref[...] = residual_grad
    low = residual_grad.astype(BF)
    low_ref[...] = low
    for head in range(HEADS):
        rows_ref[head] = times_rows(low, weight_out_ref[pl.ds(head * HEAD, HEAD), :]).astype(BF)
    own = own_mask()

    def rows_of(tile):
        return rows_ref[:, pl.ds(tile * TILE, TILE), :].reshape(HEADS * TILE, HEAD)

    def grads_of(tile):
        return times_rows(rows_of(tile), keyval_ref[pl.ds(tile * TILE, SPAN), HEAD:])

    ahead = grads_of(0)
    for tile in range(count // TILE):
        start = tile * TILE
        here = pl.ds(tile * HEADS * TILE, HEADS * TILE)
        queries = query_ref[:, pl.ds(start, TILE), :].reshape(HEADS * TILE, HEAD)
        rows = rows_of(tile)
        low_probs = probs_ref[here, :]
        probs = low_probs.astype(F32)
        prob_grad = folded(ahead, own)
        if start + TILE < count:
            ahead = grads_of(tile + 1)
        centre = jnp.sum(probs * prob_grad, axis=1, keepdims=True) / jnp.sum(
            probs, axis=1, keepdims=True
        )
        score_grad = (probs * (prob_grad - centre)).astype(BF)
        score_grad_ref[here, :] = score_grad
        earlier = pl.ds(start, WIN - start)
        key_term = times_cols(before_slots(score_grad, own, start), queries)
        value_term = times_cols(before_slots(low_probs, own, start), rows)
        if tile == 0:
            window_ref[earlier, :HEAD] = key_term
            window_ref[earlier, HEAD:] = value_term
        else:
            window_ref[earlier, :HEAD] += key_term
            window_ref[earlier, HEAD:] += value_term
    natural = natural_ref[...]
    sent_ref[:, :HEAD] = times_plain(window_ref[:, :HEAD].astype(BF), natural).astype(BF)
    sent_ref[:, HEAD:] = times_plain(window_ref[:, HEAD:].astype(BF), natural).astype(BF)


def own_kernel(rows_ref, score_grad_ref, query_ref, keyval_ref, probs_ref, query_grad_ref, own_ref):
    count = query_grad_ref.shape[0]
    own = own_mask()
    for tile in reversed(range(count // TILE)):
        start = tile * TILE
        span = pl.ds(start, SPAN)
        here = pl.ds(tile * HEADS * TILE, HEADS * TILE)
        queries = query_ref[:, pl.ds(start, TILE), :].reshape(HEADS * TILE, HEAD)
        rows = rows_ref[:, pl.ds(start, TILE), :].reshape(HEADS * TILE, HEAD)
        score_grad = score_grad_ref[here, :]
        mixed = (times_plain(unfolded(score_grad, own), keyval_ref[span, :HEAD]) * SCALE).astype(BF)
        for head in range(HEADS):
            query_grad_ref[pl.ds(start, TILE), pl.ds(head * HEAD, HEAD)] = mixed[
                head * TILE : (head + 1) * TILE
            ]
        mine = pl.ds(0, start + TILE)
        key_term = times_cols(own_slots(score_grad, own, start), queries)
        value_term = times_cols(own_slots(probs_ref[here, :], own, start), rows)
        if start + TILE == count:
            own_ref[mine, :HEAD] = key_term
            own_ref[mine, HEAD:] = value_term
        else:
            own_ref[mine, :HEAD] += key_term
            own_ref[mine, HEAD:] += value_term


def weights_kernel(
    place_ref, normed_ref, low_ref, attended_ref, query_grad_ref, weight_query_ref,
    normed_grad_ref, mine_ref, *other_refs,
):
    query_grad = query_grad_ref[...]
    normed_grad_ref[...] = times_plain(query_grad, weight_query_ref[...])
    for group, term in (
        (0, times_cols(query_grad, normed_ref[...]).astype(BF)),
        (1, times_cols(attended_ref[...], low_ref[...]).astype(BF)),
    ):
        for half in range(2):
            for owner in range(2):

                @pl.when((place_ref[0] + half) % 2 == owner)
                def _():
                    for first, rows, piece, there in head_rows(half, owner):
                        goal = mine_ref.at[piece, group]
                        if half == 1:
                            goal = other_refs[group].at[piece]
                        goal[there, :] = term[first : first + rows]


def last_kernel(
    tokens_ref, normed_ref, own_ref, came_ref, natural_ref, select_ref, weight_keyval_ref, gains_ref,
    partial_ref, residual_grad_ref, gain_two_ref,
    input_grad_ref, mine_ref, other_ref,
):
    natural = natural_ref[...]
    keyval = jnp.concatenate(
        [
            own_ref[:, :HEAD] + times_rows(came_ref[:, :HEAD], natural),
            own_ref[:, HEAD:] + times_rows(came_ref[:, HEAD:], natural),
        ],
        axis=1,
    ).astype(BF)
    grad = partial_ref[...] + times_plain(keyval, weight_keyval_ref[...])
    part, gain_grad = normalise_back(tokens_ref[...].astype(F32), gains_ref[0:1, :], grad)
    input_grad_ref[...] = residual_grad_ref[...] + part
    row = lax.broadcasted_iota(jnp.int32, (16, gain_grad.shape[1]), 0)
    gain_rows = jnp.where(
        row == 0, gain_grad, jnp.where(row == 1, gain_two_ref[0:1, :], 0.0)
    ).astype(BF)
    rows = jnp.concatenate([times_cols(keyval, normed_ref[...]).astype(BF), gain_rows], axis=0)
    mixed = times_cols(select_ref[...], rows).astype(BF)
    for piece in range(SIDE):
        mine_ref[piece] = mixed[piece * 128 : (piece + 1) * 128]
        other_ref[piece] = mixed[512 + piece * 128 : 512 + (piece + 1) * 128]


def meet_kernel(mine_ref, mine_keyval_ref, *refs):
    for last, goal in enumerate(refs[3:]):
        for k in range(3):
            mine = mine_ref[last, k] if k < 2 else mine_keyval_ref[last]
            goal[k] = (mine.astype(F32) + refs[k][last].astype(F32)).astype(goal.dtype)


def meet(mine, mine_keyval, came, after=()):
    _, rows, width = mine_keyval.shape
    return run(
        meet_kernel,
        [shape((3, rows, width), F32 if k == 0 else BF) for k in range(SIDE)],
        mine,
        mine_keyval,
        *came,
        after=after,
    )


def summed(refs):
    total = refs[0][...]
    for one in refs[1:]:
        total = total + one[...].astype(F32)
    return total


def middle_sum_kernel(*refs):
    total = summed(refs[:-SIDE])
    groups, rows, width = total.shape
    blocks = total.reshape(groups, SIDE, SIDE, 8, width)
    for k, goal in enumerate(refs[-SIDE:]):
        goal[...] = blocks[:, :, k].reshape(groups, 4 * 8, width).astype(goal.dtype)


def middle_sum(held, came, after=()):
    groups, rows, width = held.shape
    return run(
        middle_sum_kernel,
        [shape((groups, rows // SIDE, width), F32 if k == 0 else BF) for k in range(SIDE)],
        held, *came,
        after=after,
        grid=(groups // 3,),
        in_specs=[pl.BlockSpec((3, rows, width), lambda i: (i, 0, 0))] * (1 + len(came)),
        out_specs=[pl.BlockSpec((3, rows // SIDE, width), lambda i: (i, 0, 0))] * SIDE,
    )


def cut_kernel(*refs):
    total = summed(refs[:SIDE])
    rows = total.shape[1] // SIDE
    for k, goal in enumerate(refs[SIDE:]):
        goal[...] = total[:, k * rows : (k + 1) * rows].astype(goal.dtype)


def cut(pieces, came, after=()):
    groups, rows, width = pieces[0].shape
    outs = [shape((groups, rows // SIDE, width), F32 if k == 0 else BF) for k in range(SIDE)]
    return run(cut_kernel, outs, pieces[0], *came, after=after)


def end_kernel(
    place_ref, r0, r1, r2, r3, f0, f1, f2, f3, query_ref, keyval_ref, out_ref, gate_ref, up_ref, down_ref, one_ref, two_ref
):
    total = summed((r0, r1, r2, r3))
    units = summed((f0, f1, f2, f3))
    query_ref[...] = total[0]
    out_ref[...] = total[1]
    keyval_ref[...] = total[2, :4]
    for k, goal in ((0, gate_ref), (2, up_ref), (4, down_ref)):
        goal[...] = units[k : k + 2].reshape(goal.shape)
    width = one_ref.shape[0]
    full = total.shape[-1]
    rows = pltpu.roll(total[2], lax.rem(full - place_ref[0] * width, full), 1)
    one_ref[...] = rows[4, :width]
    two_ref[...] = rows[5, :width]


def local(tokens, gain_attn, gain_ffn, w_query, w_keyval, w_out, w_gate, w_up, w_down, cotangent):
    row_count, model_width = tokens.shape
    place = lax.axis_index(AXES)

    cotangent_other = to_sibling(cotangent)
    spot = place.reshape(1)
    scalar = pl.BlockSpec(memory_space=pltpu.SMEM)
    shards = (w_query, w_out, w_keyval, w_gate, w_up, w_down, gain_attn[None], gain_ffn[None])
    payload, = run(
        payload_kernel,
        [shape((9, 8, model_width), BF)],
        spot, *shards,
        in_specs=[scalar] + [OUTSIDE] * 8,
        limit=60,
        scratch_shapes=[pltpu.VMEM(one.shape, BF) for one in shards] + [pltpu.SemaphoreType.DMA((8,))],
    )
    hop = [((chip * SIDE + 3) * 2 + 1, (chip * SIDE + 7) * 2 + 1) for chip in range(SIDE**2 - 1)]
    ring = [(2 * chip, 2 * chip + 1) for chip in range(SIDE**3)]
    ring += [(2 * chip + 1, 2 * (chip // SIDE * SIDE + (chip + 1) % SIDE)) for chip in range(SIDE**3)]
    chosen, = run(
        choose_kernel,
        [shape(tokens.shape, BF)],
        place.reshape(1), tokens, lax.ppermute(tokens, AXES, hop),
        in_specs=[pl.BlockSpec(memory_space=pltpu.SMEM), WHOLE, WHOLE],
    )
    before = lax.ppermute(chosen, AXES, ring)
    select, natural = run(
        select_kernel,
        [shape((528, 1024), BF), shape((HEAD, HEAD), BF)],
        spot,
        in_specs=[scalar],
    )
    payload, = run(
        pack_kernel,
        [shape((9, SIDE, 8, model_width), BF)],
        *gather_stage(payload, 0),
        flops=4 * 10**9,
    )
    attn, units = run(
        pack_two_kernel,
        [shape((3, SIDE, SIDE, 8, model_width), BF), shape((6, SIDE, SIDE, 8, model_width), BF)],
        *gather_stage(payload, 1),
        after=(chosen, natural),
    )
    attn = gather_stage(attn.reshape(3, 128, model_width), 2)
    units = gather_stage(units.reshape(6, 128, model_width), 2)
    attn += [to_sibling(one) for one in attn]

    (
        residual, normed_two, normed, queries, keyvals, attended, probs, weight_query, weight_out, weight_keyval, gains
    ) = run(
        forward_kernel,
        (
            shape((row_count, model_width), F32),
            shape((row_count, model_width), BF),
            shape((row_count, model_width), BF),
            shape((HEADS, row_count, HEAD), BF),
            shape((2 * row_count, 2 * HEAD), BF),
            shape((row_count, HEADS * HEAD), BF),
            shape((HEADS * row_count, WIN), BF),
            shape((HEADS * HEAD, model_width), BF),
            shape((HEADS * HEAD, model_width), BF),
            shape((2 * HEAD, model_width), BF),
            shape((8, model_width), F32),
        ),
        spot, tokens, before, select, *attn,
        in_specs=[scalar] + [WHOLE] * 11,
    )

    normed_other = to_sibling(normed_two)
    def kept(count):
        return [shape((count, row_count, 512), BF), shape((count, row_count, 256), BF)]

    branch, normed_grad, both_grad, hidden = run(
        ffn_kernel,
        [shape((row_count, model_width), F32)] * 2 + kept(3),
        normed_two, cotangent, units[0], units[1], units[3],
        flops=10**10,
    )
    branch_other, normed_grad_other, both_grad_other, hidden_other = run(
        ffn_kernel,
        [shape((row_count, model_width), F32)] * 2 + kept(3),
        normed_other, cotangent_other, units[0], units[1], units[3],
        after=(normed_grad,),
    )
    branch, normed_grad, both_late, hidden_late, sums, both_late_other, hidden_late_other = run(
        ffn_last_kernel,
        [shape((row_count, model_width), F32)] * 2 + kept(1) + [shape((2, row_count, model_width), BF)] + kept(1),
        normed_two, cotangent, normed_other, cotangent_other, units[2], branch, normed_grad, branch_other, normed_grad_other,
    )
    sums = to_sibling(sums)
    full, part = (6, 128, model_width), (3, 128, model_width)
    held, right, far_right, far_left, left = run(
        ffn_terms_kernel,
        [shape(full, F32), shape(full, BF), shape(part, BF), shape(part, BF), shape(full, BF)],
        normed_two, cotangent, both_grad, hidden, both_late, hidden_late,
        normed_other, cotangent_other, both_grad_other, hidden_other, both_late_other, hidden_late_other,
    )
    from_left, from_right = sent(far_right, 2, 1), sent(far_left, 2, -1)

    output, residual_grad, low, rows, score_grad, keyval_sent, gain_two_grad = run(
        middle_kernel,
        (
            shape((row_count, model_width), BF),
            shape((row_count, model_width), F32),
            shape((row_count, model_width), BF),
            shape((HEADS, row_count, HEAD), BF),
            shape((HEADS * row_count, WIN), BF),
            shape((row_count, 2 * HEAD), BF),
            shape((8, model_width), F32),
        ),
        residual, branch, normed_grad, sums, cotangent, gains, weight_out, queries, keyvals, probs, natural,
        after=(far_left,),
        scratch_shapes=[pltpu.VMEM((row_count, 2 * HEAD), F32)],
    )
    came = shifted(keyval_sent, -1)
    query_grad, keyval_own = run(
        own_kernel,
        (shape((row_count, HEADS * HEAD), BF), shape((row_count, 2 * HEAD), F32)),
        rows, score_grad, queries, keyvals, probs,
    )
    right, left = run(
        relay_kernel, [shape(full, BF)] * 2, right, left, from_left, from_right, after=(low,)
    )
    ffn_back = [sent(right, 2, 1), sent(left, 2, -1)]
    partial, mine, *others = run(
        weights_kernel,
        (shape((row_count, model_width), F32), shape((SIDE, 2, 128, model_width), BF))
        + (shape((SIDE, 128, model_width), BF),) * 2,
        spot, normed, low, attended, query_grad, weight_query,
        after=(right,),
        in_specs=[scalar] + [WHOLE] * 5,
    )
    input_grad, mine_keyval, other_keyval = run(
        last_kernel,
        (shape((row_count, model_width), F32),) + (shape((SIDE, 128, model_width), BF),) * 2,
        tokens, normed, keyval_own, came, natural, select, weight_keyval, gains,
        partial, residual_grad, gain_two_grad,
        flops=2 * 10**9,
    )
    others.append(other_keyval)
    came = [to_sibling(one) for one in others]
    ffn_pieces = middle_sum(held, ffn_back, after=(mine_keyval,))
    ffn_back = scatter_stage(ffn_pieces, SCATTER[1])
    pieces = meet(mine, mine_keyval, came, after=(ffn_pieces[1],))
    pieces = cut(pieces, scatter_stage(pieces, SCATTER_ATTN[2]))
    back = scatter_stage(pieces, SCATTER_ATTN[1])
    ffn_pieces = cut(ffn_pieces, ffn_back, after=(pieces[1],))
    ffn_back = scatter_stage(ffn_pieces, SCATTER[0])
    pieces = cut(pieces, back, after=(ffn_pieces[1],))
    back = scatter_stage(pieces, SCATTER_ATTN[0])
    query, keyval, out, gate, up, down, gain_one, gain_two = run(
        end_kernel,
        [shape(one.shape, F32) for one in (w_query, w_keyval, w_out, w_gate, w_up, w_down, gain_attn, gain_ffn)],
        spot, pieces[0], *back, ffn_pieces[0], *ffn_back,
        in_specs=[scalar] + [WHOLE] * (2 * SIDE),
    )
    return output, input_grad, query, keyval, out, gate, up, down, gain_one, gain_two


def solution(mesh):
    rows, flat = P(AXES, None), P(AXES)
    return jax.shard_map(
        local,
        mesh=mesh,
        in_specs=(rows, flat, flat, rows, rows, rows, rows, rows, rows, rows),
        out_specs=(rows, rows, rows, rows, rows, rows, rows, rows, flat, flat),
        check_vma=False,
    )
```

```python
import math

import jax
import jax.numpy as jnp
from jax import lax
from jax.experimental import pallas as pl
from jax.experimental.pallas import tpu as pltpu
from jax.sharding import PartitionSpec as P

HEADS = 4
HEAD = 256
WIN = 512
SIDE = 4

EPSILON = 1e-06
MASKED = -1e30
AXES = ("ctx", "hd")
BF = jnp.bfloat16
F32 = jnp.float32

SCALE = 1.0 / math.sqrt(HEAD)
TILE = 128
SPAN = WIN + TILE
MEGA = 1 << 20

GATHER = ((2, 2), (1, 0), (0, 1))
SCATTER = ((1, 0), (2, 2), (0, 1))
SCATTER_ATTN = ((2, 2), (1, 0), (0, 1))


def chip_pairs(axis_of_core, steps):
    pairs = []
    for chip in range(SIDE**3):
        spot = [chip // SIDE**2, chip // SIDE % SIDE, chip % SIDE]
        for core in range(2):
            goal = list(spot)
            axis = axis_of_core[core]
            goal[axis] = (goal[axis] + steps) % SIDE
            target = (goal[0] * SIDE + goal[1]) * SIDE + goal[2]
            pairs.append((chip * 2 + core, target * 2 + core))
    return pairs


def to_sibling(value):
    return lax.ppermute(value, "hd", [(0, 1), (1, 0)])


def gather_stage(value, stage):
    return [value] + [
        lax.ppermute(value, AXES, chip_pairs(GATHER[stage], -steps)) for steps in range(1, SIDE)
    ]


def scatter_stage(pieces, axis_of_core):
    return [
        lax.ppermute(pieces[steps], AXES, chip_pairs(axis_of_core, steps))
        for steps in range(1, SIDE)
    ]


def sent(value, stage, steps):
    return lax.ppermute(value, AXES, chip_pairs(SCATTER[stage], steps))


def shifted(value, steps):
    count = lax.axis_size(AXES)
    initial, last = (max(0, -steps), min(count, count - steps))
    return lax.ppermute(value, AXES, [(source, source + steps) for source in range(initial, last)])


def times_rows(left, right):
    return lax.dot_general(left, right, (((1,), (1,)), ((), ())), preferred_element_type=F32)


def times_cols(left, right):
    return lax.dot_general(left, right, (((0,), (0,)), ((), ())), preferred_element_type=F32)


def times_plain(left, right):
    return jnp.dot(left, right, preferred_element_type=F32)


def shape(dims, kind):
    return jax.ShapeDtypeStruct(dims, kind)


WHOLE = pl.BlockSpec(memory_space=pltpu.VMEM)
ANYWHERE = pl.BlockSpec(memory_space=pl.ANY)
OUTSIDE = pl.BlockSpec(memory_space=pltpu.HBM)


def run(kernel, outs, *operands, after=(), limit=16, flops=1, in_specs=None, **more):
    count = len(operands)

    def body(*refs):
        kernel(*refs[:count], *refs[count + len(after) :])

    return pl.pallas_call(
        body,
        out_shape=outs,
        in_specs=list(in_specs or [WHOLE] * count) + [ANYWHERE] * len(after),
        cost_estimate=pl.CostEstimate(flops=flops, bytes_accessed=1, transcendentals=0),
        compiler_params=pltpu.CompilerParams(vmem_limit_bytes=limit * MEGA),
        **more,
    )(*operands, *after)


def select_kernel(place_ref, select_ref, natural_ref):
    place = place_ref[0]
    core = place % 2
    chip = place // 2
    spot = [chip // SIDE**2, chip // SIDE % SIDE, chip % SIDE]

    def device_of(half, piece, first, second):
        owner = half * (1 - core) + (1 - half) * core
        x = (spot[0] + jnp.where(owner == 0, piece, first)) % SIDE
        y = (spot[1] + jnp.where(owner == 0, first, piece)) % SIDE
        z = (spot[2] + second) % SIDE
        return ((x * SIDE + y) * SIDE + z) * 2 + owner

    row = lax.broadcasted_iota(jnp.int32, (528, 1), 0)
    feature = row % HEAD
    high, low = feature // 32 % 4, feature // 8 % 4
    device = device_of(feature // 128, high, high, low)
    goal = jnp.where(row < 512, row // HEAD * HEAD + device % 32 * 8 + feature % 8, -2)
    column = lax.broadcasted_iota(jnp.int32, (1, 1024), 1)
    device = device_of(column // 512, column // 128 % 4, column // 32 % 4, column // 8 % 4)
    part = column % 8
    have = jnp.where(part < 4, device * 4 + part, -1)
    gain = jnp.where(row >= 512, row - 508, -1)
    select_ref[...] = jnp.where(
        (goal == have) | ((gain == part) & (part < 6)), 1.0, 0.0
    ).astype(BF)
    natural_ref[...] = jnp.where(
        goal[:HEAD] == lax.broadcasted_iota(jnp.int32, (1, HEAD), 1), 1.0, 0.0
    ).astype(BF)


def normalise(values, gain):
    inverse = lax.rsqrt(jnp.mean(values * values, axis=-1, keepdims=True) + EPSILON)
    return (values * inverse * gain).astype(BF)


def normalise_back(values, gain, grad):
    inverse = lax.rsqrt(jnp.mean(values * values, axis=-1, keepdims=True) + EPSILON)
    unit = values * inverse
    gain_grad = jnp.sum(grad * unit, axis=0, keepdims=True)
    scaled = grad * gain
    return inverse * (scaled - unit * jnp.mean(scaled * unit, axis=-1, keepdims=True)), gain_grad


def own_mask():
    row = lax.broadcasted_iota(jnp.int32, (HEADS * TILE, TILE), 0) % TILE
    column = lax.broadcasted_iota(jnp.int32, (HEADS * TILE, TILE), 1)
    return column <= row


def folded(wide, own):
    return jnp.concatenate(
        [jnp.where(own, wide[:, WIN:], wide[:, :TILE]), wide[:, TILE:WIN]], axis=1
    )


def unfolded(narrow, own):
    edge = narrow[:, :TILE]
    none = jnp.zeros_like(edge)
    return jnp.concatenate(
        [jnp.where(own, none, edge), narrow[:, TILE:], jnp.where(own, edge, none)], axis=1
    )


def payload_kernel(place_ref, *refs):
    sources, (payload_ref, *places, sems) = refs[:8], refs[8:]
    copies = [
        pltpu.make_async_copy(source, goal, sems.at[k])
        for k, (source, goal) in enumerate(zip(sources, places))
    ]
    for one in copies:
        one.start()
    for one in copies:
        one.wait()
    query_ref, out_ref, keyval_ref, gate_ref, up_ref, down_ref, gain_one_ref, gain_two_ref = places
    width = gain_one_ref.shape[1]
    row = lax.broadcasted_iota(jnp.int32, (8, query_ref.shape[1]), 0)
    lane = lax.broadcasted_iota(jnp.int32, (8, query_ref.shape[1]), 1) - place_ref[0] * width
    gains = jnp.zeros(row.shape, F32)
    for k, ref in ((4, gain_one_ref), (5, gain_two_ref)):
        values = ref[...].astype(F32)
        for i in range(width):
            gains = jnp.where((row == k) & (lane == i), values[:, i : i + 1], gains)
    keyval = jnp.concatenate([keyval_ref[...].astype(F32), gains[4:]], axis=0)
    payload_ref[0] = query_ref[...]
    payload_ref[1] = out_ref[...]
    payload_ref[2] = keyval.astype(BF)
    for k, ref in ((3, gate_ref), (5, up_ref), (7, down_ref)):
        payload_ref[k : k + 2] = ref[...].reshape(2, 8, -1)


def pack_kernel(r0, r1, r2, r3, goal_ref):
    groups, rows, width = r0.shape
    for k, ref in enumerate((r0, r1, r2, r3)):
        goal_ref[:, k] = ref[...]


def choose_kernel(place_ref, own_ref, hop_ref, goal_ref):
    edge = place_ref[0] % (2 * SIDE) == 2 * SIDE - 1

    @pl.when(edge)
    def _():
        goal_ref[...] = hop_ref[...]

    @pl.when(jnp.logical_not(edge))
    def _():
        goal_ref[...] = own_ref[...]


def pack_two_kernel(r0, r1, r2, r3, attn_ref, units_ref):
    for k, ref in enumerate((r0, r1, r2, r3)):
        attn_ref[:, k] = ref[:3]
        units_ref[:, k] = ref[3:]


def before_slots(narrow, own, start):
    edge = jnp.where(own, jnp.zeros_like(narrow[:, :TILE]), narrow[:, :TILE])
    return jnp.concatenate([edge, narrow[:, TILE : WIN - start]], axis=1) if start < WIN - TILE else edge


def own_slots(narrow, own, start):
    edge = jnp.where(own, narrow[:, :TILE], jnp.zeros_like(narrow[:, :TILE]))
    return jnp.concatenate([narrow[:, WIN - start :], edge], axis=1) if start > 0 else edge


def head_rows(half, owner):
    for head in range(HEADS):
        first = head * HEAD + half * 128
        if owner == 0:
            yield first, 128, head, pl.ds(0, 128)
        else:
            for piece in range(SIDE):
                yield first + piece * 32, 32, piece, pl.ds(head * 32, 32)


def forward_kernel(
    place_ref, tokens_ref, before_ref, select_ref, a0, a1, a2, a3, b0, b1, b2, b3,
    residual_ref, normed_two_ref, normed_ref, query_ref, keyval_ref, attended_ref, probs_ref,
    weight_query_ref, weight_out_ref, weight_keyval_ref, gains_ref,
):
    count = tokens_ref.shape[0]
    halves = ((a0, a1, a2, a3), (b0, b1, b2, b3))
    for half in range(2):
        for owner in range(2):

            @pl.when((place_ref[0] + half) % 2 == owner)
            def _():
                for first, rows, piece, there in head_rows(half, owner):
                    here = pl.ds(first, rows)
                    weight_query_ref[here, :] = halves[half][piece][0, there, :]
                    weight_out_ref[here, :] = halves[half][piece][1, there, :]

    mixed = jnp.concatenate([one[2] for half in halves for one in half], axis=0)
    sorted_rows = times_plain(select_ref[...], mixed)
    weight_keyval_ref[...] = sorted_rows[:512].astype(BF)
    gains_ref[...] = sorted_rows[512:520]
    gain_one = sorted_rows[512:513]
    gain_two = sorted_rows[513:514]
    inputs = tokens_ref[...].astype(F32)
    normed = normalise(inputs, gain_one)
    normed_ref[...] = normed
    normed_before = normalise(before_ref[...].astype(F32), gain_one)
    weight_keyval = weight_keyval_ref[...]
    keyval_ref[:WIN, :] = times_rows(normed_before, weight_keyval).astype(BF)
    keyval_ref[WIN:, :] = times_rows(normed, weight_keyval).astype(BF)
    for head in range(HEADS):
        query_ref[head] = times_rows(
            normed, weight_query_ref[pl.ds(head * HEAD, HEAD), :]
        ).astype(BF) * BF(SCALE)
    own = own_mask()
    first_key = jnp.where(place_ref[0] == 0, WIN, 0)

    def scores_of(tile):
        queries = query_ref[:, pl.ds(tile * TILE, TILE), :].reshape(HEADS * TILE, HEAD)
        return times_rows(queries, keyval_ref[pl.ds(tile * TILE, SPAN), :HEAD])

    ahead = scores_of(0)
    for tile in range(count // TILE):
        start = tile * TILE
        scores = folded(ahead, own)
        if start + TILE < count:
            ahead = scores_of(tile + 1)
        slot = start + lax.broadcasted_iota(jnp.int32, (1, WIN), 1)
        hidden = jnp.where(slot >= first_key, 0.0, MASKED)
        scores = jnp.concatenate(
            [scores[:, :TILE] + jnp.where(own, 0.0, hidden[:, :TILE]), scores[:, TILE:] + hidden[:, TILE:]],
            axis=1,
        )
        raised = jnp.exp(scores - jnp.max(scores, axis=1, keepdims=True))
        probs = (raised * (1.0 / jnp.sum(raised, axis=1, keepdims=True))).astype(BF)
        probs_ref[pl.ds(tile * HEADS * TILE, HEADS * TILE), :] = probs
        mixed = times_plain(unfolded(probs, own), keyval_ref[pl.ds(start, SPAN), HEAD:]).astype(BF)
        for head in range(HEADS):
            attended_ref[pl.ds(start, TILE), pl.ds(head * HEAD, HEAD)] = mixed[
                head * TILE : (head + 1) * TILE
            ]

    residual = inputs + times_plain(attended_ref[...], weight_out_ref[...])
    residual_ref[...] = residual
    normed_two_ref[...] = normalise(residual, gain_two)


GELU_A = math.sqrt(2.0 / math.pi)
GELU_B = 0.044715


def ffn_products(normed, grad, ref):
    return times_rows(normed, ref[0:4].reshape(512, -1)), times_rows(grad, ref[4:6].reshape(256, -1))


def ffn_units(both, hidden_grad):
    gate, up = both[:, :256], both[:, 256:]
    square = gate * gate
    bend = jnp.tanh(GELU_A * gate * (1.0 + GELU_B * square))
    half = 0.5 * (1.0 + bend)
    active = gate * half
    slope = half + 0.5 * gate * (1.0 - bend * bend) * (GELU_A + (3.0 * GELU_A * GELU_B) * square)
    both_grad = jnp.concatenate(
        [(hidden_grad * up * slope).astype(BF), (hidden_grad * active).astype(BF)], axis=1
    )
    return (active * up).astype(BF), both_grad


def ffn_sums(normed_ref, grad_ref, weights, both_grad_ref, hidden_ref, branch=None, normed_grad=None):
    normed = normed_ref[...]
    grad = grad_ref[...]
    ahead = ffn_products(normed, grad, weights[0])
    for k, ref in enumerate(weights):
        now = ahead
        if k + 1 < len(weights):
            ahead = ffn_products(normed, grad, weights[k + 1])
        hidden, both_grad = ffn_units(*now)
        hidden_ref[k] = hidden
        both_grad_ref[k] = both_grad
        branch_term = times_plain(hidden, ref[4:6].reshape(256, -1))
        normed_term = times_plain(both_grad, ref[0:4].reshape(512, -1))
        branch = branch_term if branch is None else branch + branch_term
        normed_grad = normed_term if normed_grad is None else normed_grad + normed_term
    return branch, normed_grad


def ffn_kernel(normed_ref, grad_ref, w0, w1, w2, branch_ref, normed_grad_ref, both_grad_ref, hidden_ref):
    branch_ref[...], normed_grad_ref[...] = ffn_sums(
        normed_ref, grad_ref, (w0, w1, w2), both_grad_ref, hidden_ref
    )


def ffn_last_kernel(
    normed_ref, grad_ref, normed_other_ref, grad_other_ref, w0, branch_in_ref, normed_grad_in_ref, branch_other_ref, normed_grad_other_ref,
    branch_ref, normed_grad_ref, both_grad_ref, hidden_ref, sums_ref, both_grad_other_ref, hidden_other_ref,
):
    branch, normed_grad = ffn_sums(
        normed_other_ref, grad_other_ref, (w0,), both_grad_other_ref, hidden_other_ref,
        branch_other_ref[...], normed_grad_other_ref[...],
    )
    sums_ref[0] = branch.astype(BF)
    sums_ref[1] = normed_grad.astype(BF)
    branch_ref[...], normed_grad_ref[...] = ffn_sums(
        normed_ref, grad_ref, (w0,), both_grad_ref, hidden_ref, branch_in_ref[...], normed_grad_in_ref[...]
    )


def ffn_terms_kernel(
    normed_ref, grad_ref, both_ref, hidden_ref, both_late_ref, hidden_late_ref,
    normed_other_ref, grad_other_ref, both_other_ref, hidden_other_ref, both_late_other_ref, hidden_late_other_ref,
    held_ref, right_ref, far_right_ref, far_left_ref, left_ref,
):
    for k, goal in ((2, None), (0, held_ref), (1, right_ref), (3, left_ref)):
        if k == 2:
            parts = (both_late_ref[0], hidden_late_ref[0], both_late_other_ref[0], hidden_late_other_ref[0])
        else:
            parts = [ref[min(k, 2)] for ref in (both_ref, hidden_ref, both_other_ref, hidden_other_ref)]
        both = times_cols(parts[0], normed_ref[...]) + times_cols(parts[2], normed_other_ref[...])
        down = times_cols(parts[1], grad_ref[...]) + times_cols(parts[3], grad_other_ref[...])
        both, down = both.reshape(4, 128, -1), down.reshape(2, 128, -1)
        if k == 2:
            far_right_ref[...] = both[:3].astype(BF)
            far_left_ref[0:1] = both[3:].astype(BF)
            far_left_ref[1:3] = down.astype(BF)
        else:
            goal[0:4] = both.astype(goal.dtype)
            goal[4:6] = down.astype(goal.dtype)


def relay_kernel(right_ref, left_ref, from_left_ref, from_right_ref, right_goal, left_goal):
    right_goal[0:3] = (right_ref[0:3].astype(F32) + from_left_ref[...].astype(F32)).astype(BF)
    right_goal[3:6] = right_ref[3:6]
    left_goal[0:3] = left_ref[0:3]
    left_goal[3:6] = (left_ref[3:6].astype(F32) + from_right_ref[...].astype(F32)).astype(BF)


def middle_kernel(
    residual_ref, branch_ref, normed_grad_ref, sums_ref, cotangent_ref, gains_ref, weight_out_ref, query_ref, keyval_ref, probs_ref,
    natural_ref, output_ref, residual_grad_ref, low_ref, rows_ref, score_grad_ref, sent_ref, gain_ref, window_ref,
):
    count = residual_ref.shape[0]
    residual = residual_ref[...]
    output_ref[...] = (residual + branch_ref[...] + sums_ref[0].astype(F32)).astype(BF)
    normed_grad = normed_grad_ref[...] + sums_ref[1].astype(F32)
    part, gain_grad = normalise_back(residual, gains_ref[1:2, :], normed_grad)
    gain_ref[...] = jnp.broadcast_to(gain_grad, gain_ref.shape)
    residual_grad = cotangent_ref[...].astype(F32) + part
    residual_grad_ref[...] = residual_grad
    low = residual_grad.astype(BF)
    low_ref[...] = low
    for head in range(HEADS):
        rows_ref[head] = times_rows(low, weight_out_ref[pl.ds(head * HEAD, HEAD), :]).astype(BF)
    own = own_mask()

    def rows_of(tile):
        return rows_ref[:, pl.ds(tile * TILE, TILE), :].reshape(HEADS * TILE, HEAD)

    def grads_of(tile):
        return times_rows(rows_of(tile), keyval_ref[pl.ds(tile * TILE, SPAN), HEAD:])

    ahead = grads_of(0)
    for tile in range(count // TILE):
        start = tile * TILE
        here = pl.ds(tile * HEADS * TILE, HEADS * TILE)
        queries = query_ref[:, pl.ds(start, TILE), :].reshape(HEADS * TILE, HEAD)
        rows = rows_of(tile)
        low_probs = probs_ref[here, :]
        probs = low_probs.astype(F32)
        prob_grad = folded(ahead, own)
        if start + TILE < count:
            ahead = grads_of(tile + 1)
        centre = jnp.sum(probs * prob_grad, axis=1, keepdims=True) / jnp.sum(
            probs, axis=1, keepdims=True
        )
        score_grad = (probs * (prob_grad - centre)).astype(BF)
        score_grad_ref[here, :] = score_grad
        earlier = pl.ds(start, WIN - start)
        key_term = times_cols(before_slots(score_grad, own, start), queries)
        value_term = times_cols(before_slots(low_probs, own, start), rows)
        if tile == 0:
            window_ref[earlier, :HEAD] = key_term
            window_ref[earlier, HEAD:] = value_term
        else:
            window_ref[earlier, :HEAD] += key_term
            window_ref[earlier, HEAD:] += value_term
    natural = natural_ref[...]
    sent_ref[:, :HEAD] = times_plain(window_ref[:, :HEAD].astype(BF), natural).astype(BF)
    sent_ref[:, HEAD:] = times_plain(window_ref[:, HEAD:].astype(BF), natural).astype(BF)


def own_kernel(rows_ref, score_grad_ref, query_ref, keyval_ref, probs_ref, query_grad_ref, own_ref):
    count = query_grad_ref.shape[0]
    own = own_mask()
    for tile in reversed(range(count // TILE)):
        start = tile * TILE
        span = pl.ds(start, SPAN)
        here = pl.ds(tile * HEADS * TILE, HEADS * TILE)
        queries = query_ref[:, pl.ds(start, TILE), :].reshape(HEADS * TILE, HEAD)
        rows = rows_ref[:, pl.ds(start, TILE), :].reshape(HEADS * TILE, HEAD)
        score_grad = score_grad_ref[here, :]
        mixed = (times_plain(unfolded(score_grad, own), keyval_ref[span, :HEAD]) * SCALE).astype(BF)
        for head in range(HEADS):
            query_grad_ref[pl.ds(start, TILE), pl.ds(head * HEAD, HEAD)] = mixed[
                head * TILE : (head + 1) * TILE
            ]
        mine = pl.ds(0, start + TILE)
        key_term = times_cols(own_slots(score_grad, own, start), queries)
        value_term = times_cols(own_slots(probs_ref[here, :], own, start), rows)
        if start + TILE == count:
            own_ref[mine, :HEAD] = key_term
            own_ref[mine, HEAD:] = value_term
        else:
            own_ref[mine, :HEAD] += key_term
            own_ref[mine, HEAD:] += value_term


def weights_kernel(
    place_ref, normed_ref, low_ref, attended_ref, query_grad_ref, weight_query_ref,
    normed_grad_ref, mine_ref, *other_refs,
):
    query_grad = query_grad_ref[...]
    normed_grad_ref[...] = times_plain(query_grad, weight_query_ref[...])
    for group, term in (
        (0, times_cols(query_grad, normed_ref[...]).astype(BF)),
        (1, times_cols(attended_ref[...], low_ref[...]).astype(BF)),
    ):
        for half in range(2):
            for owner in range(2):

                @pl.when((place_ref[0] + half) % 2 == owner)
                def _():
                    for first, rows, piece, there in head_rows(half, owner):
                        goal = mine_ref.at[piece, group]
                        if half == 1:
                            goal = other_refs[group].at[piece]
                        goal[there, :] = term[first : first + rows]


def last_kernel(
    tokens_ref, normed_ref, own_ref, came_ref, natural_ref, select_ref, weight_keyval_ref, gains_ref,
    partial_ref, residual_grad_ref, gain_two_ref,
    input_grad_ref, mine_ref, other_ref,
):
    natural = natural_ref[...]
    keyval = jnp.concatenate(
        [
            own_ref[:, :HEAD] + times_rows(came_ref[:, :HEAD], natural),
            own_ref[:, HEAD:] + times_rows(came_ref[:, HEAD:], natural),
        ],
        axis=1,
    ).astype(BF)
    grad = partial_ref[...] + times_plain(keyval, weight_keyval_ref[...])
    part, gain_grad = normalise_back(tokens_ref[...].astype(F32), gains_ref[0:1, :], grad)
    input_grad_ref[...] = residual_grad_ref[...] + part
    row = lax.broadcasted_iota(jnp.int32, (16, gain_grad.shape[1]), 0)
    gain_rows = jnp.where(
        row == 0, gain_grad, jnp.where(row == 1, gain_two_ref[0:1, :], 0.0)
    ).astype(BF)
    rows = jnp.concatenate([times_cols(keyval, normed_ref[...]).astype(BF), gain_rows], axis=0)
    mixed = times_cols(select_ref[...], rows).astype(BF)
    for piece in range(SIDE):
        mine_ref[piece] = mixed[piece * 128 : (piece + 1) * 128]
        other_ref[piece] = mixed[512 + piece * 128 : 512 + (piece + 1) * 128]


def meet_kernel(mine_ref, mine_keyval_ref, *refs):
    for last, goal in enumerate(refs[3:]):
        for k in range(3):
            mine = mine_ref[last, k] if k < 2 else mine_keyval_ref[last]
            goal[k] = (mine.astype(F32) + refs[k][last].astype(F32)).astype(goal.dtype)


def meet(mine, mine_keyval, came, after=()):
    _, rows, width = mine_keyval.shape
    return run(
        meet_kernel,
        [shape((3, rows, width), F32 if k == 0 else BF) for k in range(SIDE)],
        mine,
        mine_keyval,
        *came,
        after=after,
    )


def summed(refs):
    total = refs[0][...]
    for one in refs[1:]:
        total = total + one[...].astype(F32)
    return total


def middle_sum_kernel(held_ref, came_right_ref, came_left_ref, held_goal, right_goal, far_right_goal, far_left_goal, left_goal):
    total = summed((held_ref, came_right_ref, came_left_ref))
    groups, rows, width = total.shape
    blocks = total.reshape(groups, SIDE, SIDE, 8, width)

    def block(k):
        return blocks[:, :, k].reshape(groups, 4 * 8, width)

    held_goal[...] = block(0)
    right_goal[...] = block(1).astype(BF)
    far_right_goal[...] = block(2)[:3].astype(BF)
    far_left_goal[...] = block(2)[3:].astype(BF)
    left_goal[...] = block(3).astype(BF)


def cut_kernel(*refs):
    total = summed(refs[:-SIDE])
    rows = total.shape[1] // SIDE
    for k, goal in enumerate(refs[-SIDE:]):
        goal[...] = total[:, k * rows : (k + 1) * rows].astype(goal.dtype)


def cut(pieces, came, after=()):
    groups, rows, width = pieces[0].shape
    outs = [shape((groups, rows // SIDE, width), F32 if k == 0 else BF) for k in range(SIDE)]
    return run(cut_kernel, outs, pieces[0], *came, after=after)


def end_kernel(
    place_ref, r0, r1, r2, r3, f0, f1, f2, f3, query_ref, keyval_ref, out_ref, gate_ref, up_ref, down_ref, one_ref, two_ref
):
    total = summed((r0, r1, r2, r3))
    units = summed((f0, f1, f2, f3))
    query_ref[...] = total[0]
    out_ref[...] = total[1]
    keyval_ref[...] = total[2, :4]
    for k, goal in ((0, gate_ref), (2, up_ref), (4, down_ref)):
        goal[...] = units[k : k + 2].reshape(goal.shape)
    width = one_ref.shape[0]
    full = total.shape[-1]
    rows = pltpu.roll(total[2], lax.rem(full - place_ref[0] * width, full), 1)
    one_ref[...] = rows[4, :width]
    two_ref[...] = rows[5, :width]


def local(tokens, gain_attn, gain_ffn, w_query, w_keyval, w_out, w_gate, w_up, w_down, cotangent):
    row_count, model_width = tokens.shape
    place = lax.axis_index(AXES)

    cotangent_other = to_sibling(cotangent)
    spot = place.reshape(1)
    scalar = pl.BlockSpec(memory_space=pltpu.SMEM)
    shards = (w_query, w_out, w_keyval, w_gate, w_up, w_down, gain_attn[None], gain_ffn[None])
    payload, = run(
        payload_kernel,
        [shape((9, 8, model_width), BF)],
        spot, *shards,
        in_specs=[scalar] + [OUTSIDE] * 8,
        limit=60,
        scratch_shapes=[pltpu.VMEM(one.shape, BF) for one in shards] + [pltpu.SemaphoreType.DMA((8,))],
    )
    hop = [((chip * SIDE + 3) * 2 + 1, (chip * SIDE + 7) * 2 + 1) for chip in range(SIDE**2 - 1)]
    ring = [(2 * chip, 2 * chip + 1) for chip in range(SIDE**3)]
    ring += [(2 * chip + 1, 2 * (chip // SIDE * SIDE + (chip + 1) % SIDE)) for chip in range(SIDE**3)]
    chosen, = run(
        choose_kernel,
        [shape(tokens.shape, BF)],
        place.reshape(1), tokens, lax.ppermute(tokens, AXES, hop),
        in_specs=[pl.BlockSpec(memory_space=pltpu.SMEM), WHOLE, WHOLE],
    )
    before = lax.ppermute(chosen, AXES, ring)
    select, natural = run(
        select_kernel,
        [shape((528, 1024), BF), shape((HEAD, HEAD), BF)],
        spot,
        in_specs=[scalar],
    )
    payload, = run(
        pack_kernel,
        [shape((9, SIDE, 8, model_width), BF)],
        *gather_stage(payload, 0),
        flops=4 * 10**9,
    )
    attn, units = run(
        pack_two_kernel,
        [shape((3, SIDE, SIDE, 8, model_width), BF), shape((6, SIDE, SIDE, 8, model_width), BF)],
        *gather_stage(payload, 1),
        after=(chosen, natural),
    )
    attn = gather_stage(attn.reshape(3, 128, model_width), 2)
    units = gather_stage(units.reshape(6, 128, model_width), 2)
    attn += [to_sibling(one) for one in attn]

    (
        residual, normed_two, normed, queries, keyvals, attended, probs, weight_query, weight_out, weight_keyval, gains
    ) = run(
        forward_kernel,
        (
            shape((row_count, model_width), F32),
            shape((row_count, model_width), BF),
            shape((row_count, model_width), BF),
            shape((HEADS, row_count, HEAD), BF),
            shape((2 * row_count, 2 * HEAD), BF),
            shape((row_count, HEADS * HEAD), BF),
            shape((HEADS * row_count, WIN), BF),
            shape((HEADS * HEAD, model_width), BF),
            shape((HEADS * HEAD, model_width), BF),
            shape((2 * HEAD, model_width), BF),
            shape((8, model_width), F32),
        ),
        spot, tokens, before, select, *attn,
        in_specs=[scalar] + [WHOLE] * 11,
    )

    normed_other = to_sibling(normed_two)
    def kept(count):
        return [shape((count, row_count, 512), BF), shape((count, row_count, 256), BF)]

    branch, normed_grad, both_grad, hidden = run(
        ffn_kernel,
        [shape((row_count, model_width), F32)] * 2 + kept(3),
        normed_two, cotangent, units[0], units[1], units[3],
        flops=10**10,
    )
    branch_other, normed_grad_other, both_grad_other, hidden_other = run(
        ffn_kernel,
        [shape((row_count, model_width), F32)] * 2 + kept(3),
        normed_other, cotangent_other, units[0], units[1], units[3],
        after=(normed_grad,),
    )
    branch, normed_grad, both_late, hidden_late, sums, both_late_other, hidden_late_other = run(
        ffn_last_kernel,
        [shape((row_count, model_width), F32)] * 2 + kept(1) + [shape((2, row_count, model_width), BF)] + kept(1),
        normed_two, cotangent, normed_other, cotangent_other, units[2], branch, normed_grad, branch_other, normed_grad_other,
    )
    sums = to_sibling(sums)
    full, part = (6, 128, model_width), (3, 128, model_width)
    held, right, far_right, far_left, left = run(
        ffn_terms_kernel,
        [shape(full, F32), shape(full, BF), shape(part, BF), shape(part, BF), shape(full, BF)],
        normed_two, cotangent, both_grad, hidden, both_late, hidden_late,
        normed_other, cotangent_other, both_grad_other, hidden_other, both_late_other, hidden_late_other,
    )
    from_left, from_right = sent(far_right, 2, 1), sent(far_left, 2, -1)

    output, residual_grad, low, rows, score_grad, keyval_sent, gain_two_grad = run(
        middle_kernel,
        (
            shape((row_count, model_width), BF),
            shape((row_count, model_width), F32),
            shape((row_count, model_width), BF),
            shape((HEADS, row_count, HEAD), BF),
            shape((HEADS * row_count, WIN), BF),
            shape((row_count, 2 * HEAD), BF),
            shape((8, model_width), F32),
        ),
        residual, branch, normed_grad, sums, cotangent, gains, weight_out, queries, keyvals, probs, natural,
        after=(far_left,),
        scratch_shapes=[pltpu.VMEM((row_count, 2 * HEAD), F32)],
    )
    came = shifted(keyval_sent, -1)
    query_grad, keyval_own = run(
        own_kernel,
        (shape((row_count, HEADS * HEAD), BF), shape((row_count, 2 * HEAD), F32)),
        rows, score_grad, queries, keyvals, probs,
    )
    right, left = run(
        relay_kernel, [shape(full, BF)] * 2, right, left, from_left, from_right, after=(low,)
    )
    ffn_back = [sent(right, 2, 1), sent(left, 2, -1)]
    partial, mine, *others = run(
        weights_kernel,
        (shape((row_count, model_width), F32), shape((SIDE, 2, 128, model_width), BF))
        + (shape((SIDE, 128, model_width), BF),) * 2,
        spot, normed, low, attended, query_grad, weight_query,
        after=(right,),
        in_specs=[scalar] + [WHOLE] * 5,
    )
    input_grad, mine_keyval, other_keyval = run(
        last_kernel,
        (shape((row_count, model_width), F32),) + (shape((SIDE, 128, model_width), BF),) * 2,
        tokens, normed, keyval_own, came, natural, select, weight_keyval, gains,
        partial, residual_grad, gain_two_grad,
        flops=2 * 10**9,
    )
    others.append(other_keyval)
    came = [to_sibling(one) for one in others]
    near, third = (6, 32, model_width), (3, 32, model_width)
    held, right, far_right, far_left, left = run(
        middle_sum_kernel,
        [shape(near, F32), shape(near, BF), shape(third, BF), shape(third, BF), shape(near, BF)],
        held, *ffn_back,
        after=(mine_keyval,),
    )
    from_left, from_right = sent(far_right, 1, 1), sent(far_left, 1, -1)
    pieces = meet(mine, mine_keyval, came, after=(right,))
    attn_back = scatter_stage(pieces, SCATTER_ATTN[2])
    right, left = run(
        relay_kernel, [shape(near, BF)] * 2, right, left, from_left, from_right, after=(pieces[1],)
    )
    ffn_pieces, ffn_back = [held], [sent(right, 1, 1), sent(left, 1, -1)]
    pieces = cut(pieces, attn_back, after=(right,))
    back = scatter_stage(pieces, SCATTER_ATTN[1])
    ffn_pieces = cut(ffn_pieces, ffn_back, after=(pieces[1],))
    ffn_back = scatter_stage(ffn_pieces, SCATTER[0])
    pieces = cut(pieces, back, after=(ffn_pieces[1],))
    back = scatter_stage(pieces, SCATTER_ATTN[0])
    query, keyval, out, gate, up, down, gain_one, gain_two = run(
        end_kernel,
        [shape(one.shape, F32) for one in (w_query, w_keyval, w_out, w_gate, w_up, w_down, gain_attn, gain_ffn)],
        spot, pieces[0], *back, ffn_pieces[0], *ffn_back,
        in_specs=[scalar] + [WHOLE] * (2 * SIDE),
    )
    return output, input_grad, query, keyval, out, gate, up, down, gain_one, gain_two


def solution(mesh):
    rows, flat = P(AXES, None), P(AXES)
    return jax.shard_map(
        local,
        mesh=mesh,
        in_specs=(rows, flat, flat, rows, rows, rows, rows, rows, rows, rows),
        out_specs=(rows, rows, rows, rows, rows, rows, rows, rows, flat, flat),
        check_vma=False,
    )
```

```python
import math

import jax
import jax.numpy as jnp
from jax import lax
from jax.experimental import pallas as pl
from jax.experimental.pallas import tpu as pltpu
from jax.sharding import PartitionSpec as P

HEADS = 4
HEAD = 256
WIN = 512
SIDE = 4

EPSILON = 1e-06
MASKED = -1e30
AXES = ("ctx", "hd")
BF = jnp.bfloat16
F32 = jnp.float32

SCALE = 1.0 / math.sqrt(HEAD)
TILE = 128
SPAN = WIN + TILE
MEGA = 1 << 20

GATHER = ((2, 2), (1, 0), (0, 1))
SCATTER = ((1, 0), (2, 2), (0, 1))
SCATTER_ATTN = ((2, 2), (1, 0), (0, 1))


def chip_pairs(axis_of_core, steps):
    pairs = []
    for chip in range(SIDE**3):
        spot = [chip // SIDE**2, chip // SIDE % SIDE, chip % SIDE]
        for core in range(2):
            goal = list(spot)
            axis = axis_of_core[core]
            goal[axis] = (goal[axis] + steps) % SIDE
            target = (goal[0] * SIDE + goal[1]) * SIDE + goal[2]
            pairs.append((chip * 2 + core, target * 2 + core))
    return pairs


def to_sibling(value):
    return lax.ppermute(value, "hd", [(0, 1), (1, 0)])


def gather_stage(value, stage):
    return [value] + [
        lax.ppermute(value, AXES, chip_pairs(GATHER[stage], -steps)) for steps in range(1, SIDE)
    ]


def scatter_stage(pieces, axis_of_core):
    return [
        lax.ppermute(pieces[steps], AXES, chip_pairs(axis_of_core, steps))
        for steps in range(1, SIDE)
    ]


def sent(value, stage, steps):
    return lax.ppermute(value, AXES, chip_pairs(SCATTER[stage], steps))


def shifted(value, steps):
    count = lax.axis_size(AXES)
    initial, last = (max(0, -steps), min(count, count - steps))
    return lax.ppermute(value, AXES, [(source, source + steps) for source in range(initial, last)])


def times_rows(left, right):
    return lax.dot_general(left, right, (((1,), (1,)), ((), ())), preferred_element_type=F32)


def times_cols(left, right):
    return lax.dot_general(left, right, (((0,), (0,)), ((), ())), preferred_element_type=F32)


def times_plain(left, right):
    return jnp.dot(left, right, preferred_element_type=F32)


def shape(dims, kind):
    return jax.ShapeDtypeStruct(dims, kind)


WHOLE = pl.BlockSpec(memory_space=pltpu.VMEM)
ANYWHERE = pl.BlockSpec(memory_space=pl.ANY)
OUTSIDE = pl.BlockSpec(memory_space=pltpu.HBM)


def run(kernel, outs, *operands, after=(), limit=16, flops=1, in_specs=None, **more):
    count = len(operands)

    def body(*refs):
        kernel(*refs[:count], *refs[count + len(after) :])

    return pl.pallas_call(
        body,
        out_shape=outs,
        in_specs=list(in_specs or [WHOLE] * count) + [ANYWHERE] * len(after),
        cost_estimate=pl.CostEstimate(flops=flops, bytes_accessed=1, transcendentals=0),
        compiler_params=pltpu.CompilerParams(vmem_limit_bytes=limit * MEGA),
        **more,
    )(*operands, *after)


def select_kernel(place_ref, select_ref, natural_ref):
    place = place_ref[0]
    core = place % 2
    chip = place // 2
    spot = [chip // SIDE**2, chip // SIDE % SIDE, chip % SIDE]

    def device_of(half, piece, first, second):
        owner = half * (1 - core) + (1 - half) * core
        x = (spot[0] + jnp.where(owner == 0, piece, first)) % SIDE
        y = (spot[1] + jnp.where(owner == 0, first, piece)) % SIDE
        z = (spot[2] + second) % SIDE
        return ((x * SIDE + y) * SIDE + z) * 2 + owner

    row = lax.broadcasted_iota(jnp.int32, (528, 1), 0)
    feature = row % HEAD
    high, low = feature // 32 % 4, feature // 8 % 4
    device = device_of(feature // 128, high, high, low)
    goal = jnp.where(row < 512, row // HEAD * HEAD + device % 32 * 8 + feature % 8, -2)
    column = lax.broadcasted_iota(jnp.int32, (1, 1024), 1)
    device = device_of(column // 512, column // 128 % 4, column // 32 % 4, column // 8 % 4)
    part = column % 8
    have = jnp.where(part < 4, device * 4 + part, -1)
    gain = jnp.where(row >= 512, row - 508, -1)
    select_ref[...] = jnp.where(
        (goal == have) | ((gain == part) & (part < 6)), 1.0, 0.0
    ).astype(BF)
    natural_ref[...] = jnp.where(
        goal[:HEAD] == lax.broadcasted_iota(jnp.int32, (1, HEAD), 1), 1.0, 0.0
    ).astype(BF)


def normalise(values, gain):
    inverse = lax.rsqrt(jnp.mean(values * values, axis=-1, keepdims=True) + EPSILON)
    return (values * inverse * gain).astype(BF)


def normalise_back(values, gain, grad):
    inverse = lax.rsqrt(jnp.mean(values * values, axis=-1, keepdims=True) + EPSILON)
    unit = values * inverse
    gain_grad = jnp.sum(grad * unit, axis=0, keepdims=True)
    scaled = grad * gain
    return inverse * (scaled - unit * jnp.mean(scaled * unit, axis=-1, keepdims=True)), gain_grad


def own_mask():
    row = lax.broadcasted_iota(jnp.int32, (HEADS * TILE, TILE), 0) % TILE
    column = lax.broadcasted_iota(jnp.int32, (HEADS * TILE, TILE), 1)
    return column <= row


def folded(wide, own):
    return jnp.concatenate(
        [jnp.where(own, wide[:, WIN:], wide[:, :TILE]), wide[:, TILE:WIN]], axis=1
    )


def unfolded(narrow, own):
    edge = narrow[:, :TILE]
    none = jnp.zeros_like(edge)
    return jnp.concatenate(
        [jnp.where(own, none, edge), narrow[:, TILE:], jnp.where(own, edge, none)], axis=1
    )


def payload_kernel(place_ref, *refs):
    sources, (payload_ref, *places, sems) = refs[:8], refs[8:]
    copies = [
        pltpu.make_async_copy(source, goal, sems.at[k])
        for k, (source, goal) in enumerate(zip(sources, places))
    ]
    for one in copies:
        one.start()
    for one in copies:
        one.wait()
    query_ref, out_ref, keyval_ref, gate_ref, up_ref, down_ref, gain_one_ref, gain_two_ref = places
    width = gain_one_ref.shape[1]
    row = lax.broadcasted_iota(jnp.int32, (8, query_ref.shape[1]), 0)
    lane = lax.broadcasted_iota(jnp.int32, (8, query_ref.shape[1]), 1) - place_ref[0] * width
    gains = jnp.zeros(row.shape, F32)
    for k, ref in ((4, gain_one_ref), (5, gain_two_ref)):
        values = ref[...].astype(F32)
        for i in range(width):
            gains = jnp.where((row == k) & (lane == i), values[:, i : i + 1], gains)
    keyval = jnp.concatenate([keyval_ref[...].astype(F32), gains[4:]], axis=0)
    payload_ref[0] = query_ref[...]
    payload_ref[1] = out_ref[...]
    payload_ref[2] = keyval.astype(BF)
    for k, ref in ((3, gate_ref), (5, up_ref), (7, down_ref)):
        payload_ref[k : k + 2] = ref[...].reshape(2, 8, -1)


def pack_kernel(r0, r1, r2, r3, goal_ref):
    groups, rows, width = r0.shape
    for k, ref in enumerate((r0, r1, r2, r3)):
        goal_ref[:, k] = ref[...]


def choose_kernel(place_ref, own_ref, hop_ref, goal_ref):
    edge = place_ref[0] % (2 * SIDE) == 2 * SIDE - 1

    @pl.when(edge)
    def _():
        goal_ref[...] = hop_ref[...]

    @pl.when(jnp.logical_not(edge))
    def _():
        goal_ref[...] = own_ref[...]


def pack_two_kernel(r0, r1, r2, r3, attn_ref, units_ref):
    for k, ref in enumerate((r0, r1, r2, r3)):
        attn_ref[:, k] = ref[:3]
        units_ref[:, k] = ref[3:]


def before_slots(narrow, own, start):
    edge = jnp.where(own, jnp.zeros_like(narrow[:, :TILE]), narrow[:, :TILE])
    return jnp.concatenate([edge, narrow[:, TILE : WIN - start]], axis=1) if start < WIN - TILE else edge


def own_slots(narrow, own, start):
    edge = jnp.where(own, narrow[:, :TILE], jnp.zeros_like(narrow[:, :TILE]))
    return jnp.concatenate([narrow[:, WIN - start :], edge], axis=1) if start > 0 else edge


def head_rows(half, owner):
    for head in range(HEADS):
        first = head * HEAD + half * 128
        if owner == 0:
            yield first, 128, head, pl.ds(0, 128)
        else:
            for piece in range(SIDE):
                yield first + piece * 32, 32, piece, pl.ds(head * 32, 32)


def forward_kernel(
    place_ref, tokens_ref, before_ref, select_ref, a0, a1, a2, a3, b0, b1, b2, b3,
    residual_ref, normed_two_ref, normed_ref, query_ref, keyval_ref, attended_ref, probs_ref,
    weight_query_ref, weight_out_ref, weight_keyval_ref, gains_ref,
):
    count = tokens_ref.shape[0]
    halves = ((a0, a1, a2, a3), (b0, b1, b2, b3))
    for half in range(2):
        for owner in range(2):

            @pl.when((place_ref[0] + half) % 2 == owner)
            def _():
                for first, rows, piece, there in head_rows(half, owner):
                    here = pl.ds(first, rows)
                    weight_query_ref[here, :] = halves[half][piece][0, there, :]
                    weight_out_ref[here, :] = halves[half][piece][1, there, :]

    mixed = jnp.concatenate([one[2] for half in halves for one in half], axis=0)
    sorted_rows = times_plain(select_ref[...], mixed)
    weight_keyval_ref[...] = sorted_rows[:512].astype(BF)
    gains_ref[...] = sorted_rows[512:520]
    gain_one = sorted_rows[512:513]
    gain_two = sorted_rows[513:514]
    inputs = tokens_ref[...].astype(F32)
    normed = normalise(inputs, gain_one)
    normed_ref[...] = normed
    normed_before = normalise(before_ref[...].astype(F32), gain_one)
    weight_keyval = weight_keyval_ref[...]
    keyval_ref[:WIN, :] = times_rows(normed_before, weight_keyval).astype(BF)
    keyval_ref[WIN:, :] = times_rows(normed, weight_keyval).astype(BF)
    for head in range(HEADS):
        query_ref[head] = times_rows(
            normed, weight_query_ref[pl.ds(head * HEAD, HEAD), :]
        ).astype(BF) * BF(SCALE)
    own = own_mask()
    first_key = jnp.where(place_ref[0] == 0, WIN, 0)

    def scores_of(tile):
        queries = query_ref[:, pl.ds(tile * TILE, TILE), :].reshape(HEADS * TILE, HEAD)
        return times_rows(queries, keyval_ref[pl.ds(tile * TILE, SPAN), :HEAD])

    ahead = scores_of(0)
    for tile in range(count // TILE):
        start = tile * TILE
        scores = folded(ahead, own)
        if start + TILE < count:
            ahead = scores_of(tile + 1)
        slot = start + lax.broadcasted_iota(jnp.int32, (1, WIN), 1)
        hidden = jnp.where(slot >= first_key, 0.0, MASKED)
        scores = jnp.concatenate(
            [scores[:, :TILE] + jnp.where(own, 0.0, hidden[:, :TILE]), scores[:, TILE:] + hidden[:, TILE:]],
            axis=1,
        )
        raised = jnp.exp(scores - jnp.max(scores, axis=1, keepdims=True))
        probs = (raised * (1.0 / jnp.sum(raised, axis=1, keepdims=True))).astype(BF)
        probs_ref[pl.ds(tile * HEADS * TILE, HEADS * TILE), :] = probs
        mixed = times_plain(unfolded(probs, own), keyval_ref[pl.ds(start, SPAN), HEAD:]).astype(BF)
        for head in range(HEADS):
            attended_ref[pl.ds(start, TILE), pl.ds(head * HEAD, HEAD)] = mixed[
                head * TILE : (head + 1) * TILE
            ]

    residual = inputs + times_plain(attended_ref[...], weight_out_ref[...])
    residual_ref[...] = residual
    normed_two_ref[...] = normalise(residual, gain_two)


GELU_A = math.sqrt(2.0 / math.pi)
GELU_B = 0.044715


def ffn_products(normed, grad, ref):
    return times_rows(normed, ref[0:4].reshape(512, -1)), times_rows(grad, ref[4:6].reshape(256, -1))


def ffn_units(both, hidden_grad):
    gate, up = both[:, :256], both[:, 256:]
    square = gate * gate
    bend = jnp.tanh(GELU_A * gate * (1.0 + GELU_B * square))
    half = 0.5 * (1.0 + bend)
    active = gate * half
    slope = half + 0.5 * gate * (1.0 - bend * bend) * (GELU_A + (3.0 * GELU_A * GELU_B) * square)
    both_grad = jnp.concatenate(
        [(hidden_grad * up * slope).astype(BF), (hidden_grad * active).astype(BF)], axis=1
    )
    return (active * up).astype(BF), both_grad


def ffn_sums(normed_ref, grad_ref, weights, both_grad_ref, hidden_ref, branch=None, normed_grad=None):
    normed = normed_ref[...]
    grad = grad_ref[...]
    ahead = ffn_products(normed, grad, weights[0])
    for k, ref in enumerate(weights):
        now = ahead
        if k + 1 < len(weights):
            ahead = ffn_products(normed, grad, weights[k + 1])
        hidden, both_grad = ffn_units(*now)
        hidden_ref[k] = hidden
        both_grad_ref[k] = both_grad
        branch_term = times_plain(hidden, ref[4:6].reshape(256, -1))
        normed_term = times_plain(both_grad, ref[0:4].reshape(512, -1))
        branch = branch_term if branch is None else branch + branch_term
        normed_grad = normed_term if normed_grad is None else normed_grad + normed_term
    return branch, normed_grad


def ffn_kernel(normed_ref, grad_ref, w0, w1, w2, branch_ref, normed_grad_ref, both_grad_ref, hidden_ref):
    branch_ref[...], normed_grad_ref[...] = ffn_sums(
        normed_ref, grad_ref, (w0, w1, w2), both_grad_ref, hidden_ref
    )


def ffn_last_kernel(
    normed_ref, grad_ref, normed_other_ref, grad_other_ref, w0, branch_in_ref, normed_grad_in_ref, branch_other_ref, normed_grad_other_ref,
    branch_ref, normed_grad_ref, both_grad_ref, hidden_ref, sums_ref, both_grad_other_ref, hidden_other_ref,
):
    branch, normed_grad = ffn_sums(
        normed_other_ref, grad_other_ref, (w0,), both_grad_other_ref, hidden_other_ref,
        branch_other_ref[...], normed_grad_other_ref[...],
    )
    sums_ref[0] = branch.astype(BF)
    sums_ref[1] = normed_grad.astype(BF)
    branch_ref[...], normed_grad_ref[...] = ffn_sums(
        normed_ref, grad_ref, (w0,), both_grad_ref, hidden_ref, branch_in_ref[...], normed_grad_in_ref[...]
    )


def ffn_terms_kernel(
    normed_ref, grad_ref, both_ref, hidden_ref, both_late_ref, hidden_late_ref,
    normed_other_ref, grad_other_ref, both_other_ref, hidden_other_ref, both_late_other_ref, hidden_late_other_ref,
    held_ref, right_ref, far_right_ref, far_left_ref, left_ref,
):
    for k, goal in ((2, None), (0, held_ref), (1, right_ref), (3, left_ref)):
        if k == 2:
            parts = (both_late_ref[0], hidden_late_ref[0], both_late_other_ref[0], hidden_late_other_ref[0])
        else:
            parts = [ref[min(k, 2)] for ref in (both_ref, hidden_ref, both_other_ref, hidden_other_ref)]
        both = times_cols(parts[0], normed_ref[...]) + times_cols(parts[2], normed_other_ref[...])
        down = times_cols(parts[1], grad_ref[...]) + times_cols(parts[3], grad_other_ref[...])
        both, down = both.reshape(4, 128, -1), down.reshape(2, 128, -1)
        if k == 2:
            far_right_ref[...] = both[:3].astype(BF)
            far_left_ref[0:1] = both[3:].astype(BF)
            far_left_ref[1:3] = down.astype(BF)
        else:
            goal[0:4] = both.astype(goal.dtype)
            goal[4:6] = down.astype(goal.dtype)


def relay_kernel(right_ref, left_ref, from_left_ref, from_right_ref, right_goal, left_goal):
    right_goal[0:3] = (right_ref[0:3].astype(F32) + from_left_ref[...].astype(F32)).astype(BF)
    right_goal[3:6] = right_ref[3:6]
    left_goal[0:3] = left_ref[0:3]
    left_goal[3:6] = (left_ref[3:6].astype(F32) + from_right_ref[...].astype(F32)).astype(BF)


def output_kernel(residual_ref, branch_ref, sums_ref, output_ref):
    output_ref[...] = (residual_ref[...] + branch_ref[...] + sums_ref[0].astype(F32)).astype(BF)


def middle_kernel(
    residual_ref, normed_grad_ref, sums_ref, cotangent_ref, gains_ref, weight_out_ref, query_ref, keyval_ref, probs_ref,
    natural_ref, residual_grad_ref, low_ref, rows_ref, score_grad_ref, sent_ref, gain_ref, window_ref,
):
    count = residual_ref.shape[0]
    residual = residual_ref[...]
    normed_grad = normed_grad_ref[...] + sums_ref[1].astype(F32)
    part, gain_grad = normalise_back(residual, gains_ref[1:2, :], normed_grad)
    gain_ref[...] = jnp.broadcast_to(gain_grad, gain_ref.shape)
    residual_grad = cotangent_ref[...].astype(F32) + part
    residual_grad_ref[...] = residual_grad
    low = residual_grad.astype(BF)
    low_ref[...] = low
    for head in range(HEADS):
        rows_ref[head] = times_rows(low, weight_out_ref[pl.ds(head * HEAD, HEAD), :]).astype(BF)
    own = own_mask()

    def rows_of(tile):
        return rows_ref[:, pl.ds(tile * TILE, TILE), :].reshape(HEADS * TILE, HEAD)

    def grads_of(tile):
        return times_rows(rows_of(tile), keyval_ref[pl.ds(tile * TILE, SPAN), HEAD:])

    ahead = grads_of(0)
    for tile in range(count // TILE):
        start = tile * TILE
        here = pl.ds(tile * HEADS * TILE, HEADS * TILE)
        queries = query_ref[:, pl.ds(start, TILE), :].reshape(HEADS * TILE, HEAD)
        rows = rows_of(tile)
        low_probs = probs_ref[here, :]
        probs = low_probs.astype(F32)
        prob_grad = folded(ahead, own)
        if start + TILE < count:
            ahead = grads_of(tile + 1)
        centre = jnp.sum(probs * prob_grad, axis=1, keepdims=True) / jnp.sum(
            probs, axis=1, keepdims=True
        )
        score_grad = (probs * (prob_grad - centre)).astype(BF)
        score_grad_ref[here, :] = score_grad
        earlier = pl.ds(start, WIN - start)
        key_term = times_cols(before_slots(score_grad, own, start), queries)
        value_term = times_cols(before_slots(low_probs, own, start), rows)
        if tile == 0:
            window_ref[earlier, :HEAD] = key_term
            window_ref[earlier, HEAD:] = value_term
        else:
            window_ref[earlier, :HEAD] += key_term
            window_ref[earlier, HEAD:] += value_term
    natural = natural_ref[...]
    sent_ref[:, :HEAD] = times_plain(window_ref[:, :HEAD].astype(BF), natural).astype(BF)
    sent_ref[:, HEAD:] = times_plain(window_ref[:, HEAD:].astype(BF), natural).astype(BF)


def own_kernel(rows_ref, score_grad_ref, query_ref, keyval_ref, probs_ref, query_grad_ref, own_ref):
    count = query_grad_ref.shape[0]
    own = own_mask()
    for tile in reversed(range(count // TILE)):
        start = tile * TILE
        span = pl.ds(start, SPAN)
        here = pl.ds(tile * HEADS * TILE, HEADS * TILE)
        queries = query_ref[:, pl.ds(start, TILE), :].reshape(HEADS * TILE, HEAD)
        rows = rows_ref[:, pl.ds(start, TILE), :].reshape(HEADS * TILE, HEAD)
        score_grad = score_grad_ref[here, :]
        mixed = (times_plain(unfolded(score_grad, own), keyval_ref[span, :HEAD]) * SCALE).astype(BF)
        for head in range(HEADS):
            query_grad_ref[pl.ds(start, TILE), pl.ds(head * HEAD, HEAD)] = mixed[
                head * TILE : (head + 1) * TILE
            ]
        mine = pl.ds(0, start + TILE)
        key_term = times_cols(own_slots(score_grad, own, start), queries)
        value_term = times_cols(own_slots(probs_ref[here, :], own, start), rows)
        if start + TILE == count:
            own_ref[mine, :HEAD] = key_term
            own_ref[mine, HEAD:] = value_term
        else:
            own_ref[mine, :HEAD] += key_term
            own_ref[mine, HEAD:] += value_term


def weights_kernel(
    place_ref, normed_ref, low_ref, attended_ref, query_grad_ref, weight_query_ref,
    normed_grad_ref, mine_ref, *other_refs,
):
    query_grad = query_grad_ref[...]
    normed_grad_ref[...] = times_plain(query_grad, weight_query_ref[...])
    for group, term in (
        (0, times_cols(query_grad, normed_ref[...]).astype(BF)),
        (1, times_cols(attended_ref[...], low_ref[...]).astype(BF)),
    ):
        for half in range(2):
            for owner in range(2):

                @pl.when((place_ref[0] + half) % 2 == owner)
                def _():
                    for first, rows, piece, there in head_rows(half, owner):
                        goal = mine_ref.at[piece, group]
                        if half == 1:
                            goal = other_refs[group].at[piece]
                        goal[there, :] = term[first : first + rows]


def last_kernel(
    tokens_ref, normed_ref, own_ref, came_ref, natural_ref, select_ref, weight_keyval_ref, gains_ref,
    partial_ref, residual_grad_ref, gain_two_ref,
    input_grad_ref, mine_ref, other_ref,
):
    natural = natural_ref[...]
    keyval = jnp.concatenate(
        [
            own_ref[:, :HEAD] + times_rows(came_ref[:, :HEAD], natural),
            own_ref[:, HEAD:] + times_rows(came_ref[:, HEAD:], natural),
        ],
        axis=1,
    ).astype(BF)
    grad = partial_ref[...] + times_plain(keyval, weight_keyval_ref[...])
    part, gain_grad = normalise_back(tokens_ref[...].astype(F32), gains_ref[0:1, :], grad)
    input_grad_ref[...] = residual_grad_ref[...] + part
    row = lax.broadcasted_iota(jnp.int32, (16, gain_grad.shape[1]), 0)
    gain_rows = jnp.where(
        row == 0, gain_grad, jnp.where(row == 1, gain_two_ref[0:1, :], 0.0)
    ).astype(BF)
    rows = jnp.concatenate([times_cols(keyval, normed_ref[...]).astype(BF), gain_rows], axis=0)
    mixed = times_cols(select_ref[...], rows).astype(BF)
    for piece in range(SIDE):
        mine_ref[piece] = mixed[piece * 128 : (piece + 1) * 128]
        other_ref[piece] = mixed[512 + piece * 128 : 512 + (piece + 1) * 128]


def meet_kernel(mine_ref, mine_keyval_ref, *refs):
    for last, goal in enumerate(refs[3:]):
        for k in range(3):
            mine = mine_ref[last, k] if k < 2 else mine_keyval_ref[last]
            goal[k] = (mine.astype(F32) + refs[k][last].astype(F32)).astype(goal.dtype)


def meet(mine, mine_keyval, came, after=()):
    _, rows, width = mine_keyval.shape
    return run(
        meet_kernel,
        [shape((3, rows, width), F32 if k == 0 else BF) for k in range(SIDE)],
        mine,
        mine_keyval,
        *came,
        after=after,
    )


def summed(refs):
    total = refs[0][...]
    for one in refs[1:]:
        total = total + one[...].astype(F32)
    return total


def middle_sum_kernel(held_ref, came_right_ref, came_left_ref, held_goal, right_goal, far_right_goal, far_left_goal, left_goal):
    total = summed((held_ref, came_right_ref, came_left_ref))
    groups, rows, width = total.shape
    blocks = total.reshape(groups, SIDE, SIDE, 8, width)

    def block(k):
        return blocks[:, :, k].reshape(groups, 4 * 8, width)

    held_goal[...] = block(0)
    right_goal[...] = block(1).astype(BF)
    far_right_goal[...] = block(2)[:3].astype(BF)
    far_left_goal[...] = block(2)[3:].astype(BF)
    left_goal[...] = block(3).astype(BF)


def cut_kernel(*refs):
    total = summed(refs[:-SIDE])
    rows = total.shape[1] // SIDE
    for k, goal in enumerate(refs[-SIDE:]):
        goal[...] = total[:, k * rows : (k + 1) * rows].astype(goal.dtype)


def cut(pieces, came, after=()):
    groups, rows, width = pieces[0].shape
    outs = [shape((groups, rows // SIDE, width), F32 if k == 0 else BF) for k in range(SIDE)]
    return run(cut_kernel, outs, pieces[0], *came, after=after)


def end_kernel(
    place_ref, r0, r1, r2, r3, f0, f1, f2, f3, query_ref, keyval_ref, out_ref, gate_ref, up_ref, down_ref, one_ref, two_ref
):
    total = summed((r0, r1, r2, r3))
    units = summed((f0, f1, f2, f3))
    query_ref[...] = total[0]
    out_ref[...] = total[1]
    keyval_ref[...] = total[2, :4]
    for k, goal in ((0, gate_ref), (2, up_ref), (4, down_ref)):
        goal[...] = units[k : k + 2].reshape(goal.shape)
    width = one_ref.shape[0]
    full = total.shape[-1]
    rows = pltpu.roll(total[2], lax.rem(full - place_ref[0] * width, full), 1)
    one_ref[...] = rows[4, :width]
    two_ref[...] = rows[5, :width]


def local(tokens, gain_attn, gain_ffn, w_query, w_keyval, w_out, w_gate, w_up, w_down, cotangent):
    row_count, model_width = tokens.shape
    place = lax.axis_index(AXES)

    cotangent_other = to_sibling(cotangent)
    spot = place.reshape(1)
    scalar = pl.BlockSpec(memory_space=pltpu.SMEM)
    shards = (w_query, w_out, w_keyval, w_gate, w_up, w_down, gain_attn[None], gain_ffn[None])
    payload, = run(
        payload_kernel,
        [shape((9, 8, model_width), BF)],
        spot, *shards,
        in_specs=[scalar] + [OUTSIDE] * 8,
        limit=60,
        scratch_shapes=[pltpu.VMEM(one.shape, BF) for one in shards] + [pltpu.SemaphoreType.DMA((8,))],
    )
    hop = [((chip * SIDE + 3) * 2 + 1, (chip * SIDE + 7) * 2 + 1) for chip in range(SIDE**2 - 1)]
    ring = [(2 * chip, 2 * chip + 1) for chip in range(SIDE**3)]
    ring += [(2 * chip + 1, 2 * (chip // SIDE * SIDE + (chip + 1) % SIDE)) for chip in range(SIDE**3)]
    chosen, = run(
        choose_kernel,
        [shape(tokens.shape, BF)],
        place.reshape(1), tokens, lax.ppermute(tokens, AXES, hop),
        in_specs=[pl.BlockSpec(memory_space=pltpu.SMEM), WHOLE, WHOLE],
    )
    before = lax.ppermute(chosen, AXES, ring)
    select, natural = run(
        select_kernel,
        [shape((528, 1024), BF), shape((HEAD, HEAD), BF)],
        spot,
        in_specs=[scalar],
    )
    payload, = run(
        pack_kernel,
        [shape((9, SIDE, 8, model_width), BF)],
        *gather_stage(payload, 0),
        flops=4 * 10**9,
    )
    attn, units = run(
        pack_two_kernel,
        [shape((3, SIDE, SIDE, 8, model_width), BF), shape((6, SIDE, SIDE, 8, model_width), BF)],
        *gather_stage(payload, 1),
        after=(chosen, natural),
    )
    attn = gather_stage(attn.reshape(3, 128, model_width), 2)
    units = gather_stage(units.reshape(6, 128, model_width), 2)
    attn += [to_sibling(one) for one in attn]

    (
        residual, normed_two, normed, queries, keyvals, attended, probs, weight_query, weight_out, weight_keyval, gains
    ) = run(
        forward_kernel,
        (
            shape((row_count, model_width), F32),
            shape((row_count, model_width), BF),
            shape((row_count, model_width), BF),
            shape((HEADS, row_count, HEAD), BF),
            shape((2 * row_count, 2 * HEAD), BF),
            shape((row_count, HEADS * HEAD), BF),
            shape((HEADS * row_count, WIN), BF),
            shape((HEADS * HEAD, model_width), BF),
            shape((HEADS * HEAD, model_width), BF),
            shape((2 * HEAD, model_width), BF),
            shape((8, model_width), F32),
        ),
        spot, tokens, before, select, *attn,
        in_specs=[scalar] + [WHOLE] * 11,
    )

    normed_other = to_sibling(normed_two)
    def kept(count):
        return [shape((count, row_count, 512), BF), shape((count, row_count, 256), BF)]

    branch, normed_grad, both_grad, hidden = run(
        ffn_kernel,
        [shape((row_count, model_width), F32)] * 2 + kept(3),
        normed_two, cotangent, units[0], units[1], units[3],
        flops=10**10,
    )
    branch_other, normed_grad_other, both_grad_other, hidden_other = run(
        ffn_kernel,
        [shape((row_count, model_width), F32)] * 2 + kept(3),
        normed_other, cotangent_other, units[0], units[1], units[3],
        after=(normed_grad,),
    )
    branch, normed_grad, both_late, hidden_late, sums, both_late_other, hidden_late_other = run(
        ffn_last_kernel,
        [shape((row_count, model_width), F32)] * 2 + kept(1) + [shape((2, row_count, model_width), BF)] + kept(1),
        normed_two, cotangent, normed_other, cotangent_other, units[2], branch, normed_grad, branch_other, normed_grad_other,
    )
    sums = to_sibling(sums)
    full, part = (6, 128, model_width), (3, 128, model_width)
    held, right, far_right, far_left, left = run(
        ffn_terms_kernel,
        [shape(full, F32), shape(full, BF), shape(part, BF), shape(part, BF), shape(full, BF)],
        normed_two, cotangent, both_grad, hidden, both_late, hidden_late,
        normed_other, cotangent_other, both_grad_other, hidden_other, both_late_other, hidden_late_other,
    )
    from_left, from_right = sent(far_right, 2, 1), sent(far_left, 2, -1)

    residual_grad, low, rows, score_grad, keyval_sent, gain_two_grad = run(
        middle_kernel,
        (
            shape((row_count, model_width), F32),
            shape((row_count, model_width), BF),
            shape((HEADS, row_count, HEAD), BF),
            shape((HEADS * row_count, WIN), BF),
            shape((row_count, 2 * HEAD), BF),
            shape((8, model_width), F32),
        ),
        residual, normed_grad, sums, cotangent, gains, weight_out, queries, keyvals, probs, natural,
        after=(far_left,),
        scratch_shapes=[pltpu.VMEM((row_count, 2 * HEAD), F32)],
    )
    came = shifted(keyval_sent, -1)
    query_grad, keyval_own = run(
        own_kernel,
        (shape((row_count, HEADS * HEAD), BF), shape((row_count, 2 * HEAD), F32)),
        rows, score_grad, queries, keyvals, probs,
    )
    right, left = run(
        relay_kernel, [shape(full, BF)] * 2, right, left, from_left, from_right, after=(low,)
    )
    ffn_back = [sent(right, 2, 1), sent(left, 2, -1)]
    partial, mine, *others = run(
        weights_kernel,
        (shape((row_count, model_width), F32), shape((SIDE, 2, 128, model_width), BF))
        + (shape((SIDE, 128, model_width), BF),) * 2,
        spot, normed, low, attended, query_grad, weight_query,
        after=(right,),
        in_specs=[scalar] + [WHOLE] * 5,
    )
    input_grad, mine_keyval, other_keyval = run(
        last_kernel,
        (shape((row_count, model_width), F32),) + (shape((SIDE, 128, model_width), BF),) * 2,
        tokens, normed, keyval_own, came, natural, select, weight_keyval, gains,
        partial, residual_grad, gain_two_grad,
        flops=2 * 10**9,
    )
    others.append(other_keyval)
    came = [to_sibling(one) for one in others]
    near, third = (6, 32, model_width), (3, 32, model_width)
    held, right, far_right, far_left, left = run(
        middle_sum_kernel,
        [shape(near, F32), shape(near, BF), shape(third, BF), shape(third, BF), shape(near, BF)],
        held, *ffn_back,
        after=(mine_keyval,),
    )
    from_left, from_right = sent(far_right, 1, 1), sent(far_left, 1, -1)
    pieces = meet(mine, mine_keyval, came, after=(right,))
    attn_back = scatter_stage(pieces, SCATTER_ATTN[2])
    output, = run(
        output_kernel, [shape((row_count, model_width), BF)], residual, branch, sums, after=(pieces[1],)
    )
    right, left = run(
        relay_kernel, [shape(near, BF)] * 2, right, left, from_left, from_right, after=(output,)
    )
    ffn_pieces, ffn_back = [held], [sent(right, 1, 1), sent(left, 1, -1)]
    pieces = cut(pieces, attn_back, after=(right,))
    back = scatter_stage(pieces, SCATTER_ATTN[1])
    ffn_pieces = cut(ffn_pieces, ffn_back, after=(pieces[1],))
    ffn_back = scatter_stage(ffn_pieces, SCATTER[0])
    pieces = cut(pieces, back, after=(ffn_pieces[1],))
    back = scatter_stage(pieces, SCATTER_ATTN[0])
    query, keyval, out, gate, up, down, gain_one, gain_two = run(
        end_kernel,
        [shape(one.shape, F32) for one in (w_query, w_keyval, w_out, w_gate, w_up, w_down, gain_attn, gain_ffn)],
        spot, pieces[0], *back, ffn_pieces[0], *ffn_back,
        in_specs=[scalar] + [WHOLE] * (2 * SIDE),
    )
    return output, input_grad, query, keyval, out, gate, up, down, gain_one, gain_two


def solution(mesh):
    rows, flat = P(AXES, None), P(AXES)
    return jax.shard_map(
        local,
        mesh=mesh,
        in_specs=(rows, flat, flat, rows, rows, rows, rows, rows, rows, rows),
        out_specs=(rows, rows, rows, rows, rows, rows, rows, rows, flat, flat),
        check_vma=False,
    )
```
